32 devices in a mesh: dp: 4 (over z), sp: 8 (over y, x, core).
Axes of the slice: x: 2, y: 2, z: 4, core: 2. Of those that a mesh axis runs over, the one named last changes fastest.
Arguments:
- hidden_in: bfloat16 [4096, 2048], P(('dp', 'sp')), may hold values from -6 to 6
- teacher: bfloat16 [4096, 2048], P(('dp', 'sp')), may hold values from -13 to 13
- seq_lengths: int32 [4, 8], replicated, may hold values from 0 to 1024, as said below
- routes: int32 [4096, 4], P(('dp', 'sp')), may hold values from 0 to 7, all different within a row; in each aligned block of 128 rows (0 to 127, 128 to 255, ...) at most 72 rows name the same one
- attn_norm: bfloat16 [2048], replicated, may hold values from 0.5 to 1.5
- qkv_proj: bfloat16 [3, 2048, 2048], P(None, None, 'sp'), may hold values from -0.125 to 0.125
- qkv_bias: bfloat16 [3, 16, 128], P(None, 'sp'), may hold values from -0.75 to 0.75
- out_proj: bfloat16 [2048, 2048], P('sp'), may hold values from -1 to 1
- ffn_norm: bfloat16 [2048], replicated, may hold values from 0.5 to 1.5
- router: bfloat16 [2048, 8], replicated, may hold values from -0.125 to 0.125
- shared_gateup: bfloat16 [2048, 2, 5632], P(None, None, 'sp'), may hold values from -0.125 to 0.125
- shared_down: bfloat16 [5632, 2048], P('sp'), may hold values from -0.078125 to 0.078125
- shared_switch: bfloat16 [2048], replicated, may hold values from -0.125 to 0.125
- expert_gateup: bfloat16 [8, 2048, 2, 1408], P('sp'), may hold values from -0.125 to 0.125
- expert_down: bfloat16 [8, 1408, 2048], P('sp'), may hold values from -0.15625 to 0.15625
Outputs:
- output: float32 [4096, 2048], P(('dp', 'sp'))
- loss_value: float32 [], replicated
- hidden_grad: float32 [4096, 2048], P(('dp', 'sp'))
- attnnorm_grad: float32 [2048], P(('dp', 'sp'))
- qkvproj_grad: float32 [3, 2048, 2048], P(None, 'dp', 'sp')
- qkvbias_grad: float32 [3, 16, 128], P(None, 'sp', 'dp')
- outproj_grad: float32 [2048, 2048], P('sp', 'dp')
- ffnnorm_grad: float32 [2048], P(('dp', 'sp'))
- router_grad: float32 [2048, 8], P(('dp', 'sp'))
- sharedgu_grad: float32 [2048, 2, 5632], P('dp', None, 'sp')
- shareddown_grad: float32 [5632, 2048], P('sp', 'dp')
- switch_grad: float32 [2048], P(('dp', 'sp'))
- expertgu_grad: float32 [8, 2048, 2, 1408], P('sp', 'dp')
- expertdown_grad: float32 [8, 1408, 2048], P('sp', None, 'dp')
The draws below stay inside these ranges and needn't reach their ends.
Inputs may be any that keep to these rules, and one draw needn't show every extreme that they name: `seq_lengths`: entries of a row past its last sequence are 0. Each row's sequences take ceil(len / 128) blocks of 128 slots and together exactly 1024 slots; some row holds one sequence of 1024 tokens. `routes`: within the 128 rows of one device, no expert is named by more than 72 rows.
All inputs are finite; a program needn't handle non-finite values.
Results may differ from the reference program's by a relative error of at most 0.012.
The reference program's roundings to bfloat16 on the way count: a program that leaves them out, or rounds other values in their place, can miss the bound.
Values may be sent and summed in bfloat16 or wider, within the bound.
No kernel may reach another device: no remote copies, remote signals or barrier semaphores. Data moves between devices by JAX's collectives and lax.ppermute only.
A program may use at most 320 MiB of HBM per device.

```python
import math
import jax
import jax.numpy as jnp
import numpy as np
from jax import lax

D = 2048
HEADS = 16
HD = 128
FFE = 1408
SH = 5632
TOP = 4
BLK = 128
PACK = 1024
TOKENS = 4096
TOK_DEV = 128
EXPERTS = 8
MAXSEQ = 8
CAP = 72
N_DP = 4
N_SP = 8


def draw_seq_lengths(key, part):
    blocks_all = PACK // BLK
    cut_key = jax.random.fold_in(key, 11)
    full_key = jax.random.fold_in(key, 12)
    trim_key = jax.random.fold_in(key, 13)
    cuts = jax.random.randint(cut_key, (N_DP, blocks_all - 1), 0, 2).astype(jnp.int32)
    whole_group = jax.random.randint(full_key, (), 0, N_DP).astype(jnp.int32)
    is_whole = jnp.arange(N_DP, dtype=jnp.int32)[:, None] == whole_group
    cuts = jnp.where(is_whole, 0, cuts)
    labels = jnp.concatenate([jnp.zeros((N_DP, 1), jnp.int32), jnp.cumsum(cuts, axis=1).astype(jnp.int32)], axis=1)
    blocks = jnp.sum((labels[:, :, None] == jnp.arange(blocks_all, dtype=jnp.int32)[None, None, :]).astype(jnp.int32), axis=1)
    trims = jax.random.randint(trim_key, (N_DP, blocks_all), 0, BLK).astype(jnp.int32)
    trims = jnp.where(is_whole, 0, trims)
    return jnp.where(blocks > 0, blocks * BLK - trims, 0).astype(jnp.int32)


def draw_teacher(key, part):
    rows = jnp.arange(TOKENS, dtype=jnp.float32)[:, None] / TOKENS
    base = jnp.clip(jax.random.normal(key, (TOKENS, D), jnp.float32), -4.0, 4.0)
    scale = 1.0 + 2.0 * rows
    return (base * scale).astype(jnp.bfloat16)


def block_levels(rng, shape, split, smallest, top_value):
    gain = 1.0
    for dim, blocks in split:
        heights = jax.random.uniform(jax.random.fold_in(jax.random.fold_in(rng, 6), dim), (blocks,), jnp.float32, smallest / len(split), top_value / len(split))
        gain = gain * jnp.repeat(jnp.exp(heights), shape[dim] // blocks).reshape((-1,) + (1,) * (len(shape) - 1 - dim))
    return gain


def deal_out(key, own, number, rows, count, top, bound, slope):
    ranking = jax.random.permutation(key, count)
    packed, common = portions_of(count, rows * top, bound, slope, True), portions_of(count, rows * top, bound, slope, False)
    places = jnp.arange(count)

    def named(tallies, turn):
        used = int((tallies > 0).sum())
        fixed = max(1, used // 4)
        shifted = fixed + (places - fixed + turn * (used - fixed)) % max(1, count - fixed)
        return jnp.zeros((count,), jnp.int32).at[ranking[jnp.where(places < fixed, places, shifted)]].set(jnp.asarray(tallies, jnp.int32))

    tallies = jnp.where(number % 4 == 0, named(packed, number // 4), named(common, number - number // 4 - 1))
    mixed = jax.random.permutation(jax.random.fold_in(own, 3), count)
    giver, sink = mixed[0:count // 2 * 2:2], mixed[1:count // 2 * 2:2]
    margin = jnp.minimum(tallies[giver] - 1, bound - tallies[sink]) // 2
    margin = jnp.where((giver == ranking[0]) | (sink == ranking[0]) | (tallies[sink] == 0), 0, jnp.maximum(margin, 0))
    shifted = jax.random.randint(jax.random.fold_in(own, 4), (count // 2,), 0, 1 << 20) % (margin + 1)
    tallies = tallies.at[giver].add(-shifted).at[sink].add(shifted)
    items = jnp.searchsorted(jnp.cumsum(tallies), jnp.arange(rows * top), side="right").astype(jnp.int32)
    listing = items.reshape(top, rows).T
    listing = listing[jax.random.permutation(jax.random.fold_in(own, 1), rows)]
    turn = jax.random.randint(jax.random.fold_in(own, 2), (rows, 1), 0, top)
    return jnp.take_along_axis(listing, (jnp.arange(top)[None, :] + turn) % top, axis=1)


def portions_of(number_of, total, reach, skew, full):
    weights = [(1 << 20) // math.isqrt(standing ** skew) + 1 for standing in range(1, number_of + 1)]
    largest = reach if full else min(reach, max(-(-total // number_of), total * weights[0] // sum(weights)))
    least = 1 if total - largest >= number_of - 1 else 0
    holding, surplus = [largest] + [least] * (number_of - 1), total - largest - least * (number_of - 1)
    while surplus > 0:
        candidates = [i for i in range(1, number_of) if holding[i] < largest] or [i for i in range(1, number_of) if holding[i] < reach]
        mass, remaining = sum([weights[i] for i in candidates]), surplus
        for i in candidates:
            addition = min(reach - holding[i], max(1, remaining * weights[i] // mass), surplus)
            holding[i] = holding[i] + addition
            surplus = surplus - addition
    return np.array(holding)


def normal_values(own_key, shape, deviation, bound, shards=(), kind=jnp.bfloat16):
    level = block_levels(own_key, shape, shards, -0.22, 0.18) if shards else 1.0
    array = jax.random.normal(own_key, shape, jnp.float32) * deviation * level
    return jnp.minimum(jnp.maximum(array, -bound), bound).astype(kind)


def setup_inputs(seed: int = 0) -> dict:
    keys = jax.random.split(jax.random.key(seed), 16)
    hidden_in = normal_values(keys[0], (TOKENS, D), 1.0, 6.0, ((0, 32),))
    teacher = draw_teacher(jax.random.fold_in(keys[15], 71), 0)
    seq_lengths = draw_seq_lengths(jax.random.fold_in(keys[15], 71), 0)
    routes_keys = jax.random.split(jax.random.fold_in(keys[3], 1), TOKENS // TOK_DEV)
    routes_turns = jax.random.permutation(jax.random.fold_in(keys[3], 3), TOKENS // TOK_DEV)
    routes = jax.vmap(lambda own, number: deal_out(jax.random.fold_in(keys[3], 2), own, number, TOK_DEV, EXPERTS, TOP, CAP, 1))(routes_keys, routes_turns).reshape((TOKENS, TOP))
    attn_norm = jnp.clip(1.0 + 0.1 * jax.random.normal(keys[4], (D,), jnp.float32), 0.5, 1.5).astype(jnp.bfloat16)
    qkv_proj = normal_values(keys[5], (3, D, HEADS * HD), D ** -0.5, 0.125, ((2, 8),))
    qkv_bias = normal_values(keys[6], (3, HEADS, HD), 0.05, 0.75, ((1, 8),))
    out_proj = normal_values(keys[7], (HEADS * HD, D), (D // 64) ** -0.5, 1.0, ((0, 8),))
    ffn_norm = jnp.clip(1.0 + 0.1 * jax.random.normal(keys[8], (D,), jnp.float32), 0.5, 1.5).astype(jnp.bfloat16)
    router = normal_values(keys[9], (D, EXPERTS), D ** -0.5, 0.125)
    shared_gateup = normal_values(keys[10], (D, 2, SH), D ** -0.5, 0.125, ((2, 8),))
    shared_down = normal_values(keys[11], (SH, D), SH ** -0.5, 0.078125, ((0, 8),))
    shared_switch = normal_values(keys[12], (D,), D ** -0.5, 0.125)
    expert_gateup = normal_values(keys[13], (EXPERTS, D, 2, FFE), D ** -0.5, 0.125, ((0, 8),))
    expert_down = normal_values(keys[14], (EXPERTS, FFE, D), FFE ** -0.5, 0.15625, ((0, 8),))
    return {"hidden_in": hidden_in, "teacher": teacher, "seq_lengths": seq_lengths, "routes": routes, "attn_norm": attn_norm, "qkv_proj": qkv_proj, "qkv_bias": qkv_bias, "out_proj": out_proj, "ffn_norm": ffn_norm, "router": router, "shared_gateup": shared_gateup, "shared_down": shared_down, "shared_switch": shared_switch, "expert_gateup": expert_gateup, "expert_down": expert_down}


@jax.custom_vjp
def low(v):
    return lax.optimization_barrier(v.astype(jnp.bfloat16)).astype(jnp.float32)

@jax.custom_vjp
def low_back(v):
    return v

def low_keep(v):
    return (low(v), None)

def low_pass(kept, grad):
    return (grad,)

def back_keep(v):
    return (v, None)

def back_low(kept, grad):
    return (low(grad),)
low.defvjp(low_keep, low_pass)
low_back.defvjp(back_keep, back_low)
EPS = 1e-06
THETA = 1000000.0
FLOOR = -1e+30
HIGH = lax.Precision.HIGHEST

def layout(length_row):
    length_row = length_row.astype(jnp.int32)
    blocks = (length_row + BLK - 1) // BLK
    ends = jnp.cumsum(blocks).astype(jnp.int32)
    starts = ends - blocks
    place = jnp.arange(PACK, dtype=jnp.int32)
    which = lax.optimization_barrier(jnp.sum((place[:, None] // BLK >= ends[None, :]).astype(jnp.int32), axis=1))
    member = which[:, None] == jnp.arange(MAXSEQ, dtype=jnp.int32)[None, :]
    opening = lax.optimization_barrier(jnp.sum(jnp.where(member, starts[None, :], 0), axis=1)).astype(jnp.int32)
    seq_len = lax.optimization_barrier(jnp.sum(jnp.where(member, length_row[None, :], 0), axis=1)).astype(jnp.int32)
    position = place - opening * BLK
    return (which, position, position < seq_len)

def rope_tables(position):
    half_dim = HD // 2
    freq = THETA ** (-2.0 * jnp.arange(half_dim, dtype=jnp.float32) / HD)
    angle = position.astype(jnp.float32)[:, None] * freq[None, :]
    return (jnp.concatenate([jnp.cos(angle), jnp.cos(angle)], -1), jnp.concatenate([jnp.sin(angle), jnp.sin(angle)], -1))

def rotate(flat_rows, cosine, sine_table):
    count = flat_rows.shape[0]
    shaped = flat_rows.reshape(count, -1, HD)
    half_dim = HD // 2
    turned = jnp.concatenate([-shaped[..., half_dim:], shaped[..., :half_dim]], -1)
    return (shaped * cosine[:, None, :] + turned * sine_table[:, None, :]).reshape(count, -1)

def normalize(values, gain_vec):
    return values * lax.rsqrt(lax.optimization_barrier(jnp.mean(values * values, axis=-1, keepdims=True)) + EPS) * gain_vec

def attend(queries, key_rows, values, segment, position, is_valid):
    count = queries.shape[0]
    q_heads = queries.reshape(count, HEADS, HD)
    k_heads = key_rows.reshape(count, HEADS, HD)
    v_heads = values.reshape(count, HEADS, HD)
    scores = jnp.einsum('qhd,khd->hqk', q_heads, k_heads, precision=HIGH) * HD ** (-0.5)
    allowed = (segment[:, None] == segment[None, :]) & (position[None, :] <= position[:, None]) & is_valid[None, :]
    scores = low_back(jnp.where(allowed[None], scores, FLOOR))
    weights = low(jax.nn.softmax(scores, axis=-1))
    mixed = jnp.einsum('hqk,khd->qhd', weights, v_heads, precision=HIGH)
    return mixed.reshape(count, HEADS * HD)

def group_forward(params, hidden_rows, teacher_rows, route_rows, length_row):
    attn_norm, qkv_proj, qkv_bias, out_proj, ffn_norm, router, shared_gateup, shared_down, shared_switch, expert_gateup, expert_down = params
    segment, position, is_valid = layout(length_row)
    cosine, sine_table = rope_tables(position)
    normed = low(normalize(hidden_rows, attn_norm))
    projected = jnp.einsum('td,jdc->jtc', normed, qkv_proj, precision=HIGH) + qkv_bias.reshape(3, 1, HEADS * HD)
    projected = low_back(projected)
    queries = low_back(low(rotate(projected[0], cosine, sine_table)))
    key_rows = low_back(low(rotate(projected[1], cosine, sine_table)))
    values = low_back(low(projected[2]))
    mixed = low_back(low(attend(queries, key_rows, values, segment, position, is_valid)))
    middle = hidden_rows + low_back(jnp.dot(mixed, out_proj, precision=HIGH))
    normed_two = low(normalize(middle, ffn_norm))
    probs = jax.nn.softmax(jnp.dot(normed_two, router, precision=HIGH), axis=-1)
    chosen = jnp.take_along_axis(probs, route_rows, axis=1)
    capacity = N_SP * CAP
    token_index = jnp.arange(PACK, dtype=jnp.int32)
    mixture = jnp.zeros((PACK, D), jnp.float32)
    for expert in range(EXPERTS):
        picked = route_rows == expert
        routed = jnp.any(picked, axis=1)
        weight_row = lax.optimization_barrier(jnp.sum(jnp.where(picked, chosen, 0.0), axis=1))
        order = jnp.argsort(jnp.where(routed, token_index, PACK + token_index)).astype(jnp.int32)[:capacity]
        rows_in = low_back(normed_two[order])
        gate_up = jnp.einsum('td,dgf->tgf', rows_in, expert_gateup[expert], precision=HIGH)
        gate_part = low_back(gate_up[:, 0])
        up_part = low_back(gate_up[:, 1])
        acted = low(jax.nn.silu(gate_part) * up_part)
        result = low_back(low(jnp.dot(acted, expert_down[expert], precision=HIGH)))
        mixture = mixture.at[order].add(result * weight_row[order][:, None])
    shared_mid = jnp.einsum('td,dgf->tgf', normed_two, shared_gateup, precision=HIGH)
    gate_half = low_back(shared_mid[:, 0])
    up_half = low_back(shared_mid[:, 1])
    shared_act = low(jax.nn.silu(gate_half) * up_half)
    shared_out = low_back(jnp.dot(shared_act, shared_down, precision=HIGH))
    switch = jax.nn.sigmoid(jnp.dot(normed_two, shared_switch, precision=HIGH))
    output = middle + mixture + switch[:, None] * shared_out
    error = (output - teacher_rows) * is_valid[:, None].astype(jnp.float32)
    return (output, 0.5 * jnp.sum(error * error))

def reference(hidden_in, teacher, seq_lengths, routes, attn_norm, qkv_proj, qkv_bias, out_proj, ffn_norm, router, shared_gateup, shared_down, shared_switch, expert_gateup, expert_down):
    params = tuple((item.astype(jnp.float32) for item in (attn_norm, qkv_proj, qkv_bias, out_proj, ffn_norm, router, shared_gateup, shared_down, shared_switch, expert_gateup, expert_down)))
    stacked = hidden_in.astype(jnp.float32).reshape(N_DP, PACK, D)
    targets = teacher.astype(jnp.float32).reshape(N_DP, PACK, D)
    route_groups = routes.reshape(N_DP, PACK, TOP)

    def whole(weights, inputs):

        def one_group(running, items):
            output, half_sum = group_forward(weights, items[0], items[1], items[2], items[3])
            return (running + half_sum, output)
        summed, outputs = lax.scan(jax.checkpoint(one_group), jnp.zeros((), jnp.float32), (inputs, targets, route_groups, seq_lengths))
        return (outputs, summed)
    (outputs, summed), pullback = jax.vjp(whole, params, stacked)
    weight_grads, input_grads = pullback((jnp.zeros_like(outputs), jnp.ones_like(summed)))
    count = jnp.sum(seq_lengths).astype(jnp.float32)
    loss_value = summed / (count * D)
    return (outputs.reshape(N_DP * PACK, D), loss_value, input_grads.reshape(N_DP * PACK, D), weight_grads[0], weight_grads[1], weight_grads[2], weight_grads[3], weight_grads[4], weight_grads[5], weight_grads[6], weight_grads[7], weight_grads[8], weight_grads[9], weight_grads[10])
```

```python
import jax
import jax.numpy as jnp
from jax import lax
from jax.sharding import PartitionSpec as P

D = 2048
HD = 128
BLK = 128
MAXSEQ = 8

EPS = 1e-06
THETA = 1000000.0
FLOOR = -1e30
HIGH = lax.Precision.HIGHEST
BF = jnp.bfloat16
F32 = jnp.float32

ORDER = (0, 2, 4, 6, 1, 3, 5, 7)


def barrier(*values):
    return lax.optimization_barrier(values)


def dot(left, right, dims, dtype=F32):
    return lax.dot_general(left, right, (dims, ((), ())), preferred_element_type=F32).astype(dtype)


def swap(values, distance):
    return lax.ppermute(values, "sp", [(i, i ^ distance) for i in range(8)])


def gather_rows(own):
    half = own.shape[0] // 2
    over_x, over_y, over_c = swap(own, 2), swap(own, 4), swap(own, 1)
    far_top, far_bottom = swap(over_y[:half], 2), swap(over_x[half:], 4)
    far = jnp.concatenate([far_top, far_bottom], 0)
    rest = [swap(over_x, 1), swap(over_y, 1), swap(far, 1)]
    return jnp.concatenate([own, over_x, over_y, far, over_c] + rest, 0)


def gather_small(own):
    held = own[None]
    for distance in (2, 4, 1):
        held = jnp.concatenate([held, swap(held, distance)], 0)
    return held


def sum_small(parts):
    for distance in (1, 4, 2):
        keep = parts.shape[0] // 2
        parts = parts[:keep] + swap(parts[keep:], distance)
    return parts[0]


def sum_rows(upper, lower):
    rows = lower.shape[0] // 4
    half = rows // 2
    got = swap(upper, 1)
    chip = lower.astype(F32) + got.astype(F32)
    low = chip.astype(BF)
    own, over_x, over_y, far = (slice(k * rows, (k + 1) * rows) for k in range(4))
    low_x, low_y, low_far = low[over_x], low[over_y], low[far]
    from_x = swap(jnp.concatenate([low_far[:half], low_x[:half]], 0), 2)
    from_y = swap(jnp.concatenate([low_far[half:], low_y[half:]], 0), 4)
    pass_y = (chip[over_y][:half] + from_x[:half].astype(F32)).astype(BF)
    pass_x = (chip[over_x][half:] + from_y[:half].astype(F32)).astype(BF)
    last_y, last_x = swap(pass_y, 4), swap(pass_x, 2)
    mine = chip[own]
    top = mine[:half] + from_x[half:].astype(F32) + last_y.astype(F32)
    bottom = mine[half:] + from_y[half:].astype(F32) + last_x.astype(F32)
    return jnp.concatenate([top, bottom], 0)


def sum_groups(grads, dim):
    return lax.psum_scatter(grads, "dp", scatter_dimension=dim, tiled=True).astype(F32)


def shift_groups(blocks):
    size = lax.axis_size("dp")
    me = lax.axis_index("dp")
    pick = lambda k: lax.dynamic_index_in_dim(blocks, (me + k) % size, 0, keepdims=False)
    total = pick(0)
    for k in range(1, size):
        total = total + lax.ppermute(pick(k), "dp", [(i, (i + k) % size) for i in range(size)])
    return total


def sum_everywhere(values):
    for distance in (1, 2, 4):
        values = values + swap(values, distance)
    size = lax.axis_size("dp")
    step = 1
    while step < size:
        values = values + lax.ppermute(values, "dp", [(i, i ^ step) for i in range(size)])
        step *= 2
    return values


def layout(length_row, place):
    blocks = (length_row + BLK - 1) // BLK
    ends = jnp.cumsum(blocks)
    starts = ends - blocks
    which = jnp.sum((place[:, None] // BLK >= ends[None, :]).astype(jnp.int32), axis=1)
    member = which[:, None] == jnp.arange(length_row.shape[0], dtype=jnp.int32)[None, :]
    opening = jnp.sum(jnp.where(member, starts[None, :], 0), axis=1)
    seq_len = jnp.sum(jnp.where(member, length_row[None, :], 0), axis=1)
    position = place - opening * BLK
    return (which, position, position < seq_len)


def rope_tables(position):
    half_dim = HD // 2
    freq = THETA ** (-2.0 * jnp.arange(half_dim, dtype=F32) / HD)
    angle = position.astype(F32)[:, None] * freq[None, :]
    return (
        jnp.concatenate([jnp.cos(angle), jnp.cos(angle)], -1),
        jnp.concatenate([jnp.sin(angle), jnp.sin(angle)], -1),
    )


def rotate(flat_rows, cosine, sine_table):
    count = flat_rows.shape[0]
    shaped = flat_rows.reshape(count, -1, HD)
    half_dim = HD // 2
    turned = jnp.concatenate([-shaped[..., half_dim:], shaped[..., :half_dim]], -1)
    return (shaped * cosine[:, None, :] + turned * sine_table[:, None, :]).reshape(count, -1)


def rotate_back(flat_rows, cosine, sine_table):
    count = flat_rows.shape[0]
    shaped = flat_rows.reshape(count, -1, HD)
    half_dim = HD // 2
    sined = shaped * sine_table[:, None, :]
    turned = jnp.concatenate([sined[..., half_dim:], -sined[..., :half_dim]], -1)
    return (shaped * cosine[:, None, :] + turned).reshape(count, -1)


def normalize(values, gain_vec):
    inverse = lax.rsqrt(jnp.mean(values * values, axis=-1, keepdims=True) + EPS)
    return (values * inverse * gain_vec, inverse)


def norm_back(values, inverse, gain_vec, gradient):
    scaled = values * inverse
    gain_term = jnp.sum(gradient * scaled, axis=0)
    grad_scaled = gradient * gain_vec
    back = inverse * (grad_scaled - scaled * jnp.mean(grad_scaled * scaled, axis=-1, keepdims=True))
    return (back, gain_term)


def silu_slope(values):
    sig = jax.nn.sigmoid(values)
    return sig * (1.0 + values * (1.0 - sig))


def scores_of(queries, key_rows, allowed):
    scores = dot(queries, key_rows, ((1,), (1,))) * HD ** (-0.5)
    return jnp.where(allowed, scores, FLOOR)


def attend_forward(queries, key_rows, values, allowed):
    pieces, totals = [], []
    for start in range(0, queries.shape[1], HD):
        head = slice(start, start + HD)
        scores = scores_of(queries[:, head], key_rows[:, head], allowed)
        peak = jnp.max(scores, axis=-1, keepdims=True)
        expon = jnp.exp(scores - peak)
        summed = jnp.sum(expon, axis=-1, keepdims=True)
        weights = (expon / summed).astype(BF)
        pieces.append(dot(weights, values[:, head], ((1,), (0,)), BF))
        totals.append(peak + jnp.log(summed))
    return (jnp.concatenate(pieces, 1), totals)


def attend_back(queries, key_rows, values, allowed, totals, grad_mixed):
    scale = HD ** (-0.5)
    grads = ([], [], [])
    for start, total in zip(range(0, queries.shape[1], HD), totals):
        head = slice(start, start + HD)
        block_q, block_k, block_g = queries[:, head], key_rows[:, head], grad_mixed[:, head]
        probs = jnp.exp(scores_of(block_q, block_k, allowed) - total)
        grad_p = dot(block_g, values[:, head], ((1,), (1,)))
        grad_s = (probs * (grad_p - jnp.sum(probs * grad_p, axis=-1, keepdims=True))).astype(BF)
        grads[0].append((dot(grad_s, block_k, ((1,), (0,))) * scale).astype(BF))
        grads[1].append((dot(grad_s, block_q, ((0,), (0,))) * scale).astype(BF))
        grads[2].append(dot(probs.astype(BF), block_g, ((0,), (0,)), BF))
    return tuple(jnp.concatenate(g, 1) for g in grads)


def on_device(
    hidden_in,
    teacher,
    seq_lengths,
    routes,
    attn_norm,
    qkv_proj,
    qkv_bias,
    out_proj,
    ffn_norm,
    router,
    shared_gateup,
    shared_down,
    shared_switch,
    expert_gateup,
    expert_down,
):
    tok_rows, width = hidden_in.shape
    sp_size = lax.axis_size("sp")
    dp_size = lax.axis_size("dp")
    me = lax.axis_index("sp")
    total_rows = tok_rows * sp_size
    lower_rows = total_rows // 2
    experts = router.shape[1]
    top_k = routes.shape[1]
    capacity = sp_size * min(tok_rows, 9 * tok_rows * top_k // (8 * experts))

    inputs = hidden_in.astype(F32)
    gain_one = attn_norm.astype(F32)
    normed_f, inverse_one = normalize(inputs, gain_one)
    normed_all = gather_rows(normed_f.astype(BF))
    route_all = gather_small(routes.T)

    owners = me ^ jnp.array(ORDER, jnp.int32)
    place = (owners[:, None] * tok_rows + jnp.arange(tok_rows, dtype=jnp.int32)[None, :]).reshape(-1)
    length_row = lax.dynamic_index_in_dim(seq_lengths, lax.axis_index("dp"), 0, keepdims=False)
    segment, position, is_valid = layout(length_row, place)
    cosine, sine_table = rope_tables(position)
    local_valid = is_valid[:tok_rows].astype(F32)
    allowed = (
        (segment[:, None] == segment[None, :])
        & (position[None, :] <= position[:, None])
        & is_valid[None, :]
    )

    mask = jnp.any(route_all == me, axis=1).reshape(total_rows)
    slot = jnp.cumsum(mask.astype(jnp.int32)) - 1
    slot = jnp.where(mask, slot, -1)
    pick = (slot[None, :] == jnp.arange(capacity, dtype=jnp.int32)[:, None]).astype(BF)

    bias = qkv_bias.reshape(3, 1, -1).astype(F32)
    projected = [dot(normed_all, qkv_proj[j], ((1,), (0,))) + bias[j] for j in range(3)]
    queries = rotate(projected[0], cosine, sine_table).astype(BF)
    key_rows = rotate(projected[1], cosine, sine_table).astype(BF)
    values = projected[2].astype(BF)
    mixed, totals = attend_forward(queries, key_rows, values, allowed)
    upper = dot(mixed[lower_rows:], out_proj, ((1,), (0,)), BF)
    lower = dot(mixed[:lower_rows], out_proj, ((1,), (0,)), BF)
    middle = inputs + sum_rows(upper, lower)

    gain_two = ffn_norm.astype(F32)
    normed_two_f, inverse_two = normalize(middle, gain_two)
    normed_two = normed_two_f.astype(BF)
    two_all = gather_rows(normed_two)

    heads_in = jnp.concatenate([router, shared_switch[:, None]], axis=1)
    logits = dot(two_all, heads_in, ((1,), (0,)))
    probs = jax.nn.softmax(logits[:, :experts], axis=-1)
    switch = jax.nn.sigmoid(logits[:, experts:])
    is_me = (jnp.arange(experts) == me).astype(F32)
    share = jnp.sum(probs * is_me[None, :], axis=1) * mask.astype(F32)
    share_rows = jnp.sum(pick.astype(F32) * share[None, :], axis=1, keepdims=True)

    gate_w, up_w = expert_gateup[0, :, 0, :], expert_gateup[0, :, 1, :]
    down_w = expert_down[0]
    rows_in = dot(pick, two_all, ((1,), (0,)), BF)
    gate_e = dot(rows_in, gate_w, ((1,), (0,)))
    up_e = dot(rows_in, up_w, ((1,), (0,)))
    acted_e = (jax.nn.silu(gate_e) * up_e).astype(BF)
    made = dot(acted_e, down_w, ((1,), (0,)), BF)

    gate_sw, up_sw = shared_gateup[:, 0, :], shared_gateup[:, 1, :]
    gate_s = dot(two_all, gate_sw, ((1,), (0,)))
    up_s = dot(two_all, up_sw, ((1,), (0,)))
    acted_s = (jax.nn.silu(gate_s) * up_s).astype(BF)

    def ffn_part(rows):
        shared = dot(acted_s[rows], shared_down, ((1,), (0,)))
        routed = dot(pick[:, rows], made, ((0,), (0,)))
        return (switch[rows] * shared + share[rows, None] * routed).astype(BF)

    upper_half, lower_half = slice(lower_rows, None), slice(0, lower_rows)
    ffn_upper = ffn_part(upper_half)
    ffn_lower = ffn_part(lower_half)
    output = middle + sum_rows(ffn_upper, ffn_lower)

    error = (output - teacher.astype(F32)) * local_valid[:, None]
    squares = sum_everywhere(jnp.full((8, 128), jnp.sum(error * error), F32))[0, 0]
    count = jnp.sum(seq_lengths).astype(F32)
    loss_value = squares / (2.0 * count * D)

    error_all = gather_rows(error.astype(BF))
    rows_g = dot(pick, error_all, ((1,), (0,)))
    grad_made = (share_rows * rows_g).astype(BF)
    grad_acted = dot(grad_made, down_w, ((1,), (1,)))
    gain_rows = jnp.sum(acted_e.astype(F32) * grad_acted, axis=1, keepdims=True)
    grad_gate_e = (grad_acted * up_e * silu_slope(gate_e)).astype(BF)
    grad_up_e = (grad_acted * jax.nn.silu(gate_e)).astype(BF)
    gate_term = dot(rows_in, grad_gate_e, ((0,), (0,)), BF)
    up_term = dot(rows_in, grad_up_e, ((0,), (0,)), BF)
    down_term = dot(acted_e, grad_made, ((0,), (0,)), BF)
    expert_grads = (sum_groups(gate_term, 0), sum_groups(up_term, 0), sum_groups(down_term, 1))

    grad_shared = (switch * error_all.astype(F32)).astype(BF)
    grad_act_s = dot(grad_shared, shared_down, ((1,), (1,)))
    switch_part = jnp.sum(acted_s.astype(F32) * grad_act_s, axis=1)
    grad_gate_s = (grad_act_s * up_s * silu_slope(gate_s)).astype(BF)
    grad_up_s = (grad_act_s * jax.nn.silu(gate_s)).astype(BF)

    back_e = (dot(grad_gate_e, gate_w, ((1,), (1,))) + dot(grad_up_e, up_w, ((1,), (1,)))).astype(BF)

    def back_part(rows):
        return (
            dot(grad_gate_s[rows], gate_sw, ((1,), (1,)))
            + dot(grad_up_s[rows], up_sw, ((1,), (1,)))
            + dot(pick[:, rows], back_e, ((0,), (0,)))
        ).astype(BF)

    back_upper = back_part(upper_half)
    back_lower = back_part(lower_half)
    gain_tokens = jnp.sum(pick.astype(F32) * gain_rows, axis=0)
    scalars = jnp.concatenate(
        [gain_tokens[None, :] * is_me[:, None], switch_part[None, :], jnp.zeros((7, total_rows), F32)], axis=0
    )
    scalars = sum_small(scalars.reshape(16, sp_size, tok_rows).transpose(1, 0, 2))
    gains, switch_sum = scalars[:experts].T, scalars[experts]
    my_probs, my_switch = probs[:tok_rows], switch[:tok_rows, 0]
    grad_switch = switch_sum * (1.0 - my_switch)
    grad_logits = gains - my_probs * jnp.sum(gains, axis=1, keepdims=True)
    steer = jnp.concatenate([grad_logits, grad_switch[:, None]], axis=1)
    grad_normed = sum_rows(back_upper, back_lower) + jnp.einsum(
        "te,de->td", steer, heads_in.astype(F32), precision=HIGH
    )
    steer_term = jnp.einsum("te,td->ed", steer, normed_two.astype(F32), precision=HIGH)
    grad_middle_n, ffnnorm_term = norm_back(middle, inverse_two, gain_two, grad_normed)
    grad_middle = error + grad_middle_n

    shared_terms = (
        dot(two_all, grad_gate_s, ((0,), (0,)), BF),
        dot(two_all, grad_up_s, ((0,), (0,)), BF),
        dot(acted_s, grad_shared, ((0,), (0,)), BF),
    )

    attn_all = gather_rows(grad_middle.astype(BF))
    grad_mixed = dot(attn_all, out_proj, ((1,), (1,)), BF)
    grad_q, grad_k, grad_v = attend_back(
        queries, key_rows, values, allowed, totals, grad_mixed
    )
    grad_proj = (
        rotate_back(grad_q.astype(F32), cosine, sine_table).astype(BF),
        rotate_back(grad_k.astype(F32), cosine, sine_table).astype(BF),
        grad_v,
    )

    def input_part(rows):
        return sum(dot(grad_proj[j][rows], qkv_proj[j], ((1,), (1,))) for j in range(3)).astype(BF)

    input_upper = input_part(upper_half)
    input_lower = input_part(lower_half)
    grad_normed_one = sum_rows(input_upper, input_lower)
    grad_input_n, attnnorm_term = norm_back(inputs, inverse_one, gain_one, grad_normed_one)
    hidden_grad = grad_middle + grad_input_n
    outproj_term = dot(mixed, attn_all, ((0,), (0,)), BF)
    qkv_terms = jnp.stack([dot(normed_all, g, ((0,), (0,)), BF) for g in grad_proj], 0)
    bias_term = jnp.stack([jnp.sum(g.astype(F32), axis=0) for g in grad_proj], 0)

    shared_grads = (
        sum_groups(shared_terms[0], 0),
        sum_groups(shared_terms[1], 0),
        sum_groups(shared_terms[2], 1),
    )
    outproj_grad = sum_groups(outproj_term, 1)
    qkvproj_grad = sum_groups(qkv_terms, 1)

    small = jnp.concatenate([attnnorm_term[None], ffnnorm_term[None], steer_term], axis=0)
    kinds = small.shape[0]
    cell = width // (dp_size * sp_size)
    small = small.reshape(kinds, dp_size, sp_size, cell).transpose(2, 1, 0, 3)[owners]
    small = sum_small(small.reshape(sp_size, dp_size, kinds * cell))
    pairs = bias_term.reshape(-1, HD)
    bias_cells = pairs.reshape(pairs.shape[0], dp_size, -1).transpose(1, 0, 2).reshape(dp_size, -1)
    small = shift_groups(jnp.concatenate([small, bias_cells], axis=1))
    gains_out = small[: kinds * cell].reshape(kinds, cell)
    qkvbias_grad = small[kinds * cell :].reshape(3, -1, HD // dp_size)
    return (
        output,
        loss_value,
        hidden_grad,
        gains_out[0],
        qkvproj_grad,
        qkvbias_grad,
        outproj_grad,
        gains_out[1],
        gains_out[2 : 2 + experts].T,
        jnp.stack(shared_grads[:2], axis=1),
        shared_grads[2],
        gains_out[2 + experts],
        jnp.stack(expert_grads[:2], axis=1)[None],
        expert_grads[2][None],
    )


def solution(mesh):
    in_specs = (
        P(("dp", "sp"), None),
        P(("dp", "sp"), None),
        P(),
        P(("dp", "sp"), None),
        P(),
        P(None, None, "sp"),
        P(None, "sp", None),
        P("sp", None),
        P(),
        P(),
        P(None, None, "sp"),
        P("sp", None),
        P(),
        P("sp", None, None, None),
        P("sp", None, None),
    )
    out_specs = (
        P(("dp", "sp"), None),
        P(),
        P(("dp", "sp"), None),
        P(("dp", "sp")),
        P(None, "dp", "sp"),
        P(None, "sp", "dp"),
        P("sp", "dp"),
        P(("dp", "sp")),
        P(("dp", "sp"), None),
        P("dp", None, "sp"),
        P("sp", "dp"),
        P(("dp", "sp")),
        P("sp", "dp", None, None),
        P("sp", None, "dp"),
    )
    return jax.shard_map(
        on_device, mesh=mesh, in_specs=in_specs, out_specs=out_specs, check_vma=False
    )
```

```python
import jax
import jax.numpy as jnp
from jax import lax
from jax.experimental import pallas as pl
from jax.experimental.pallas import tpu as pltpu
from jax.sharding import PartitionSpec as P

D = 2048
HD = 128
BLK = 128
MAXSEQ = 8

EPS = 1e-06
THETA = 1000000.0
FLOOR = -1e30
HIGH = lax.Precision.HIGHEST
BF = jnp.bfloat16
F32 = jnp.float32

ORDER = (0, 2, 4, 6, 1, 3, 5, 7)


def after(values, work):
    values, work = tuple(values), tuple(work)
    if not work or not values:
        return values, work
    tied = lax.optimization_barrier((*values, *work))
    return tied[: len(values)], tied[len(values) :]


def between(first, last, task):
    if task is None:
        return tuple(last), ()
    function, *inputs = task
    inputs, _ = after(inputs, first)
    return after(last, function(*inputs))


def dot(left, right, dims, dtype=F32):
    return lax.dot_general(left, right, (dims, ((), ())), preferred_element_type=F32).astype(dtype)


def swap(values, distance):
    return lax.ppermute(values, "sp", [(i, i ^ distance) for i in range(8)])


def gather_rows(own, task=None):
    half = own.shape[0] // 2
    over_x, over_y = swap(own, 2), swap(own, 4)
    (over_x, over_y), work = between((own,), (over_x, over_y), task)
    far_top, far_bottom = swap(over_y[:half], 2), swap(over_x[half:], 4)
    lower = jnp.concatenate([own, over_x, over_y, far_top, far_bottom], 0)
    return lower, swap(lower, 1), work


def gather_far(own):
    same = lax.all_gather(own, "sp", axis_index_groups=[[0, 2, 4, 6], [1, 3, 5, 7]])
    return same, swap(same, 1)


def gather_small(own):
    held = own[None]
    for distance in (2, 4, 1):
        held = jnp.concatenate([held, swap(held, distance)], 0)
    return held


def sum_small(parts, total):
    for distance in (1, 4, 2):
        keep = parts.shape[0] // 2
        got = swap(jnp.concatenate([parts[keep:], total], 0), distance)
        parts, total = parts[:keep] + got[:keep], total + got[keep:]
    return parts[0], total[0]


def sum_rows(upper, lower, task=None):
    rows = lower.shape[0] // 4
    half = rows // 2
    got = swap(upper, 1)
    chip = lower.astype(F32) + got.astype(F32)
    low = chip.astype(BF)
    own, over_x, over_y, far = (slice(k * rows, (k + 1) * rows) for k in range(4))
    low_x, low_y, low_far = low[over_x], low[over_y], low[far]
    from_x = swap(jnp.concatenate([low_far[:half], low_x[:half]], 0), 2)
    from_y = swap(jnp.concatenate([low_far[half:], low_y[half:]], 0), 4)
    (from_x, from_y), work = between((low,), (from_x, from_y), task)
    pass_y = (chip[over_y][:half] + from_x[:half].astype(F32)).astype(BF)
    pass_x = (chip[over_x][half:] + from_y[:half].astype(F32)).astype(BF)
    last_y, last_x = swap(pass_y, 4), swap(pass_x, 2)
    mine = chip[own]
    top = mine[:half] + from_x[half:].astype(F32) + last_y.astype(F32)
    bottom = mine[half:] + from_y[half:].astype(F32) + last_x.astype(F32)
    return jnp.concatenate([top, bottom], 0), work


def sum_groups(grads, dim):
    return lax.psum_scatter(grads, "dp", scatter_dimension=dim, tiled=True).astype(F32)


def shift_groups(blocks, total):
    size = lax.axis_size("dp")
    me = lax.axis_index("dp")
    pick = lambda k: lax.dynamic_index_in_dim(blocks, (me + k) % size, 0, keepdims=False)
    mine = jnp.stack([pick(0), total])
    summed = mine[0]
    totals = jnp.zeros((size,) + total.shape, total.dtype).at[me].set(total)
    for k in range(1, size):
        got = lax.ppermute(jnp.stack([pick(k), total]), "dp", [(i, (i + k) % size) for i in range(size)])
        summed = summed + got[0]
        totals = totals.at[(me - k) % size].set(got[1])
    return summed, jnp.sum(totals, axis=0)


def fetch_groups(own):
    size = lax.axis_size("dp")
    return [lax.ppermute(own, "dp", [((i + k) % size, i) for i in range(size)]) for k in range(1, size)]


def own_columns(values, axis):
    share = values.shape[axis] // lax.axis_size("dp")
    return lax.dynamic_slice_in_dim(values, lax.axis_index("dp") * share, share, axis)


def slots_of(mask):
    return jnp.where(mask, jnp.cumsum(mask.astype(jnp.int32), axis=-1) - 1, -1)


def local_call(kernel, name, flops, **spec):
    return pl.pallas_call(
        kernel,
        name=name,
        cost_estimate=pl.CostEstimate(flops=flops, bytes_accessed=flops // 300, transcendentals=0),
        compiler_params=pltpu.CompilerParams(vmem_limit_bytes=56 * 2**20),
        **spec,
    )


def pick_kernel(slot_ref, scale_ref, lower_ref, upper_ref, out_ref):
    capacity, columns = out_ref.shape
    total = slot_ref.shape[-1]
    chosen = (slot_ref[...] == lax.broadcasted_iota(jnp.int32, (capacity, total), 0)).astype(F32).astype(BF)
    half = total // 2
    rows = jnp.dot(chosen[:, :half], lower_ref[...].reshape(half, columns), preferred_element_type=F32)
    rows += jnp.dot(chosen[:, half:], upper_ref[...].reshape(half, columns), preferred_element_type=F32)
    out_ref[...] = (rows * scale_ref[...]).astype(BF)


def pick_rows(slots, scale, lower, upper):
    blocks, groups, count, width = lower.shape
    total = 2 * blocks * count
    capacity = scale.shape[1]
    tile = 1024
    rows = pl.BlockSpec((blocks, None, count, tile), lambda g, j: (0, g, 0, j))
    return local_call(
        pick_kernel,
        "pick_rows",
        2 * groups * capacity * total * width,
        grid=(groups, width // tile),
        in_specs=[
            pl.BlockSpec((None, 1, total), lambda g, j: (g, 0, 0)),
            pl.BlockSpec((None, capacity, 1), lambda g, j: (g, 0, 0)),
            rows,
            rows,
        ],
        out_specs=pl.BlockSpec((None, capacity, tile), lambda g, j: (g, 0, j)),
        out_shape=jax.ShapeDtypeStruct((groups, capacity, width), BF),
    )(slots[:, None, :], scale, lower, upper)


def dot_nn(left, right):
    return lax.dot_general(left, right, (((1,), (0,)), ((), ())), preferred_element_type=F32)


def dot_nt(left, right):
    return lax.dot_general(left, right, (((1,), (1,)), ((), ())), preferred_element_type=F32)


def dot_tn(left, right):
    return lax.dot_general(left, right, (((0,), (0,)), ((), ())), preferred_element_type=F32)


def expert_kernel(x_ref, gateup_w, down_w, gate_ref, up_ref, act_ref, made_ref):
    x = x_ref[...]
    gate, up = dot_nn(x, gateup_w[0]), dot_nn(x, gateup_w[1])
    gate_ref[...], up_ref[...] = gate, up
    act = (gate * jax.nn.sigmoid(gate) * up).astype(BF)
    act_ref[...] = act
    made_ref[...] = dot_nn(act, down_w[...]).astype(BF)


def row_spec(block, columns):
    return pl.BlockSpec((block, columns), lambda i: (i, 0))


def held_spec(array):
    return pl.BlockSpec(array.shape, lambda i: (0,) * array.ndim, pipeline_mode=pl.Buffered(1))


def row_block(count):
    return max(b for b in range(16, min(count, 288) + 1, 16) if count % b == 0)


def expert_forward(x, gateup_w, down_w):
    count, width = x.shape
    hidden = gateup_w.shape[2]
    block = row_block(count)
    wide_shape = lambda dtype: jax.ShapeDtypeStruct((count, hidden), dtype)
    return local_call(
        expert_kernel,
        "expert_forward",
        6 * count * width * hidden,
        grid=(count // block,),
        in_specs=[row_spec(block, width), held_spec(gateup_w), held_spec(down_w)],
        out_specs=[row_spec(block, hidden)] * 3 + [row_spec(block, width)],
        out_shape=[wide_shape(F32), wide_shape(F32), wide_shape(BF), jax.ShapeDtypeStruct((count, width), BF)],
    )(x, gateup_w, down_w)


def middle_grads(gate, up, grad):
    sig = jax.nn.sigmoid(gate)
    slope = sig * (1.0 + gate * (1.0 - sig))
    return (grad * up * slope).astype(BF), (grad * (gate * sig)).astype(BF)


def expert_back_kernel(g_ref, gate_ref, up_ref, act_ref, gateup_w, down_w, gg_ref, gu_ref, back_ref, gain_ref):
    grad = dot_nt(g_ref[...], down_w[...])
    gain_ref[...] = jnp.sum(act_ref[...].astype(F32) * grad, axis=1, keepdims=True)
    grad_gate, grad_up = middle_grads(gate_ref[...], up_ref[...], grad)
    gg_ref[...], gu_ref[...] = grad_gate, grad_up
    back_ref[...] = (dot_nt(grad_gate, gateup_w[0]) + dot_nt(grad_up, gateup_w[1])).astype(BF)


def expert_back(g, gate, up, act, gateup_w, down_w):
    count, width = g.shape
    hidden = gateup_w.shape[2]
    block = row_block(count)
    rows, mids = row_spec(block, width), row_spec(block, hidden)
    return local_call(
        expert_back_kernel,
        "expert_back",
        6 * count * width * hidden,
        grid=(count // block,),
        in_specs=[rows, mids, mids, mids, held_spec(gateup_w), held_spec(down_w)],
        out_specs=[mids, mids, rows, row_spec(block, 1)],
        out_shape=[jax.ShapeDtypeStruct((count, hidden), BF)] * 2
        + [jax.ShapeDtypeStruct((count, width), BF), jax.ShapeDtypeStruct((count, 1), F32)],
    )(g, gate, up, act, gateup_w, down_w)


def expert_far_kernel(x_ref, g_ref, gateup_w, down_w, act_ref, gg_ref, gu_ref):
    x = x_ref[...]
    gate, up = dot_nn(x, gateup_w[0]), dot_nn(x, gateup_w[1])
    act_ref[...] = (gate * jax.nn.sigmoid(gate) * up).astype(BF)
    gg_ref[...], gu_ref[...] = middle_grads(gate, up, dot_nt(g_ref[...], down_w[...]))


def expert_far(x, g, gateup_w, down_w):
    count, width = x.shape
    hidden = gateup_w.shape[2]
    block = row_block(count)
    rows, mids = row_spec(block, width), row_spec(block, hidden)
    return local_call(
        expert_far_kernel,
        "expert_far",
        6 * count * width * hidden,
        grid=(count // block,),
        in_specs=[rows, rows, held_spec(gateup_w), held_spec(down_w)],
        out_specs=[mids] * 3,
        out_shape=[jax.ShapeDtypeStruct((count, hidden), BF)] * 3,
    )(x, g, gateup_w, down_w)


def expert_grad_kernel(_, x, g, act, gg, gu, far_x, far_g, far_act, far_gg, far_gu, gateup_ref, down_ref, acc_g, acc_u):
    step = pl.program_id(0)

    @pl.when(step == 0)
    def _():
        rows = x[...]
        acc_g[...] = dot_tn(rows, gg[...])
        acc_u[...] = dot_tn(rows, gu[...])
        down_ref[...] = dot_tn(act[...], g[...])

    @pl.when(step > 0)
    def _():
        rows = far_x[...]
        acc_g[...] += dot_tn(rows, far_gg[...])
        acc_u[...] += dot_tn(rows, far_gu[...])
        down_ref[...] += dot_tn(far_act[...], far_g[...])

    @pl.when(step == pl.num_programs(0) - 1)
    def _():
        gateup_ref[:, 0, :] = acc_g[...]
        gateup_ref[:, 1, :] = acc_u[...]


def expert_grads_of(own, far):
    count, width = own[0].shape
    hidden = own[2].shape[1]
    share = width // lax.axis_size("dp")
    steps = 1 + far[0].shape[0] // count
    held = lambda i, d: (0, 0)
    near_rows = pl.BlockSpec((count, share), lambda i, d: (0, d[0]))
    near_mid = pl.BlockSpec((count, hidden), held)
    far_rows = pl.BlockSpec((count, share), lambda i, d: (jnp.maximum(i - 1, 0), d[0]))
    far_mid = pl.BlockSpec((count, hidden), lambda i, d: (jnp.maximum(i - 1, 0), 0))
    return local_call(
        expert_grad_kernel,
        "expert_grads",
        6 * count * steps * share * hidden,
        grid_spec=pltpu.PrefetchScalarGridSpec(
            num_scalar_prefetch=1,
            grid=(steps,),
            in_specs=[near_rows, near_rows] + [near_mid] * 3 + [far_rows, far_rows] + [far_mid] * 3,
            out_specs=[
                pl.BlockSpec((share, 2, hidden), lambda i, d: (0, 0, 0)),
                pl.BlockSpec((hidden, share), held),
            ],
            scratch_shapes=[pltpu.VMEM((share, hidden), F32)] * 2,
        ),
        out_shape=[
            jax.ShapeDtypeStruct((share, 2, hidden), F32),
            jax.ShapeDtypeStruct((hidden, share), F32),
        ],
    )(lax.axis_index("dp").reshape(1), *own, *far)


def layout(length_row, place):
    blocks = (length_row + BLK - 1) // BLK
    ends = jnp.cumsum(blocks)
    starts = ends - blocks
    which = jnp.sum((place[:, None] // BLK >= ends[None, :]).astype(jnp.int32), axis=1)
    member = which[:, None] == jnp.arange(length_row.shape[0], dtype=jnp.int32)[None, :]
    opening = jnp.sum(jnp.where(member, starts[None, :], 0), axis=1)
    seq_len = jnp.sum(jnp.where(member, length_row[None, :], 0), axis=1)
    position = place - opening * BLK
    return (which, position, position < seq_len)


def rope_tables(position):
    half_dim = HD // 2
    freq = THETA ** (-2.0 * jnp.arange(half_dim, dtype=F32) / HD)
    angle = position.astype(F32)[:, None] * freq[None, :]
    return (
        jnp.concatenate([jnp.cos(angle), jnp.cos(angle)], -1),
        jnp.concatenate([jnp.sin(angle), jnp.sin(angle)], -1),
    )


def rotate(flat_rows, cosine, sine_table):
    count = flat_rows.shape[0]
    shaped = flat_rows.reshape(count, -1, HD)
    half_dim = HD // 2
    turned = jnp.concatenate([-shaped[..., half_dim:], shaped[..., :half_dim]], -1)
    return (shaped * cosine[:, None, :] + turned * sine_table[:, None, :]).reshape(count, -1)


def rotate_back(flat_rows, cosine, sine_table):
    count = flat_rows.shape[0]
    shaped = flat_rows.reshape(count, -1, HD)
    half_dim = HD // 2
    sined = shaped * sine_table[:, None, :]
    turned = jnp.concatenate([sined[..., half_dim:], -sined[..., :half_dim]], -1)
    return (shaped * cosine[:, None, :] + turned).reshape(count, -1)


def normalize(values, gain_vec):
    inverse = lax.rsqrt(jnp.mean(values * values, axis=-1, keepdims=True) + EPS)
    return (values * inverse * gain_vec, inverse)


def norm_back(values, inverse, gain_vec, gradient):
    scaled = values * inverse
    gain_term = jnp.sum(gradient * scaled, axis=0)
    grad_scaled = gradient * gain_vec
    back = inverse * (grad_scaled - scaled * jnp.mean(grad_scaled * scaled, axis=-1, keepdims=True))
    return (back, gain_term)


def silu_slope(values):
    sig = jax.nn.sigmoid(values)
    return sig * (1.0 + values * (1.0 - sig))


def scores_of(queries, key_rows, allowed):
    scores = dot(queries, key_rows, ((1,), (1,))) * HD ** (-0.5)
    return jnp.where(allowed, scores, FLOOR)


def attend_forward(queries, key_rows, values, allowed):
    pieces, totals = [], []
    for start in range(0, queries.shape[1], HD):
        head = slice(start, start + HD)
        scores = scores_of(queries[:, head], key_rows[:, head], allowed)
        peak = jnp.max(scores, axis=-1, keepdims=True)
        expon = jnp.exp(scores - peak)
        summed = jnp.sum(expon, axis=-1, keepdims=True)
        weights = (expon / summed).astype(BF)
        pieces.append(dot(weights, values[:, head], ((1,), (0,)), BF))
        totals.append(peak + jnp.log(summed))
    return (jnp.concatenate(pieces, 1), totals)


def attend_back(queries, key_rows, values, allowed, totals, grad_mixed):
    scale = HD ** (-0.5)
    grads = ([], [], [])
    for start, total in zip(range(0, queries.shape[1], HD), totals):
        head = slice(start, start + HD)
        block_q, block_k, block_g = queries[:, head], key_rows[:, head], grad_mixed[:, head]
        probs = jnp.exp(scores_of(block_q, block_k, allowed) - total)
        grad_p = dot(block_g, values[:, head], ((1,), (1,)))
        grad_s = (probs * (grad_p - jnp.sum(probs * grad_p, axis=-1, keepdims=True))).astype(BF)
        grads[0].append((dot(grad_s, block_k, ((1,), (0,))) * scale).astype(BF))
        grads[1].append((dot(grad_s, block_q, ((0,), (0,))) * scale).astype(BF))
        grads[2].append(dot(probs.astype(BF), block_g, ((0,), (0,)), BF))
    return tuple(jnp.concatenate(g, 1) for g in grads)


def on_device(
    hidden_in,
    teacher,
    seq_lengths,
    routes,
    attn_norm,
    qkv_proj,
    qkv_bias,
    out_proj,
    ffn_norm,
    router,
    shared_gateup,
    shared_down,
    shared_switch,
    expert_gateup,
    expert_down,
):
    tok_rows, width = hidden_in.shape
    sp_size = lax.axis_size("sp")
    dp_size = lax.axis_size("dp")
    me = lax.axis_index("sp")
    total_rows = tok_rows * sp_size
    lower_rows = total_rows // 2
    experts = router.shape[1]
    top_k = routes.shape[1]
    capacity = sp_size * min(tok_rows, 9 * tok_rows * top_k // (8 * experts))

    inputs = hidden_in.astype(F32)
    gain_one = attn_norm.astype(F32)
    normed_f, inverse_one = normalize(inputs, gain_one)
    *normed_halves, (gateup_w,) = gather_rows(
        normed_f.astype(BF), (lambda w: (w.transpose(1, 0, 2),), expert_gateup[0])
    )
    wide = dp_size <= 4
    route_own = routes.T[None]
    if wide:
        route_own = jnp.concatenate([route_own] + fetch_groups(route_own), 0)
    route_all = gather_small(route_own.reshape(-1, tok_rows))
    route_all = route_all.reshape(sp_size, -1, top_k, tok_rows)

    owners = me ^ jnp.array(ORDER, jnp.int32)
    place = (owners[:, None] * tok_rows + jnp.arange(tok_rows, dtype=jnp.int32)[None, :]).reshape(-1)
    length_row = lax.dynamic_index_in_dim(seq_lengths, lax.axis_index("dp"), 0, keepdims=False)
    segment, position, is_valid = layout(length_row, place)
    cosine, sine_table = rope_tables(position)
    local_valid = is_valid[:tok_rows].astype(F32)
    allowed = (
        (segment[:, None] == segment[None, :])
        & (position[None, :] <= position[:, None])
        & is_valid[None, :]
    )

    masks = jnp.any(route_all == me, axis=2)
    mask = masks[:, 0].reshape(total_rows)
    slots = slots_of(mask)[None]
    slot_range = jnp.arange(capacity, dtype=jnp.int32)
    pick = (slots[0][None, :] == slot_range[:, None]).astype(BF)

    bias = qkv_bias.reshape(3, 1, -1).astype(F32)
    projected = [
        jnp.concatenate([dot(rows, qkv_proj[j], ((1,), (0,))) for rows in normed_halves], 0) + bias[j]
        for j in range(3)
    ]
    queries = rotate(projected[0], cosine, sine_table).astype(BF)
    key_rows = rotate(projected[1], cosine, sine_table).astype(BF)
    values = projected[2].astype(BF)
    mixed, totals = attend_forward(queries, key_rows, values, allowed)
    upper = dot(mixed[lower_rows:], out_proj, ((1,), (0,)), BF)
    lower = dot(mixed[:lower_rows], out_proj, ((1,), (0,)), BF)
    middle = inputs + sum_rows(upper, lower)[0]

    gain_two = ffn_norm.astype(F32)
    normed_two_f, inverse_two = normalize(middle, gain_two)
    normed_two = normed_two_f.astype(BF)
    *two_halves, _ = gather_rows(normed_two)
    fetched_two = fetch_groups(normed_two) if wide else []

    heads_in = jnp.concatenate([router, shared_switch[:, None]], axis=1)
    is_me = (jnp.arange(experts) == me).astype(F32)

    def steer_rows(rows):
        logits = dot(rows, heads_in, ((1,), (0,)))
        return jax.nn.softmax(logits[:, :experts], axis=-1), jax.nn.sigmoid(logits[:, experts:])

    steered = [steer_rows(rows) for rows in two_halves]
    probs, switch = (jnp.concatenate(both, 0) for both in zip(*steered))
    share = jnp.sum(probs * is_me[None, :], axis=1) * mask.astype(F32)
    share_rows = jnp.sum(pick.astype(F32) * share[None, :], axis=1, keepdims=True)

    down_w = expert_down[0]
    blocks = (sp_size // 2, 1, tok_rows, width)
    ones = jnp.ones((1, capacity, 1), F32)
    rows_in = pick_rows(slots, ones, *(rows.reshape(blocks) for rows in two_halves))[0]
    gate_e, up_e, acted_e, made = expert_forward(rows_in, gateup_w, down_w)

    gate_sw, up_sw = shared_gateup[:, 0, :], shared_gateup[:, 1, :]
    gate_s = [dot(rows, gate_sw, ((1,), (0,))) for rows in two_halves]
    up_s = [dot(rows, up_sw, ((1,), (0,))) for rows in two_halves]
    acted_s = [(jax.nn.silu(g) * u).astype(BF) for g, u in zip(gate_s, up_s)]
    (acted_s[1],), fetched_two = after((acted_s[1],), fetched_two)
    if wide:
        two_far = gather_far(jnp.stack(fetched_two, 0))
    halves = (slice(0, lower_rows), slice(lower_rows, None))

    def ffn_part(side):
        rows = halves[side]
        shared = dot(acted_s[side], shared_down, ((1,), (0,)))
        routed = dot(pick[:, rows], made, ((0,), (0,)))
        return (steered[side][1] * shared + share[rows, None] * routed).astype(BF)

    ffn_upper = ffn_part(1)
    ffn_lower = ffn_part(0)
    output = middle + sum_rows(ffn_upper, ffn_lower)[0]

    error = (output - teacher.astype(F32)) * local_valid[:, None]
    squares = jnp.sum(error * error)
    count = jnp.sum(seq_lengths).astype(F32)

    far_task = None
    if wide:
        others = dp_size - 1
        sides = (me % 2) ^ jnp.arange(2, dtype=jnp.int32)
        in_order = (2 * jnp.arange(sp_size // 2, dtype=jnp.int32)[None, :] + sides[:, None]).reshape(-1)
        in_order = jnp.argmax((in_order[:, None] ^ me) == jnp.array(ORDER, jnp.int32)[None, :], axis=1)
        far_slots = slots_of(masks[:, 1:].transpose(1, 0, 2).reshape(others, total_rows))
        sp_slots = far_slots.reshape(others, sp_size, tok_rows)[:, in_order].reshape(others, total_rows)

        def pick_far(*rows_far):
            far_probs = [steer_rows(rows.reshape(-1, width))[0] for rows in rows_far]
            share = jnp.concatenate([jnp.sum(p * is_me[None, :], axis=1) for p in far_probs], 0)
            share = share.reshape(sp_size, others, tok_rows).transpose(1, 0, 2).reshape(others, 1, total_rows)
            share = jnp.where(sp_slots[:, None, :] == slot_range[None, :, None], share, 0.0)
            share = jnp.sum(share, axis=2, keepdims=True)
            return share, pick_rows(sp_slots, jnp.ones_like(share), *rows_far).reshape(-1, width)

        far_task = (pick_far, *two_far)

    error_low = error.astype(BF)
    fetched_error = fetch_groups(error_low) if wide else []
    *error_halves, far_work = gather_rows(error_low, far_task)
    grad_shared = [(s[1] * rows.astype(F32)).astype(BF) for s, rows in zip(steered, error_halves)]
    joined = lambda sides: jnp.concatenate(sides, 0)
    down_term = dot(joined(acted_s), joined(grad_shared), ((0,), (0,)), BF)
    grad_made = pick_rows(slots, share_rows[None], *(rows.reshape(blocks) for rows in error_halves))[0]
    (grad_made,), (down_term, *fetched_error) = after((grad_made,), (down_term, *fetched_error))
    down_shared = sum_groups(down_term, 1)
    if wide:
        far_own = jnp.stack(fetched_error, 0)
        far_half = tok_rows // 2
        far_x, far_y = swap(far_own, 2), swap(far_own, 4)
    grad_gate_e, grad_up_e, back_e, gain_rows = expert_back(
        grad_made, gate_e, up_e, acted_e, gateup_w, down_w
    )

    if wide:
        (back_e,), (far_x, far_y) = after((back_e,), (far_x, far_y))
        far_diag = jnp.concatenate([swap(far_y[:, :far_half], 2), swap(far_x[:, far_half:], 4)], 1)
    grad_act_s = [dot(g, shared_down, ((1,), (1,))) for g in grad_shared]
    switch_part = jnp.concatenate(
        [jnp.sum(a.astype(F32) * g, axis=1) for a, g in zip(acted_s, grad_act_s)], 0
    )
    grad_gate_s = [(g * u * silu_slope(v)).astype(BF) for g, u, v in zip(grad_act_s, up_s, gate_s)]
    grad_up_s = [(g * jax.nn.silu(v)).astype(BF) for g, v in zip(grad_act_s, gate_s)]

    def back_part(side):
        return (
            dot(grad_gate_s[side], gate_sw, ((1,), (1,)))
            + dot(grad_up_s[side], up_sw, ((1,), (1,)))
            + dot(pick[:, halves[side]], back_e, ((0,), (0,)))
        ).astype(BF)

    back_upper = back_part(1)
    back_lower = back_part(0)
    gain_tokens = jnp.sum(pick.astype(F32) * gain_rows, axis=0)
    scalars = jnp.concatenate(
        [gain_tokens[None, :] * is_me[:, None], switch_part[None, :], jnp.zeros((7, total_rows), F32)], axis=0
    )
    scalars, _ = sum_small(scalars.reshape(16, sp_size, tok_rows).transpose(1, 0, 2), jnp.zeros((1, 16, tok_rows), F32))
    gains, switch_sum = scalars[:experts].T, scalars[experts]
    my_probs, my_switch = probs[:tok_rows], switch[:tok_rows, 0]
    grad_switch = switch_sum * (1.0 - my_switch)
    grad_logits = gains - my_probs * jnp.sum(gains, axis=1, keepdims=True)
    steer = jnp.concatenate([grad_logits, grad_switch[:, None]], axis=1)
    if wide:
        (back_lower,), (far_diag,) = after((back_lower,), (far_diag,))
        error_far = jnp.stack([far_own, far_x, far_y, far_diag], 0)
        error_far = (error_far, swap(error_far, 1))
    summed, (gate_term, up_term) = sum_rows(
        back_upper,
        back_lower,
        (
            lambda rows, *grads: [dot(rows, g, ((0,), (0,)), BF) for g in grads],
            joined(two_halves),
            joined(grad_gate_s),
            joined(grad_up_s),
        ),
    )
    gate_shared, up_shared = sum_groups(gate_term, 0), sum_groups(up_term, 0)
    grad_normed = summed + jnp.einsum(
        "te,de->td", steer, heads_in.astype(F32), precision=HIGH
    )
    steer_term = jnp.einsum("te,td->ed", steer, normed_two.astype(F32), precision=HIGH)
    grad_middle_n, ffnnorm_term = norm_back(middle, inverse_two, gain_two, grad_normed)
    grad_middle = error + grad_middle_n

    far_task = None
    if wide:
        far_share, far_in = far_work
        far_task = (lambda *rows: (pick_rows(far_slots, far_share, *rows).reshape(-1, width),), *error_far)
    *attn_halves, far_work = gather_rows(grad_middle.astype(BF), far_task)
    grad_mixed = joined([dot(rows, out_proj, ((1,), (1,)), BF) for rows in attn_halves])
    grad_q, grad_k, grad_v = attend_back(
        queries, key_rows, values, allowed, totals, grad_mixed
    )
    grad_proj = (
        rotate_back(grad_q.astype(F32), cosine, sine_table).astype(BF),
        rotate_back(grad_k.astype(F32), cosine, sine_table).astype(BF),
        grad_v,
    )

    def input_part(rows):
        return sum(dot(grad_proj[j][rows], qkv_proj[j], ((1,), (1,))) for j in range(3)).astype(BF)

    input_upper = input_part(halves[1])
    input_lower = input_part(halves[0])
    normed_all = joined(normed_halves)
    outproj_term = dot(mixed, joined(attn_halves), ((0,), (0,)), BF)
    qkv_terms = jnp.stack([dot(normed_all, g, ((0,), (0,)), BF) for g in grad_proj], 0)
    bias_term = jnp.stack([jnp.sum(g.astype(F32), axis=0) for g in grad_proj], 0)
    if wide:
        (far_made,) = far_work
        grad_normed_one, far_work = sum_rows(
            input_upper,
            input_lower,
            (lambda made, *terms: (*terms, made, *expert_far(far_in, made, gateup_w, down_w)), far_made, outproj_term, qkv_terms),
        )
        outproj_term, qkv_terms, far_made, far_act, far_gate, far_up = far_work
        gateup_expert, down_expert = expert_grads_of(
            (rows_in, grad_made, acted_e, grad_gate_e, grad_up_e),
            (far_in, far_made, far_act, far_gate, far_up),
        )
    else:
        grad_normed_one, _ = sum_rows(input_upper, input_lower)
        gateup_expert = jnp.stack(
            [
                sum_groups(dot(rows_in, grad_gate_e, ((0,), (0,)), BF), 0),
                sum_groups(dot(rows_in, grad_up_e, ((0,), (0,)), BF), 0),
            ],
            axis=1,
        )
        down_expert = sum_groups(dot(acted_e, grad_made, ((0,), (0,)), BF), 1)
    grad_input_n, attnnorm_term = norm_back(inputs, inverse_one, gain_one, grad_normed_one)
    hidden_grad = grad_middle + grad_input_n
    outproj_grad = sum_groups(outproj_term, 1)
    qkvproj_grad = sum_groups(qkv_terms, 1)

    small = jnp.concatenate([attnnorm_term[None], ffnnorm_term[None], steer_term], axis=0)
    kinds = small.shape[0]
    cell = width // (dp_size * sp_size)
    small = small.reshape(kinds, dp_size, sp_size, cell).transpose(2, 1, 0, 3)[owners]
    small = small.reshape(sp_size, dp_size, kinds * cell)
    small, squares = sum_small(small, jnp.full((1,) + small.shape[1:], squares, F32))
    pairs = bias_term.reshape(-1, HD)
    bias_cells = pairs.reshape(pairs.shape[0], dp_size, -1).transpose(1, 0, 2).reshape(dp_size, -1)
    small = jnp.concatenate([small, bias_cells], axis=1)
    small, squares = shift_groups(small, jnp.full(small.shape[1:], squares[0, 0], F32))
    loss_value = squares[0] / (2.0 * count * D)
    gains_out = small[: kinds * cell].reshape(kinds, cell)
    qkvbias_grad = small[kinds * cell :].reshape(3, -1, HD // dp_size)
    return (
        output,
        loss_value,
        hidden_grad,
        gains_out[0],
        qkvproj_grad,
        qkvbias_grad,
        outproj_grad,
        gains_out[1],
        gains_out[2 : 2 + experts].T,
        jnp.stack([gate_shared, up_shared], axis=1),
        down_shared,
        gains_out[2 + experts],
        gateup_expert[None],
        down_expert[None],
    )


def solution(mesh):
    in_specs = (
        P(("dp", "sp"), None),
        P(("dp", "sp"), None),
        P(),
        P(("dp", "sp"), None),
        P(),
        P(None, None, "sp"),
        P(None, "sp", None),
        P("sp", None),
        P(),
        P(),
        P(None, None, "sp"),
        P("sp", None),
        P(),
        P("sp", None, None, None),
        P("sp", None, None),
    )
    out_specs = (
        P(("dp", "sp"), None),
        P(),
        P(("dp", "sp"), None),
        P(("dp", "sp")),
        P(None, "dp", "sp"),
        P(None, "sp", "dp"),
        P("sp", "dp"),
        P(("dp", "sp")),
        P(("dp", "sp"), None),
        P("dp", None, "sp"),
        P("sp", "dp"),
        P(("dp", "sp")),
        P("sp", "dp", None, None),
        P("sp", None, "dp"),
    )
    return jax.shard_map(
        on_device, mesh=mesh, in_specs=in_specs, out_specs=out_specs, check_vma=False
    )
```

```python
import jax
import jax.numpy as jnp
from jax import lax
from jax.experimental import pallas as pl
from jax.experimental.pallas import tpu as pltpu
from jax.sharding import PartitionSpec as P

D = 2048
HD = 128
BLK = 128
MAXSEQ = 8

EPS = 1e-06
THETA = 1000000.0
FLOOR = -1e30
HIGH = lax.Precision.HIGHEST
BF = jnp.bfloat16
F32 = jnp.float32

ORDER = (0, 2, 4, 6, 1, 3, 5, 7)


def after(values, work):
    values, work = tuple(values), tuple(work)
    if not work or not values:
        return values, work
    tied = lax.optimization_barrier((*values, *work))
    return tied[: len(values)], tied[len(values) :]


def between(first, last, task):
    if task is None:
        return tuple(last), ()
    function, *inputs = task
    inputs, _ = after(inputs, first)
    return after(last, function(*inputs))


def dot(left, right, dims, dtype=F32):
    return lax.dot_general(left, right, (dims, ((), ())), preferred_element_type=F32).astype(dtype)


def swap(values, distance):
    return lax.ppermute(values, "sp", [(i, i ^ distance) for i in range(8)])


def gather_rows(own, task=None, first=()):
    half = own.shape[0] // 2
    over_x, over_y = swap(own, 2), swap(own, 4)
    (over_x, over_y), work = between((own,), (over_x, over_y), task)
    (over_x, over_y), first = after((over_x, over_y), first)
    far_top, far_bottom = swap(over_y[:half], 2), swap(over_x[half:], 4)
    lower = jnp.concatenate([own, over_x, over_y, far_top, far_bottom], 0)
    return lower, swap(lower, 1), work, first


def gather_side(own):
    return lax.all_gather(own, "sp", axis_index_groups=[[0, 2, 4, 6], [1, 3, 5, 7]])


def gather_small(own):
    held = own[None]
    for distance in (2, 4, 1):
        held = jnp.concatenate([held, swap(held, distance)], 0)
    return held


def sum_small(parts, total):
    for distance in (1, 4, 2):
        keep = parts.shape[0] // 2
        got = swap(jnp.concatenate([parts[keep:], total], 0), distance)
        parts, total = parts[:keep] + got[:keep], total + got[keep:]
    return parts[0], total[0]


def sum_rows(upper, lower, task=None):
    rows = lower.shape[0] // 4
    half = rows // 2
    got = swap(upper, 1)
    chip = lower.astype(F32) + got.astype(F32)
    low = chip.astype(BF)
    own, over_x, over_y, far = (slice(k * rows, (k + 1) * rows) for k in range(4))
    low_x, low_y, low_far = low[over_x], low[over_y], low[far]
    from_x = swap(jnp.concatenate([low_far[:half], low_x[:half]], 0), 2)
    from_y = swap(jnp.concatenate([low_far[half:], low_y[half:]], 0), 4)
    (from_x, from_y), work = between((low,), (from_x, from_y), task)
    pass_y = (chip[over_y][:half] + from_x[:half].astype(F32)).astype(BF)
    pass_x = (chip[over_x][half:] + from_y[:half].astype(F32)).astype(BF)
    last_y, last_x = swap(pass_y, 4), swap(pass_x, 2)
    mine = chip[own]
    top = mine[:half] + from_x[half:].astype(F32) + last_y.astype(F32)
    bottom = mine[half:] + from_y[half:].astype(F32) + last_x.astype(F32)
    return jnp.concatenate([top, bottom], 0), work


def sum_groups(grads, dim):
    return lax.psum_scatter(grads, "dp", scatter_dimension=dim, tiled=True).astype(F32)


def shift_groups(blocks, total):
    size = lax.axis_size("dp")
    me = lax.axis_index("dp")
    pick = lambda k: lax.dynamic_index_in_dim(blocks, (me + k) % size, 0, keepdims=False)
    mine = jnp.stack([pick(0), total])
    summed = mine[0]
    totals = jnp.zeros((size,) + total.shape, total.dtype).at[me].set(total)
    for k in range(1, size):
        got = lax.ppermute(jnp.stack([pick(k), total]), "dp", [(i, (i + k) % size) for i in range(size)])
        summed = summed + got[0]
        totals = totals.at[(me - k) % size].set(got[1])
    return summed, jnp.sum(totals, axis=0)


def fetch_groups(own, chained=True):
    size = lax.axis_size("dp")
    got = []
    for k in range(1, size):
        moved, _ = after((own,), got[-1:] if chained else ())
        got.append(lax.ppermute(moved[0], "dp", [((i + k) % size, i) for i in range(size)]))
    return got


def own_columns(values, axis):
    share = values.shape[axis] // lax.axis_size("dp")
    return lax.dynamic_slice_in_dim(values, lax.axis_index("dp") * share, share, axis)


def slots_of(mask):
    return jnp.where(mask, jnp.cumsum(mask.astype(jnp.int32), axis=-1) - 1, -1)


def local_call(kernel, name, flops, **spec):
    return pl.pallas_call(
        kernel,
        name=name,
        cost_estimate=pl.CostEstimate(flops=flops, bytes_accessed=flops // 300, transcendentals=0),
        compiler_params=pltpu.CompilerParams(vmem_limit_bytes=56 * 2**20),
        **spec,
    )


def pick_kernel(slot_ref, scale_ref, lower_ref, upper_ref, out_ref):
    capacity, columns = out_ref.shape
    total = slot_ref.shape[-1]
    chosen = (slot_ref[...] == lax.broadcasted_iota(jnp.int32, (capacity, total), 0)).astype(F32).astype(BF)
    half = total // 2
    rows = jnp.dot(chosen[:, :half], lower_ref[...].reshape(half, columns), preferred_element_type=F32)
    rows += jnp.dot(chosen[:, half:], upper_ref[...].reshape(half, columns), preferred_element_type=F32)
    out_ref[...] = (rows * scale_ref[...]).astype(BF)


def pick_rows(slots, scale, lower, upper):
    blocks, groups, count, width = lower.shape
    total = 2 * blocks * count
    capacity = scale.shape[1]
    tile = 1024
    rows = pl.BlockSpec((blocks, None, count, tile), lambda g, j: (0, g, 0, j))
    return local_call(
        pick_kernel,
        "pick_rows",
        2 * groups * capacity * total * width,
        grid=(groups, width // tile),
        in_specs=[
            pl.BlockSpec((None, 1, total), lambda g, j: (g, 0, 0)),
            pl.BlockSpec((None, capacity, 1), lambda g, j: (g, 0, 0)),
            rows,
            rows,
        ],
        out_specs=pl.BlockSpec((None, capacity, tile), lambda g, j: (g, 0, j)),
        out_shape=jax.ShapeDtypeStruct((groups, capacity, width), BF),
    )(slots[:, None, :], scale, lower, upper)


def dot_nn(left, right):
    return lax.dot_general(left, right, (((1,), (0,)), ((), ())), preferred_element_type=F32)


def dot_nt(left, right):
    return lax.dot_general(left, right, (((1,), (1,)), ((), ())), preferred_element_type=F32)


def dot_tn(left, right):
    return lax.dot_general(left, right, (((0,), (0,)), ((), ())), preferred_element_type=F32)


def expert_kernel(x_ref, gateup_w, down_w, gate_ref, up_ref, act_ref, made_ref):
    x = x_ref[...]
    gate, up = dot_nn(x, gateup_w[0]), dot_nn(x, gateup_w[1])
    gate_ref[...], up_ref[...] = gate, up
    act = (gate * jax.nn.sigmoid(gate) * up).astype(BF)
    act_ref[...] = act
    made_ref[...] = dot_nn(act, down_w[...]).astype(BF)


def row_spec(block, columns):
    return pl.BlockSpec((block, columns), lambda i: (i, 0))


def held_spec(array):
    return pl.BlockSpec(array.shape, lambda i: (0,) * array.ndim, pipeline_mode=pl.Buffered(1))


def row_block(count):
    return max(b for b in range(16, min(count, 288) + 1, 16) if count % b == 0)


def expert_forward(x, gateup_w, down_w):
    count, width = x.shape
    hidden = gateup_w.shape[2]
    block = row_block(count)
    wide_shape = lambda dtype: jax.ShapeDtypeStruct((count, hidden), dtype)
    return local_call(
        expert_kernel,
        "expert_forward",
        6 * count * width * hidden,
        grid=(count // block,),
        in_specs=[row_spec(block, width), held_spec(gateup_w), held_spec(down_w)],
        out_specs=[row_spec(block, hidden)] * 3 + [row_spec(block, width)],
        out_shape=[wide_shape(F32), wide_shape(F32), wide_shape(BF), jax.ShapeDtypeStruct((count, width), BF)],
    )(x, gateup_w, down_w)


def middle_grads(gate, up, grad):
    sig = jax.nn.sigmoid(gate)
    slope = sig * (1.0 + gate * (1.0 - sig))
    return (grad * up * slope).astype(BF), (grad * (gate * sig)).astype(BF)


def expert_back_kernel(g_ref, gate_ref, up_ref, act_ref, gateup_w, down_w, gg_ref, gu_ref, back_ref, gain_ref):
    grad = dot_nt(g_ref[...], down_w[...])
    gain_ref[...] = jnp.sum(act_ref[...].astype(F32) * grad, axis=1, keepdims=True)
    grad_gate, grad_up = middle_grads(gate_ref[...], up_ref[...], grad)
    gg_ref[...], gu_ref[...] = grad_gate, grad_up
    back_ref[...] = (dot_nt(grad_gate, gateup_w[0]) + dot_nt(grad_up, gateup_w[1])).astype(BF)


def expert_back(g, gate, up, act, gateup_w, down_w):
    count, width = g.shape
    hidden = gateup_w.shape[2]
    block = row_block(count)
    rows, mids = row_spec(block, width), row_spec(block, hidden)
    return local_call(
        expert_back_kernel,
        "expert_back",
        6 * count * width * hidden,
        grid=(count // block,),
        in_specs=[rows, mids, mids, mids, held_spec(gateup_w), held_spec(down_w)],
        out_specs=[mids, mids, rows, row_spec(block, 1)],
        out_shape=[jax.ShapeDtypeStruct((count, hidden), BF)] * 2
        + [jax.ShapeDtypeStruct((count, width), BF), jax.ShapeDtypeStruct((count, 1), F32)],
    )(g, gate, up, act, gateup_w, down_w)


def expert_far_kernel(x_ref, g_ref, gateup_w, down_w, act_ref, gg_ref, gu_ref):
    x = x_ref[...]
    gate, up = dot_nn(x, gateup_w[0]), dot_nn(x, gateup_w[1])
    act_ref[...] = (gate * jax.nn.sigmoid(gate) * up).astype(BF)
    gg_ref[...], gu_ref[...] = middle_grads(gate, up, dot_nt(g_ref[...], down_w[...]))


def expert_far(x, g, gateup_w, down_w):
    count, width = x.shape
    hidden = gateup_w.shape[2]
    block = row_block(count)
    rows, mids = row_spec(block, width), row_spec(block, hidden)
    return local_call(
        expert_far_kernel,
        "expert_far",
        6 * count * width * hidden,
        grid=(count // block,),
        in_specs=[rows, rows, held_spec(gateup_w), held_spec(down_w)],
        out_specs=[mids] * 3,
        out_shape=[jax.ShapeDtypeStruct((count, hidden), BF)] * 3,
    )(x, g, gateup_w, down_w)


def expert_grad_kernel(_, x, g, act, gg, gu, far_x, far_g, far_act, far_gg, far_gu, gateup_ref, down_ref, acc_g, acc_u):
    step = pl.program_id(0)

    @pl.when(step == 0)
    def _():
        rows = x[...]
        acc_g[...] = dot_tn(rows, gg[...])
        acc_u[...] = dot_tn(rows, gu[...])
        down_ref[...] = dot_tn(act[...], g[...])

    @pl.when(step > 0)
    def _():
        rows = far_x[...]
        acc_g[...] += dot_tn(rows, far_gg[...])
        acc_u[...] += dot_tn(rows, far_gu[...])
        down_ref[...] += dot_tn(far_act[...], far_g[...])

    @pl.when(step == pl.num_programs(0) - 1)
    def _():
        gateup_ref[:, 0, :] = acc_g[...]
        gateup_ref[:, 1, :] = acc_u[...]


def expert_grads_of(own, far):
    count, width = own[0].shape
    hidden = own[2].shape[1]
    share = width // lax.axis_size("dp")
    steps = 1 + far[0].shape[0] // count
    held = lambda i, d: (0, 0)
    near_rows = pl.BlockSpec((count, share), lambda i, d: (0, d[0]))
    near_mid = pl.BlockSpec((count, hidden), held)
    far_rows = pl.BlockSpec((count, share), lambda i, d: (jnp.maximum(i - 1, 0), d[0]))
    far_mid = pl.BlockSpec((count, hidden), lambda i, d: (jnp.maximum(i - 1, 0), 0))
    return local_call(
        expert_grad_kernel,
        "expert_grads",
        6 * count * steps * share * hidden,
        grid_spec=pltpu.PrefetchScalarGridSpec(
            num_scalar_prefetch=1,
            grid=(steps,),
            in_specs=[near_rows, near_rows] + [near_mid] * 3 + [far_rows, far_rows] + [far_mid] * 3,
            out_specs=[
                pl.BlockSpec((share, 2, hidden), lambda i, d: (0, 0, 0)),
                pl.BlockSpec((hidden, share), held),
            ],
            scratch_shapes=[pltpu.VMEM((share, hidden), F32)] * 2,
        ),
        out_shape=[
            jax.ShapeDtypeStruct((share, 2, hidden), F32),
            jax.ShapeDtypeStruct((hidden, share), F32),
        ],
    )(lax.axis_index("dp").reshape(1), *own, *far)


def layout(length_row, place):
    blocks = (length_row + BLK - 1) // BLK
    ends = jnp.cumsum(blocks)
    starts = ends - blocks
    which = jnp.sum((place[:, None] // BLK >= ends[None, :]).astype(jnp.int32), axis=1)
    member = which[:, None] == jnp.arange(length_row.shape[0], dtype=jnp.int32)[None, :]
    opening = jnp.sum(jnp.where(member, starts[None, :], 0), axis=1)
    seq_len = jnp.sum(jnp.where(member, length_row[None, :], 0), axis=1)
    position = place - opening * BLK
    return (which, position, position < seq_len)


def rope_tables(position):
    half_dim = HD // 2
    freq = THETA ** (-2.0 * jnp.arange(half_dim, dtype=F32) / HD)
    angle = position.astype(F32)[:, None] * freq[None, :]
    return (
        jnp.concatenate([jnp.cos(angle), jnp.cos(angle)], -1),
        jnp.concatenate([jnp.sin(angle), jnp.sin(angle)], -1),
    )


def rotate(flat_rows, cosine, sine_table):
    count = flat_rows.shape[0]
    shaped = flat_rows.reshape(count, -1, HD)
    half_dim = HD // 2
    turned = jnp.concatenate([-shaped[..., half_dim:], shaped[..., :half_dim]], -1)
    return (shaped * cosine[:, None, :] + turned * sine_table[:, None, :]).reshape(count, -1)


def rotate_back(flat_rows, cosine, sine_table):
    count = flat_rows.shape[0]
    shaped = flat_rows.reshape(count, -1, HD)
    half_dim = HD // 2
    sined = shaped * sine_table[:, None, :]
    turned = jnp.concatenate([sined[..., half_dim:], -sined[..., :half_dim]], -1)
    return (shaped * cosine[:, None, :] + turned).reshape(count, -1)


def normalize(values, gain_vec):
    inverse = lax.rsqrt(jnp.mean(values * values, axis=-1, keepdims=True) + EPS)
    return (values * inverse * gain_vec, inverse)


def norm_back(values, inverse, gain_vec, gradient):
    scaled = values * inverse
    gain_term = jnp.sum(gradient * scaled, axis=0)
    grad_scaled = gradient * gain_vec
    back = inverse * (grad_scaled - scaled * jnp.mean(grad_scaled * scaled, axis=-1, keepdims=True))
    return (back, gain_term)


def silu_slope(values):
    sig = jax.nn.sigmoid(values)
    return sig * (1.0 + values * (1.0 - sig))


def scores_of(queries, key_rows, allowed):
    scores = dot(queries, key_rows, ((1,), (1,))) * HD ** (-0.5)
    return jnp.where(allowed, scores, FLOOR)


def attend_forward(queries, key_rows, values, allowed):
    pieces, totals = [], []
    for start in range(0, queries.shape[1], HD):
        head = slice(start, start + HD)
        scores = scores_of(queries[:, head], key_rows[:, head], allowed)
        peak = jnp.max(scores, axis=-1, keepdims=True)
        expon = jnp.exp(scores - peak)
        summed = jnp.sum(expon, axis=-1, keepdims=True)
        weights = (expon / summed).astype(BF)
        pieces.append(dot(weights, values[:, head], ((1,), (0,)), BF))
        totals.append(peak + jnp.log(summed))
    return (jnp.concatenate(pieces, 1), totals)


def attend_back(queries, key_rows, values, allowed, totals, grad_mixed):
    scale = HD ** (-0.5)
    grads = ([], [], [])
    for start, total in zip(range(0, queries.shape[1], HD), totals):
        head = slice(start, start + HD)
        block_q, block_k, block_g = queries[:, head], key_rows[:, head], grad_mixed[:, head]
        probs = jnp.exp(scores_of(block_q, block_k, allowed) - total)
        grad_p = dot(block_g, values[:, head], ((1,), (1,)))
        grad_s = (probs * (grad_p - jnp.sum(probs * grad_p, axis=-1, keepdims=True))).astype(BF)
        grads[0].append((dot(grad_s, block_k, ((1,), (0,))) * scale).astype(BF))
        grads[1].append((dot(grad_s, block_q, ((0,), (0,))) * scale).astype(BF))
        grads[2].append(dot(probs.astype(BF), block_g, ((0,), (0,)), BF))
    return tuple(jnp.concatenate(g, 1) for g in grads)


def on_device(
    hidden_in,
    teacher,
    seq_lengths,
    routes,
    attn_norm,
    qkv_proj,
    qkv_bias,
    out_proj,
    ffn_norm,
    router,
    shared_gateup,
    shared_down,
    shared_switch,
    expert_gateup,
    expert_down,
):
    tok_rows, width = hidden_in.shape
    sp_size = lax.axis_size("sp")
    dp_size = lax.axis_size("dp")
    me = lax.axis_index("sp")
    total_rows = tok_rows * sp_size
    lower_rows = total_rows // 2
    experts = router.shape[1]
    top_k = routes.shape[1]
    capacity = sp_size * min(tok_rows, 9 * tok_rows * top_k // (8 * experts))

    inputs = hidden_in.astype(F32)
    gain_one = attn_norm.astype(F32)
    normed_f, inverse_one = normalize(inputs, gain_one)
    *normed_halves, (gateup_w,), _ = gather_rows(
        normed_f.astype(BF), (lambda w: (w.transpose(1, 0, 2),), expert_gateup[0])
    )
    wide = dp_size <= 4

    owners = me ^ jnp.array(ORDER, jnp.int32)
    place = (owners[:, None] * tok_rows + jnp.arange(tok_rows, dtype=jnp.int32)[None, :]).reshape(-1)
    length_row = lax.dynamic_index_in_dim(seq_lengths, lax.axis_index("dp"), 0, keepdims=False)
    segment, position, is_valid = layout(length_row, place)
    cosine, sine_table = rope_tables(position)
    local_valid = is_valid[:tok_rows].astype(F32)
    allowed = (
        (segment[:, None] == segment[None, :])
        & (position[None, :] <= position[:, None])
        & is_valid[None, :]
    )

    bias = qkv_bias.reshape(3, 1, -1).astype(F32)
    normed_all = jnp.concatenate(normed_halves, 0)
    projected = [dot(normed_all, qkv_proj[j], ((1,), (0,))) + bias[j] for j in range(3)]
    queries = rotate(projected[0], cosine, sine_table).astype(BF)
    key_rows = rotate(projected[1], cosine, sine_table).astype(BF)
    values = projected[2].astype(BF)
    mixed, totals = attend_forward(queries, key_rows, values, allowed)
    upper = dot(mixed[lower_rows:], out_proj, ((1,), (0,)), BF)
    lower = dot(mixed[:lower_rows], out_proj, ((1,), (0,)), BF)

    (route_own,), _ = after((routes.T[None],), (mixed,))
    if wide:
        route_own = jnp.concatenate([route_own] + fetch_groups(route_own, False), 0)
    route_all = gather_small(route_own.reshape(-1, tok_rows))
    route_all = route_all.reshape(sp_size, -1, top_k, tok_rows)
    masks = jnp.any(route_all == me, axis=2)
    mask = masks[:, 0].reshape(total_rows)
    slots = slots_of(mask)[None]
    slot_range = jnp.arange(capacity, dtype=jnp.int32)
    pick = (slots[0][None, :] == slot_range[:, None]).astype(BF)

    middle = inputs + sum_rows(upper, lower)[0]

    gain_two = ffn_norm.astype(F32)
    normed_two_f, inverse_two = normalize(middle, gain_two)
    normed_two = normed_two_f.astype(BF)
    fetched_two = fetch_groups(normed_two, False) if wide else []
    *two_halves, _, (pick, slots) = gather_rows(normed_two, None, (pick, slots))

    heads_in = jnp.concatenate([router, shared_switch[:, None]], axis=1)
    is_me = (jnp.arange(experts) == me).astype(F32)

    def steer_rows(rows):
        logits = dot(rows, heads_in, ((1,), (0,)))
        return jax.nn.softmax(logits[:, :experts], axis=-1), jax.nn.sigmoid(logits[:, experts:])

    steered = [steer_rows(rows) for rows in two_halves]
    probs, switch = (jnp.concatenate(both, 0) for both in zip(*steered))
    share = jnp.sum(probs * is_me[None, :], axis=1) * mask.astype(F32)
    share_rows = jnp.sum(pick.astype(F32) * share[None, :], axis=1, keepdims=True)

    down_w = expert_down[0]
    blocks = (sp_size // 2, 1, tok_rows, width)
    ones = jnp.ones((1, capacity, 1), F32)
    rows_in = pick_rows(slots, ones, *(rows.reshape(blocks) for rows in two_halves))[0]
    gate_e, up_e, acted_e, made = expert_forward(rows_in, gateup_w, down_w)
    two_halves, (made, *fetched_two) = after(two_halves, (made, *fetched_two))

    gate_sw, up_sw = shared_gateup[:, 0, :], shared_gateup[:, 1, :]
    gate_s = [dot(rows, gate_sw, ((1,), (0,))) for rows in two_halves]
    up_s = [dot(rows, up_sw, ((1,), (0,))) for rows in two_halves]
    acted_s = [(jax.nn.silu(g) * u).astype(BF) for g, u in zip(gate_s, up_s)]
    halves = (slice(0, lower_rows), slice(lower_rows, None))

    def ffn_part(side):
        rows = halves[side]
        shared = dot(acted_s[side], shared_down, ((1,), (0,)))
        routed = dot(pick[:, rows], made, ((0,), (0,)))
        return (steered[side][1] * shared + share[rows, None] * routed).astype(BF)

    ffn_upper = ffn_part(1)
    ffn_lower = ffn_part(0)
    output = middle + sum_rows(ffn_upper, ffn_lower)[0]
    error = (output - teacher.astype(F32)) * local_valid[:, None]
    squares = jnp.sum(error * error)
    count = jnp.sum(seq_lengths).astype(F32)

    if wide:
        others = dp_size - 1
        sides = (me % 2) ^ jnp.arange(2, dtype=jnp.int32)
        in_order = (2 * jnp.arange(sp_size // 2, dtype=jnp.int32)[None, :] + sides[:, None]).reshape(-1)
        same_place = (in_order[:, None] ^ me) == jnp.array(ORDER, jnp.int32)[None, :]
        in_order = jnp.argmax(same_place, axis=1)
        far_slots = slots_of(masks[:, 1:].transpose(1, 0, 2).reshape(others, total_rows))
        sp_slots = far_slots.reshape(others, sp_size, tok_rows)[:, in_order].reshape(others, total_rows)

        def share_far(*rows_far):
            far_probs = [steer_rows(rows.reshape(-1, width))[0] for rows in rows_far]
            share = jnp.concatenate([jnp.sum(p * is_me[None, :], axis=1) for p in far_probs], 0)
            share = share.reshape(sp_size, others, tok_rows).transpose(1, 0, 2).reshape(others, 1, total_rows)
            share = jnp.where(sp_slots[:, None, :] == slot_range[None, :, None], share, 0.0)
            return jnp.sum(share, axis=2, keepdims=True)

    error_low = error.astype(BF)
    fetched_error = fetch_groups(error_low) if wide else []
    *error_halves, _, fetched_error[:1] = gather_rows(error_low, None, fetched_error[:1])
    if wide:
        fetched_two, _ = after(fetched_two, error_halves)
        two_side = gather_side(jnp.stack(fetched_two, 0))
    grad_shared = [(s[1] * rows.astype(F32)).astype(BF) for s, rows in zip(steered, error_halves)]
    joined = lambda sides: jnp.concatenate(sides, 0)
    grad_act_s = [dot(g, shared_down, ((1,), (1,))) for g in grad_shared]
    grad_gate_s = [(g * u * silu_slope(v)).astype(BF) for g, u, v in zip(grad_act_s, up_s, gate_s)]
    grad_up_s = [(g * jax.nn.silu(v)).astype(BF) for g, v in zip(grad_act_s, gate_s)]
    own_act, own_grad = joined(acted_s), joined(grad_shared)
    down_term = dot(own_act, own_grad, ((0,), (0,)), BF)
    grad_up_s, (down_term, *fetched_error[1:2]) = after(grad_up_s, (down_term, *fetched_error[1:2]))
    two_all = joined(two_halves)
    mid_term = dot(two_all, jnp.concatenate([joined(grad_gate_s), joined(grad_up_s)], 1), ((0,), (0,)), BF)
    grad_made = pick_rows(slots, share_rows[None], *(rows.reshape(blocks) for rows in error_halves))[0]
    (grad_made,), (mid_term, *fetched_error[2:]) = after((grad_made,), (mid_term, *fetched_error[2:]))
    down_shared = sum_groups(down_term, 1)
    mid_shared = sum_groups(mid_term, 0)
    if wide:
        far_own = jnp.stack(fetched_error, 0)
        far_half = tok_rows // 2
        far_x, far_y = swap(far_own, 2), swap(far_own, 4)
    grad_gate_e, grad_up_e, back_e, gain_rows = expert_back(
        grad_made, gate_e, up_e, acted_e, gateup_w, down_w
    )
    if wide:
        (back_e,), (far_x, far_y) = after((back_e,), (far_x, far_y))
        far_diag = jnp.concatenate([swap(far_y[:, :far_half], 2), swap(far_x[:, far_half:], 4)], 1)
    switch_part = jnp.concatenate(
        [jnp.sum(a.astype(F32) * g, axis=1) for a, g in zip(acted_s, grad_act_s)], 0
    )

    def back_part(side):
        return (
            dot(grad_gate_s[side], gate_sw, ((1,), (1,)))
            + dot(grad_up_s[side], up_sw, ((1,), (1,)))
            + dot(pick[:, halves[side]], back_e, ((0,), (0,)))
        ).astype(BF)

    back_upper = back_part(1)
    back_lower = back_part(0)
    gain_tokens = jnp.sum(pick.astype(F32) * gain_rows, axis=0)
    scalars = jnp.concatenate(
        [gain_tokens[None, :] * is_me[:, None], switch_part[None, :], jnp.zeros((7, total_rows), F32)], axis=0
    )
    scalars, _ = sum_small(scalars.reshape(16, sp_size, tok_rows).transpose(1, 0, 2), jnp.zeros((1, 16, tok_rows), F32))
    gains, switch_sum = scalars[:experts].T, scalars[experts]
    my_probs, my_switch = probs[:tok_rows], switch[:tok_rows, 0]
    grad_switch = switch_sum * (1.0 - my_switch)
    grad_logits = gains - my_probs * jnp.sum(gains, axis=1, keepdims=True)
    steer = jnp.concatenate([grad_logits, grad_switch[:, None]], axis=1)
    if wide:
        (back_lower,), (far_diag,) = after((back_lower,), (far_diag,))
        error_far = jnp.stack([far_own, far_x, far_y, far_diag], 0)
        error_far = (error_far, swap(error_far, 1))
        two_far = (two_side, swap(two_side, 1))
    far_task = None
    if wide:

        def make_far(lower, upper, *rows_far):
            share = share_far(*rows_far)
            return pick_rows(far_slots, share, lower, upper).reshape(-1, width), *rows_far

        far_task = (make_far, *error_far, *two_far)
    (back_lower,), (down_shared,) = after((back_lower,), (down_shared,))
    summed, far_work = sum_rows(back_upper, back_lower, far_task)
    grad_normed = summed + jnp.einsum(
        "te,de->td", steer, heads_in.astype(F32), precision=HIGH
    )
    steer_term = jnp.einsum("te,td->ed", steer, normed_two.astype(F32), precision=HIGH)
    grad_middle_n, ffnnorm_term = norm_back(middle, inverse_two, gain_two, grad_normed)
    grad_middle = error + grad_middle_n

    far_task = None
    if wide:
        far_made, *two_far = far_work
        ones_far = jnp.ones((others, capacity, 1), F32)
        far_task = (lambda *rows: (pick_rows(sp_slots, ones_far, *rows).reshape(-1, width),), *two_far)
    *attn_halves, far_work, _ = gather_rows(grad_middle.astype(BF), far_task)
    grad_mixed = joined([dot(rows, out_proj, ((1,), (1,)), BF) for rows in attn_halves])
    grad_q, grad_k, grad_v = attend_back(
        queries, key_rows, values, allowed, totals, grad_mixed
    )
    grad_proj = (
        rotate_back(grad_q.astype(F32), cosine, sine_table).astype(BF),
        rotate_back(grad_k.astype(F32), cosine, sine_table).astype(BF),
        grad_v,
    )

    def input_part(rows):
        return sum(dot(grad_proj[j][rows], qkv_proj[j], ((1,), (1,))) for j in range(3)).astype(BF)

    input_upper = input_part(halves[1])
    input_lower = input_part(halves[0])
    outproj_term = dot(mixed, joined(attn_halves), ((0,), (0,)), BF)
    qkv_terms = jnp.stack([dot(normed_all, g, ((0,), (0,)), BF) for g in grad_proj], 0)
    bias_term = jnp.stack([jnp.sum(g.astype(F32), axis=0) for g in grad_proj], 0)
    if wide:
        (far_in,) = far_work
        grad_normed_one, far_work = sum_rows(
            input_upper,
            input_lower,
            (lambda made, *_: (made, *expert_far(far_in, made, gateup_w, down_w)), far_made, outproj_term, qkv_terms, mid_shared),
        )
        far_made, far_act, far_gate, far_up = far_work
        gateup_expert, down_expert = expert_grads_of(
            (rows_in, grad_made, acted_e, grad_gate_e, grad_up_e),
            (far_in, far_made, far_act, far_gate, far_up),
        )
    else:
        grad_normed_one, _ = sum_rows(input_upper, input_lower)
        gateup_expert = jnp.stack(
            [
                sum_groups(dot(rows_in, grad_gate_e, ((0,), (0,)), BF), 0),
                sum_groups(dot(rows_in, grad_up_e, ((0,), (0,)), BF), 0),
            ],
            axis=1,
        )
        down_expert = sum_groups(dot(acted_e, grad_made, ((0,), (0,)), BF), 1)
    grad_input_n, attnnorm_term = norm_back(inputs, inverse_one, gain_one, grad_normed_one)
    hidden_grad = grad_middle + grad_input_n
    outproj_grad = sum_groups(outproj_term, 1)
    qkvproj_grad = sum_groups(qkv_terms, 1)

    small = jnp.concatenate([attnnorm_term[None], ffnnorm_term[None], steer_term], axis=0)
    kinds = small.shape[0]
    cell = width // (dp_size * sp_size)
    small = small.reshape(kinds, dp_size, sp_size, cell).transpose(2, 1, 0, 3)[owners]
    small = small.reshape(sp_size, dp_size, kinds * cell)
    small, squares = sum_small(small, jnp.full((1,) + small.shape[1:], squares, F32))
    pairs = bias_term.reshape(-1, HD)
    bias_cells = pairs.reshape(pairs.shape[0], dp_size, -1).transpose(1, 0, 2).reshape(dp_size, -1)
    small = jnp.concatenate([small, bias_cells], axis=1)
    small, squares = shift_groups(small, jnp.full(small.shape[1:], squares[0, 0], F32))
    loss_value = squares[0] / (2.0 * count * D)
    gains_out = small[: kinds * cell].reshape(kinds, cell)
    qkvbias_grad = small[kinds * cell :].reshape(3, -1, HD // dp_size)
    return (
        output,
        loss_value,
        hidden_grad,
        gains_out[0],
        qkvproj_grad,
        qkvbias_grad,
        outproj_grad,
        gains_out[1],
        gains_out[2 : 2 + experts].T,
        mid_shared.reshape(-1, 2, gate_sw.shape[1]),
        down_shared,
        gains_out[2 + experts],
        gateup_expert[None],
        down_expert[None],
    )


def solution(mesh):
    in_specs = (
        P(("dp", "sp"), None),
        P(("dp", "sp"), None),
        P(),
        P(("dp", "sp"), None),
        P(),
        P(None, None, "sp"),
        P(None, "sp", None),
        P("sp", None),
        P(),
        P(),
        P(None, None, "sp"),
        P("sp", None),
        P(),
        P("sp", None, None, None),
        P("sp", None, None),
    )
    out_specs = (
        P(("dp", "sp"), None),
        P(),
        P(("dp", "sp"), None),
        P(("dp", "sp")),
        P(None, "dp", "sp"),
        P(None, "sp", "dp"),
        P("sp", "dp"),
        P(("dp", "sp")),
        P(("dp", "sp"), None),
        P("dp", None, "sp"),
        P("sp", "dp"),
        P(("dp", "sp")),
        P("sp", "dp", None, None),
        P("sp", None, "dp"),
    )
    return jax.shard_map(
        on_device, mesh=mesh, in_specs=in_specs, out_specs=out_specs, check_vma=False
    )
```

```python
import jax
import jax.numpy as jnp
from jax import lax
from jax.experimental import pallas as pl
from jax.experimental.pallas import tpu as pltpu
from jax.sharding import PartitionSpec as P

D = 2048
HD = 128
BLK = 128
MAXSEQ = 8

EPS = 1e-06
THETA = 1000000.0
FLOOR = -1e30
HIGH = lax.Precision.HIGHEST
BF = jnp.bfloat16
F32 = jnp.float32

ORDER = (0, 2, 4, 6, 1, 3, 5, 7)


def after(values, work):
    values, work = tuple(values), tuple(work)
    if not work or not values:
        return values, work
    tied = lax.optimization_barrier((*values, *work))
    return tied[: len(values)], tied[len(values) :]


def between(first, last, task):
    if task is None:
        return tuple(last), ()
    function, *inputs = task
    inputs, _ = after(inputs, first)
    return after(last, function(*inputs))


def dot(left, right, dims, dtype=F32):
    return lax.dot_general(left, right, (dims, ((), ())), preferred_element_type=F32).astype(dtype)


def swap(values, distance):
    return lax.ppermute(values, "sp", [(i, i ^ distance) for i in range(8)])


def gather_rows(own, task=None, first=()):
    half = own.shape[0] // 2
    over_x, over_y = swap(own, 2), swap(own, 4)
    (over_x, over_y), work = between((own,), (over_x, over_y), task)
    (over_x, over_y), first = after((over_x, over_y), first)
    far_top, far_bottom = swap(over_y[:half], 2), swap(over_x[half:], 4)
    lower = jnp.concatenate([own, over_x, over_y, far_top, far_bottom], 0)
    return lower, swap(lower, 1), work, first


def gather_side(own):
    return lax.all_gather(own, "sp", axis_index_groups=[[0, 2, 4, 6], [1, 3, 5, 7]])


def gather_small(own):
    held = own[None]
    for distance in (2, 4, 1):
        held = jnp.concatenate([held, swap(held, distance)], 0)
    return held


def sum_small(parts, total):
    for distance in (1, 4, 2):
        keep = parts.shape[0] // 2
        got = swap(jnp.concatenate([parts[keep:], total], 0), distance)
        parts, total = parts[:keep] + got[:keep], total + got[keep:]
    return parts[0], total[0]


def sum_rows(upper, lower, task=None):
    rows = lower.shape[0] // 4
    half = rows // 2
    got = swap(upper, 1)
    chip = lower.astype(F32) + got.astype(F32)
    low = chip.astype(BF)
    own, over_x, over_y, far = (slice(k * rows, (k + 1) * rows) for k in range(4))
    low_x, low_y, low_far = low[over_x], low[over_y], low[far]
    from_x = swap(jnp.concatenate([low_far[:half], low_x[:half]], 0), 2)
    from_y = swap(jnp.concatenate([low_far[half:], low_y[half:]], 0), 4)
    (from_x, from_y), work = between((low,), (from_x, from_y), task)
    pass_y = (chip[over_y][:half] + from_x[:half].astype(F32)).astype(BF)
    pass_x = (chip[over_x][half:] + from_y[:half].astype(F32)).astype(BF)
    last_y, last_x = swap(pass_y, 4), swap(pass_x, 2)
    mine = chip[own]
    top = mine[:half] + from_x[half:].astype(F32) + last_y.astype(F32)
    bottom = mine[half:] + from_y[half:].astype(F32) + last_x.astype(F32)
    return jnp.concatenate([top, bottom], 0), work


def sum_groups(grads, dim):
    return lax.psum_scatter(grads, "dp", scatter_dimension=dim, tiled=True).astype(F32)


def shift_groups(blocks, total):
    size = lax.axis_size("dp")
    me = lax.axis_index("dp")
    pick = lambda k: lax.dynamic_index_in_dim(blocks, (me + k) % size, 0, keepdims=False)
    mine = jnp.stack([pick(0), total])
    summed = mine[0]
    totals = jnp.zeros((size,) + total.shape, total.dtype).at[me].set(total)
    for k in range(1, size):
        got = lax.ppermute(jnp.stack([pick(k), total]), "dp", [(i, (i + k) % size) for i in range(size)])
        summed = summed + got[0]
        totals = totals.at[(me - k) % size].set(got[1])
    return summed, jnp.sum(totals, axis=0)


def fetch_groups(own, chained=True):
    size = lax.axis_size("dp")
    got = []
    for k in range(1, size):
        moved, _ = after((own,), got[-1:] if chained else ())
        got.append(lax.ppermute(moved[0], "dp", [((i + k) % size, i) for i in range(size)]))
    return got


def own_columns(values, axis):
    share = values.shape[axis] // lax.axis_size("dp")
    return lax.dynamic_slice_in_dim(values, lax.axis_index("dp") * share, share, axis)


def slots_of(mask):
    return jnp.where(mask, jnp.cumsum(mask.astype(jnp.int32), axis=-1) - 1, -1)


def local_call(kernel, name, flops, **spec):
    return pl.pallas_call(
        kernel,
        name=name,
        cost_estimate=pl.CostEstimate(flops=flops, bytes_accessed=flops // 300, transcendentals=0),
        compiler_params=pltpu.CompilerParams(vmem_limit_bytes=56 * 2**20),
        **spec,
    )


def pick_kernel(slot_ref, scale_ref, lower_ref, upper_ref, out_ref):
    capacity, columns = out_ref.shape
    total = slot_ref.shape[-1]
    chosen = (slot_ref[...] == lax.broadcasted_iota(jnp.int32, (capacity, total), 0)).astype(F32).astype(BF)
    half = total // 2
    rows = jnp.dot(chosen[:, :half], lower_ref[...].reshape(half, columns), preferred_element_type=F32)
    rows += jnp.dot(chosen[:, half:], upper_ref[...].reshape(half, columns), preferred_element_type=F32)
    out_ref[...] = (rows * scale_ref[...]).astype(BF)


def pick_rows(slots, scale, lower, upper):
    blocks, groups, count, width = lower.shape
    total = 2 * blocks * count
    capacity = scale.shape[1]
    tile = 1024
    rows = pl.BlockSpec((blocks, None, count, tile), lambda g, j: (0, g, 0, j))
    return local_call(
        pick_kernel,
        "pick_rows",
        2 * groups * capacity * total * width,
        grid=(groups, width // tile),
        in_specs=[
            pl.BlockSpec((None, 1, total), lambda g, j: (g, 0, 0)),
            pl.BlockSpec((None, capacity, 1), lambda g, j: (g, 0, 0)),
            rows,
            rows,
        ],
        out_specs=pl.BlockSpec((None, capacity, tile), lambda g, j: (g, 0, j)),
        out_shape=jax.ShapeDtypeStruct((groups, capacity, width), BF),
    )(slots[:, None, :], scale, lower, upper)


def dot_nn(left, right):
    return lax.dot_general(left, right, (((1,), (0,)), ((), ())), preferred_element_type=F32)


def dot_nt(left, right):
    return lax.dot_general(left, right, (((1,), (1,)), ((), ())), preferred_element_type=F32)


def dot_tn(left, right):
    return lax.dot_general(left, right, (((0,), (0,)), ((), ())), preferred_element_type=F32)


def expert_kernel(x_ref, gateup_w, down_w, gate_ref, up_ref, act_ref, made_ref):
    x = x_ref[...]
    gate, up = dot_nn(x, gateup_w[0]), dot_nn(x, gateup_w[1])
    gate_ref[...], up_ref[...] = gate, up
    act = (gate * jax.nn.sigmoid(gate) * up).astype(BF)
    act_ref[...] = act
    made_ref[...] = dot_nn(act, down_w[...]).astype(BF)


def row_spec(block, columns):
    return pl.BlockSpec((block, columns), lambda i: (i, 0))


def held_spec(array):
    return pl.BlockSpec(array.shape, lambda i: (0,) * array.ndim, pipeline_mode=pl.Buffered(1))


def row_block(count):
    return max(b for b in range(16, min(count, 288) + 1, 16) if count % b == 0)


def expert_forward(x, gateup_w, down_w):
    count, width = x.shape
    hidden = gateup_w.shape[2]
    block = row_block(count)
    wide_shape = lambda dtype: jax.ShapeDtypeStruct((count, hidden), dtype)
    return local_call(
        expert_kernel,
        "expert_forward",
        6 * count * width * hidden,
        grid=(count // block,),
        in_specs=[row_spec(block, width), held_spec(gateup_w), held_spec(down_w)],
        out_specs=[row_spec(block, hidden)] * 3 + [row_spec(block, width)],
        out_shape=[wide_shape(F32), wide_shape(F32), wide_shape(BF), jax.ShapeDtypeStruct((count, width), BF)],
    )(x, gateup_w, down_w)


def middle_grads(gate, up, grad):
    sig = jax.nn.sigmoid(gate)
    slope = sig * (1.0 + gate * (1.0 - sig))
    return (grad * up * slope).astype(BF), (grad * (gate * sig)).astype(BF)


def expert_back_kernel(g_ref, gate_ref, up_ref, act_ref, gateup_w, down_w, gg_ref, gu_ref, back_ref, gain_ref):
    grad = dot_nt(g_ref[...], down_w[...])
    gain_ref[...] = jnp.sum(act_ref[...].astype(F32) * grad, axis=1, keepdims=True)
    grad_gate, grad_up = middle_grads(gate_ref[...], up_ref[...], grad)
    gg_ref[...], gu_ref[...] = grad_gate, grad_up
    back_ref[...] = (dot_nt(grad_gate, gateup_w[0]) + dot_nt(grad_up, gateup_w[1])).astype(BF)


def expert_back(g, gate, up, act, gateup_w, down_w):
    count, width = g.shape
    hidden = gateup_w.shape[2]
    block = row_block(count)
    rows, mids = row_spec(block, width), row_spec(block, hidden)
    return local_call(
        expert_back_kernel,
        "expert_back",
        6 * count * width * hidden,
        grid=(count // block,),
        in_specs=[rows, mids, mids, mids, held_spec(gateup_w), held_spec(down_w)],
        out_specs=[mids, mids, rows, row_spec(block, 1)],
        out_shape=[jax.ShapeDtypeStruct((count, hidden), BF)] * 2
        + [jax.ShapeDtypeStruct((count, width), BF), jax.ShapeDtypeStruct((count, 1), F32)],
    )(g, gate, up, act, gateup_w, down_w)


def expert_far_kernel(x_ref, g_ref, gateup_w, down_w, act_ref, gg_ref, gu_ref):
    x = x_ref[...]
    gate, up = dot_nn(x, gateup_w[0]), dot_nn(x, gateup_w[1])
    act_ref[...] = (gate * jax.nn.sigmoid(gate) * up).astype(BF)
    gg_ref[...], gu_ref[...] = middle_grads(gate, up, dot_nt(g_ref[...], down_w[...]))


def expert_far(x, g, gateup_w, down_w):
    count, width = x.shape
    hidden = gateup_w.shape[2]
    block = row_block(count)
    rows, mids = row_spec(block, width), row_spec(block, hidden)
    return local_call(
        expert_far_kernel,
        "expert_far",
        6 * count * width * hidden,
        grid=(count // block,),
        in_specs=[rows, rows, held_spec(gateup_w), held_spec(down_w)],
        out_specs=[mids] * 3,
        out_shape=[jax.ShapeDtypeStruct((count, hidden), BF)] * 3,
    )(x, g, gateup_w, down_w)


def expert_grad_kernel(_, x, g, act, gg, gu, far_x, far_g, far_act, far_gg, far_gu, gateup_ref, down_ref, acc_g, acc_u):
    step = pl.program_id(0)

    @pl.when(step == 0)
    def _():
        rows = x[...]
        acc_g[...] = dot_tn(rows, gg[...])
        acc_u[...] = dot_tn(rows, gu[...])
        down_ref[...] = dot_tn(act[...], g[...])

    @pl.when(step > 0)
    def _():
        rows = far_x[...]
        acc_g[...] += dot_tn(rows, far_gg[...])
        acc_u[...] += dot_tn(rows, far_gu[...])
        down_ref[...] += dot_tn(far_act[...], far_g[...])

    @pl.when(step == pl.num_programs(0) - 1)
    def _():
        gateup_ref[:, 0, :] = acc_g[...]
        gateup_ref[:, 1, :] = acc_u[...]


def expert_grads_of(own, far):
    count, width = own[0].shape
    hidden = own[2].shape[1]
    share = width // lax.axis_size("dp")
    steps = 1 + far[0].shape[0] // count
    held = lambda i, d: (0, 0)
    near_rows = pl.BlockSpec((count, share), lambda i, d: (0, d[0]))
    near_mid = pl.BlockSpec((count, hidden), held)
    far_rows = pl.BlockSpec((count, share), lambda i, d: (jnp.maximum(i - 1, 0), d[0]))
    far_mid = pl.BlockSpec((count, hidden), lambda i, d: (jnp.maximum(i - 1, 0), 0))
    return local_call(
        expert_grad_kernel,
        "expert_grads",
        6 * count * steps * share * hidden,
        grid_spec=pltpu.PrefetchScalarGridSpec(
            num_scalar_prefetch=1,
            grid=(steps,),
            in_specs=[near_rows, near_rows] + [near_mid] * 3 + [far_rows, far_rows] + [far_mid] * 3,
            out_specs=[
                pl.BlockSpec((share, 2, hidden), lambda i, d: (0, 0, 0)),
                pl.BlockSpec((hidden, share), held),
            ],
            scratch_shapes=[pltpu.VMEM((share, hidden), F32)] * 2,
        ),
        out_shape=[
            jax.ShapeDtypeStruct((share, 2, hidden), F32),
            jax.ShapeDtypeStruct((hidden, share), F32),
        ],
    )(lax.axis_index("dp").reshape(1), *own, *far)


def layout(length_row, place):
    blocks = (length_row + BLK - 1) // BLK
    ends = jnp.cumsum(blocks)
    starts = ends - blocks
    which = jnp.sum((place[:, None] // BLK >= ends[None, :]).astype(jnp.int32), axis=1)
    member = which[:, None] == jnp.arange(length_row.shape[0], dtype=jnp.int32)[None, :]
    opening = jnp.sum(jnp.where(member, starts[None, :], 0), axis=1)
    seq_len = jnp.sum(jnp.where(member, length_row[None, :], 0), axis=1)
    position = place - opening * BLK
    return (which, position, position < seq_len)


def rope_tables(position):
    half_dim = HD // 2
    freq = THETA ** (-2.0 * jnp.arange(half_dim, dtype=F32) / HD)
    angle = position.astype(F32)[:, None] * freq[None, :]
    return (
        jnp.concatenate([jnp.cos(angle), jnp.cos(angle)], -1),
        jnp.concatenate([jnp.sin(angle), jnp.sin(angle)], -1),
    )


def rotate(flat_rows, cosine, sine_table):
    count = flat_rows.shape[0]
    shaped = flat_rows.reshape(count, -1, HD)
    half_dim = HD // 2
    turned = jnp.concatenate([-shaped[..., half_dim:], shaped[..., :half_dim]], -1)
    return (shaped * cosine[:, None, :] + turned * sine_table[:, None, :]).reshape(count, -1)


def rotate_back(flat_rows, cosine, sine_table):
    count = flat_rows.shape[0]
    shaped = flat_rows.reshape(count, -1, HD)
    half_dim = HD // 2
    sined = shaped * sine_table[:, None, :]
    turned = jnp.concatenate([sined[..., half_dim:], -sined[..., :half_dim]], -1)
    return (shaped * cosine[:, None, :] + turned).reshape(count, -1)


def normalize(values, gain_vec):
    inverse = lax.rsqrt(jnp.mean(values * values, axis=-1, keepdims=True) + EPS)
    return (values * inverse * gain_vec, inverse)


def norm_back(values, inverse, gain_vec, gradient):
    scaled = values * inverse
    gain_term = jnp.sum(gradient * scaled, axis=0)
    grad_scaled = gradient * gain_vec
    back = inverse * (grad_scaled - scaled * jnp.mean(grad_scaled * scaled, axis=-1, keepdims=True))
    return (back, gain_term)


def silu_slope(values):
    sig = jax.nn.sigmoid(values)
    return sig * (1.0 + values * (1.0 - sig))


def scores_of(queries, key_rows, allowed):
    scores = dot(queries, key_rows, ((1,), (1,))) * HD ** (-0.5)
    return jnp.where(allowed, scores, FLOOR)


def attend_forward(queries, key_rows, values, allowed):
    pieces, totals = [], []
    for start in range(0, queries.shape[1], HD):
        head = slice(start, start + HD)
        scores = scores_of(queries[:, head], key_rows[:, head], allowed)
        peak = jnp.max(scores, axis=-1, keepdims=True)
        expon = jnp.exp(scores - peak)
        summed = jnp.sum(expon, axis=-1, keepdims=True)
        weights = (expon / summed).astype(BF)
        pieces.append(dot(weights, values[:, head], ((1,), (0,)), BF))
        totals.append(peak + jnp.log(summed))
    return (jnp.concatenate(pieces, 1), totals)


def attend_back(queries, key_rows, values, allowed, totals, grad_mixed):
    scale = HD ** (-0.5)
    grads = ([], [], [])
    for start, total in zip(range(0, queries.shape[1], HD), totals):
        head = slice(start, start + HD)
        block_q, block_k, block_g = queries[:, head], key_rows[:, head], grad_mixed[:, head]
        probs = jnp.exp(scores_of(block_q, block_k, allowed) - total)
        grad_p = dot(block_g, values[:, head], ((1,), (1,)))
        grad_s = (probs * (grad_p - jnp.sum(probs * grad_p, axis=-1, keepdims=True))).astype(BF)
        grads[0].append((dot(grad_s, block_k, ((1,), (0,))) * scale).astype(BF))
        grads[1].append((dot(grad_s, block_q, ((0,), (0,))) * scale).astype(BF))
        grads[2].append(dot(probs.astype(BF), block_g, ((0,), (0,)), BF))
    return tuple(jnp.concatenate(g, 1) for g in grads)


def on_device(
    hidden_in,
    teacher,
    seq_lengths,
    routes,
    attn_norm,
    qkv_proj,
    qkv_bias,
    out_proj,
    ffn_norm,
    router,
    shared_gateup,
    shared_down,
    shared_switch,
    expert_gateup,
    expert_down,
):
    tok_rows, width = hidden_in.shape
    sp_size = lax.axis_size("sp")
    dp_size = lax.axis_size("dp")
    me = lax.axis_index("sp")
    total_rows = tok_rows * sp_size
    lower_rows = total_rows // 2
    experts = router.shape[1]
    top_k = routes.shape[1]
    capacity = sp_size * min(tok_rows, 9 * tok_rows * top_k // (8 * experts))

    inputs = hidden_in.astype(F32)
    gain_one = attn_norm.astype(F32)
    normed_f, inverse_one = normalize(inputs, gain_one)
    *normed_halves, (gateup_w,), _ = gather_rows(
        normed_f.astype(BF), (lambda w: (w.transpose(1, 0, 2),), expert_gateup[0])
    )
    wide = dp_size <= 4

    owners = me ^ jnp.array(ORDER, jnp.int32)
    place = (owners[:, None] * tok_rows + jnp.arange(tok_rows, dtype=jnp.int32)[None, :]).reshape(-1)
    length_row = lax.dynamic_index_in_dim(seq_lengths, lax.axis_index("dp"), 0, keepdims=False)
    segment, position, is_valid = layout(length_row, place)
    cosine, sine_table = rope_tables(position)
    local_valid = is_valid[:tok_rows].astype(F32)
    allowed = (
        (segment[:, None] == segment[None, :])
        & (position[None, :] <= position[:, None])
        & is_valid[None, :]
    )

    bias = qkv_bias.reshape(3, 1, -1).astype(F32)
    normed_all = jnp.concatenate(normed_halves, 0)
    projected = [dot(normed_all, qkv_proj[j], ((1,), (0,))) + bias[j] for j in range(3)]
    queries = rotate(projected[0], cosine, sine_table).astype(BF)
    key_rows = rotate(projected[1], cosine, sine_table).astype(BF)
    values = projected[2].astype(BF)
    mixed, totals = attend_forward(queries, key_rows, values, allowed)
    upper = dot(mixed[lower_rows:], out_proj, ((1,), (0,)), BF)
    lower = dot(mixed[:lower_rows], out_proj, ((1,), (0,)), BF)

    (route_own,), _ = after((routes.T[None],), (mixed,))
    if wide:
        route_own = jnp.concatenate([route_own] + fetch_groups(route_own, False), 0)
    route_all = gather_small(route_own.reshape(-1, tok_rows))
    route_all = route_all.reshape(sp_size, -1, top_k, tok_rows)
    masks = jnp.any(route_all == me, axis=2)
    mask = masks[:, 0].reshape(total_rows)
    slots = slots_of(mask)[None]
    slot_range = jnp.arange(capacity, dtype=jnp.int32)
    pick = (slots[0][None, :] == slot_range[:, None]).astype(BF)

    middle = inputs + sum_rows(upper, lower)[0]

    gain_two = ffn_norm.astype(F32)
    normed_two_f, inverse_two = normalize(middle, gain_two)
    normed_two = normed_two_f.astype(BF)
    fetched_two = fetch_groups(normed_two, False) if wide else []
    *two_halves, _, (pick, slots) = gather_rows(normed_two, None, (pick, slots))

    heads_in = jnp.concatenate([router, shared_switch[:, None]], axis=1)
    is_me = (jnp.arange(experts) == me).astype(F32)

    def steer_rows(rows):
        logits = dot(rows, heads_in, ((1,), (0,)))
        return jax.nn.softmax(logits[:, :experts], axis=-1), jax.nn.sigmoid(logits[:, experts:])

    steered = [steer_rows(rows) for rows in two_halves]
    probs, switch = (jnp.concatenate(both, 0) for both in zip(*steered))
    share = jnp.sum(probs * is_me[None, :], axis=1) * mask.astype(F32)
    share_rows = jnp.sum(pick.astype(F32) * share[None, :], axis=1, keepdims=True)

    down_w = expert_down[0]
    blocks = (sp_size // 2, 1, tok_rows, width)
    ones = jnp.ones((1, capacity, 1), F32)
    rows_in = pick_rows(slots, ones, *(rows.reshape(blocks) for rows in two_halves))[0]
    gate_e, up_e, acted_e, made = expert_forward(rows_in, gateup_w, down_w)
    two_halves, (made, *fetched_two[:1]) = after(two_halves, (made, *fetched_two[:1]))

    gate_sw, up_sw = shared_gateup[:, 0, :], shared_gateup[:, 1, :]
    gate_s = [dot(rows, gate_sw, ((1,), (0,))) for rows in two_halves]
    up_s = [dot(rows, up_sw, ((1,), (0,))) for rows in two_halves]
    acted_s = [(jax.nn.silu(g) * u).astype(BF) for g, u in zip(gate_s, up_s)]
    (acted_s[1],), fetched_two[1:2] = after((acted_s[1],), fetched_two[1:2])
    halves = (slice(0, lower_rows), slice(lower_rows, None))

    def ffn_part(side):
        rows = halves[side]
        shared = dot(acted_s[side], shared_down, ((1,), (0,)))
        routed = dot(pick[:, rows], made, ((0,), (0,)))
        return (steered[side][1] * shared + share[rows, None] * routed).astype(BF)

    ffn_upper = ffn_part(1)
    ffn_lower = ffn_part(0)
    (ffn_lower,), fetched_two[2:] = after((ffn_lower,), fetched_two[2:])
    output = middle + sum_rows(ffn_upper, ffn_lower)[0]
    error = (output - teacher.astype(F32)) * local_valid[:, None]
    squares = jnp.sum(error * error)
    count = jnp.sum(seq_lengths).astype(F32)

    if wide:
        others = dp_size - 1
        sides = (me % 2) ^ jnp.arange(2, dtype=jnp.int32)
        in_order = (2 * jnp.arange(sp_size // 2, dtype=jnp.int32)[None, :] + sides[:, None]).reshape(-1)
        same_place = (in_order[:, None] ^ me) == jnp.array(ORDER, jnp.int32)[None, :]
        in_order = jnp.argmax(same_place, axis=1)
        far_slots = slots_of(masks[:, 1:].transpose(1, 0, 2).reshape(others, total_rows))
        sp_slots = far_slots.reshape(others, sp_size, tok_rows)[:, in_order].reshape(others, total_rows)

        def share_far(*rows_far):
            far_probs = [steer_rows(rows.reshape(-1, width))[0] for rows in rows_far]
            share = jnp.concatenate([jnp.sum(p * is_me[None, :], axis=1) for p in far_probs], 0)
            share = share.reshape(sp_size, others, tok_rows).transpose(1, 0, 2).reshape(others, 1, total_rows)
            share = jnp.where(sp_slots[:, None, :] == slot_range[None, :, None], share, 0.0)
            return jnp.sum(share, axis=2, keepdims=True)

    error_low = error.astype(BF)
    fetched_error = fetch_groups(error_low, False) if wide else []
    *error_halves, _, fetched_error[:1] = gather_rows(error_low, None, fetched_error[:1])
    if wide:
        fetched_two, _ = after(fetched_two, (output,))
        two_side = gather_side(jnp.stack(fetched_two, 0))
    grad_made = pick_rows(slots, share_rows[None], *(rows.reshape(blocks) for rows in error_halves))[0]
    grad_gate_e, grad_up_e, back_e, gain_rows = expert_back(
        grad_made, gate_e, up_e, acted_e, gateup_w, down_w
    )
    error_halves, (back_e, *fetched_error[1:2]) = after(error_halves, (back_e, *fetched_error[1:2]))
    grad_shared = [(s[1] * rows.astype(F32)).astype(BF) for s, rows in zip(steered, error_halves)]
    joined = lambda sides: jnp.concatenate(sides, 0)
    grad_act_s = [dot(g, shared_down, ((1,), (1,))) for g in grad_shared]
    grad_gate_s = [(g * u * silu_slope(v)).astype(BF) for g, u, v in zip(grad_act_s, up_s, gate_s)]
    grad_up_s = [(g * jax.nn.silu(v)).astype(BF) for g, v in zip(grad_act_s, gate_s)]
    own_act, own_grad = joined(acted_s), joined(grad_shared)
    down_term = dot(own_act, own_grad, ((0,), (0,)), BF)
    grad_up_s, (down_term, *fetched_error[2:]) = after(grad_up_s, (down_term, *fetched_error[2:]))
    if wide:
        far_own = jnp.stack(fetched_error, 0)
        far_half = tok_rows // 2
        far_x, far_y = swap(far_own, 2), swap(far_own, 4)
    two_all = joined(two_halves)
    mid_term = dot(two_all, jnp.concatenate([joined(grad_gate_s), joined(grad_up_s)], 1), ((0,), (0,)), BF)
    down_shared = sum_groups(down_term, 1)
    mid_shared = sum_groups(mid_term, 0)
    if wide:
        (back_e,), (far_x, far_y, _) = after((back_e,), (far_x, far_y, mid_term))
        far_diag = jnp.concatenate([swap(far_y[:, :far_half], 2), swap(far_x[:, far_half:], 4)], 1)
    switch_part = jnp.concatenate(
        [jnp.sum(a.astype(F32) * g, axis=1) for a, g in zip(acted_s, grad_act_s)], 0
    )

    def back_part(side):
        return (
            dot(grad_gate_s[side], gate_sw, ((1,), (1,)))
            + dot(grad_up_s[side], up_sw, ((1,), (1,)))
            + dot(pick[:, halves[side]], back_e, ((0,), (0,)))
        ).astype(BF)

    back_upper = back_part(1)
    back_lower = back_part(0)
    gain_tokens = jnp.sum(pick.astype(F32) * gain_rows, axis=0)
    scalars = jnp.concatenate(
        [gain_tokens[None, :] * is_me[:, None], switch_part[None, :], jnp.zeros((7, total_rows), F32)], axis=0
    )
    scalars, _ = sum_small(scalars.reshape(16, sp_size, tok_rows).transpose(1, 0, 2), jnp.zeros((1, 16, tok_rows), F32))
    gains, switch_sum = scalars[:experts].T, scalars[experts]
    my_probs, my_switch = probs[:tok_rows], switch[:tok_rows, 0]
    grad_switch = switch_sum * (1.0 - my_switch)
    grad_logits = gains - my_probs * jnp.sum(gains, axis=1, keepdims=True)
    steer = jnp.concatenate([grad_logits, grad_switch[:, None]], axis=1)
    if wide:
        (back_lower,), (far_diag,) = after((back_lower,), (far_diag,))
        error_far = jnp.stack([far_own, far_x, far_y, far_diag], 0)
        error_far = (error_far, swap(error_far, 1))
        two_far = (two_side, swap(two_side, 1))
    far_task = None
    if wide:

        def make_far(lower, upper, *rows_far):
            share = share_far(*rows_far)
            return pick_rows(far_slots, share, lower, upper).reshape(-1, width), *rows_far

        far_task = (make_far, *error_far, *two_far)
    (back_lower,), (down_shared,) = after((back_lower,), (down_shared,))
    summed, far_work = sum_rows(back_upper, back_lower, far_task)
    grad_normed = summed + jnp.einsum(
        "te,de->td", steer, heads_in.astype(F32), precision=HIGH
    )
    steer_term = jnp.einsum("te,td->ed", steer, normed_two.astype(F32), precision=HIGH)
    grad_middle_n, ffnnorm_term = norm_back(middle, inverse_two, gain_two, grad_normed)
    grad_middle = error + grad_middle_n

    far_task = None
    if wide:
        far_made, *two_far = far_work
        ones_far = jnp.ones((others, capacity, 1), F32)
        far_task = (lambda *rows: (pick_rows(sp_slots, ones_far, *rows).reshape(-1, width),), *two_far)
    *attn_halves, far_work, _ = gather_rows(grad_middle.astype(BF), far_task)
    grad_mixed = joined([dot(rows, out_proj, ((1,), (1,)), BF) for rows in attn_halves])
    grad_q, grad_k, grad_v = attend_back(
        queries, key_rows, values, allowed, totals, grad_mixed
    )
    grad_proj = (
        rotate_back(grad_q.astype(F32), cosine, sine_table).astype(BF),
        rotate_back(grad_k.astype(F32), cosine, sine_table).astype(BF),
        grad_v,
    )

    def input_part(rows):
        return sum(dot(grad_proj[j][rows], qkv_proj[j], ((1,), (1,))) for j in range(3)).astype(BF)

    input_upper = input_part(halves[1])
    input_lower = input_part(halves[0])
    outproj_term = dot(mixed, joined(attn_halves), ((0,), (0,)), BF)
    qkv_terms = jnp.stack([dot(normed_all, g, ((0,), (0,)), BF) for g in grad_proj], 0)
    bias_term = jnp.stack([jnp.sum(g.astype(F32), axis=0) for g in grad_proj], 0)
    if wide:
        (far_in,) = far_work
        grad_normed_one, far_work = sum_rows(
            input_upper,
            input_lower,
            (lambda made, *_: (made, *expert_far(far_in, made, gateup_w, down_w)), far_made, outproj_term, qkv_terms, mid_shared),
        )
        far_made, far_act, far_gate, far_up = far_work
        gateup_expert, down_expert = expert_grads_of(
            (rows_in, grad_made, acted_e, grad_gate_e, grad_up_e),
            (far_in, far_made, far_act, far_gate, far_up),
        )
    else:
        grad_normed_one, _ = sum_rows(input_upper, input_lower)
        gateup_expert = jnp.stack(
            [
                sum_groups(dot(rows_in, grad_gate_e, ((0,), (0,)), BF), 0),
                sum_groups(dot(rows_in, grad_up_e, ((0,), (0,)), BF), 0),
            ],
            axis=1,
        )
        down_expert = sum_groups(dot(acted_e, grad_made, ((0,), (0,)), BF), 1)
    grad_input_n, attnnorm_term = norm_back(inputs, inverse_one, gain_one, grad_normed_one)
    hidden_grad = grad_middle + grad_input_n
    outproj_grad = sum_groups(outproj_term, 1)
    qkvproj_grad = sum_groups(qkv_terms, 1)

    small = jnp.concatenate([attnnorm_term[None], ffnnorm_term[None], steer_term], axis=0)
    kinds = small.shape[0]
    cell = width // (dp_size * sp_size)
    small = small.reshape(kinds, dp_size, sp_size, cell).transpose(2, 1, 0, 3)[owners]
    small = small.reshape(sp_size, dp_size, kinds * cell)
    small, squares = sum_small(small, jnp.full((1,) + small.shape[1:], squares, F32))
    pairs = bias_term.reshape(-1, HD)
    bias_cells = pairs.reshape(pairs.shape[0], dp_size, -1).transpose(1, 0, 2).reshape(dp_size, -1)
    small = jnp.concatenate([small, bias_cells], axis=1)
    small, squares = shift_groups(small, jnp.full(small.shape[1:], squares[0, 0], F32))
    loss_value = squares[0] / (2.0 * count * D)
    gains_out = small[: kinds * cell].reshape(kinds, cell)
    qkvbias_grad = small[kinds * cell :].reshape(3, -1, HD // dp_size)
    return (
        output,
        loss_value,
        hidden_grad,
        gains_out[0],
        qkvproj_grad,
        qkvbias_grad,
        outproj_grad,
        gains_out[1],
        gains_out[2 : 2 + experts].T,
        mid_shared.reshape(-1, 2, gate_sw.shape[1]),
        down_shared,
        gains_out[2 + experts],
        gateup_expert[None],
        down_expert[None],
    )


def solution(mesh):
    in_specs = (
        P(("dp", "sp"), None),
        P(("dp", "sp"), None),
        P(),
        P(("dp", "sp"), None),
        P(),
        P(None, None, "sp"),
        P(None, "sp", None),
        P("sp", None),
        P(),
        P(),
        P(None, None, "sp"),
        P("sp", None),
        P(),
        P("sp", None, None, None),
        P("sp", None, None),
    )
    out_specs = (
        P(("dp", "sp"), None),
        P(),
        P(("dp", "sp"), None),
        P(("dp", "sp")),
        P(None, "dp", "sp"),
        P(None, "sp", "dp"),
        P("sp", "dp"),
        P(("dp", "sp")),
        P(("dp", "sp"), None),
        P("dp", None, "sp"),
        P("sp", "dp"),
        P(("dp", "sp")),
        P("sp", "dp", None, None),
        P("sp", None, "dp"),
    )
    return jax.shard_map(
        on_device, mesh=mesh, in_specs=in_specs, out_specs=out_specs, check_vma=False
    )
```

```python
import jax
import jax.numpy as jnp
from jax import lax
from jax.experimental import pallas as pl
from jax.experimental.pallas import tpu as pltpu
from jax.sharding import PartitionSpec as P

D = 2048
HD = 128
BLK = 128
MAXSEQ = 8

EPS = 1e-06
THETA = 1000000.0
FLOOR = -1e30
HIGH = lax.Precision.HIGHEST
BF = jnp.bfloat16
F32 = jnp.float32

ORDER = (0, 2, 4, 6, 1, 3, 5, 7)


def after(values, work):
    values, work = tuple(values), tuple(work)
    if not work or not values:
        return values, work
    tied = lax.optimization_barrier((*values, *work))
    return tied[: len(values)], tied[len(values) :]


def between(first, last, task):
    if task is None:
        return tuple(last), ()
    function, *inputs = task
    inputs, _ = after(inputs, first)
    return after(last, function(*inputs))


def dot(left, right, dims, dtype=F32):
    return lax.dot_general(left, right, (dims, ((), ())), preferred_element_type=F32).astype(dtype)


def swap(values, distance):
    return lax.ppermute(values, "sp", [(i, i ^ distance) for i in range(8)])


def gather_rows(own, task=None, first=()):
    half = own.shape[0] // 2
    over_x, over_y = swap(own, 2), swap(own, 4)
    (over_x, over_y), work = between((own,), (over_x, over_y), task)
    (over_x, over_y), first = after((over_x, over_y), first)
    far_top, far_bottom = swap(over_y[:half], 2), swap(over_x[half:], 4)
    lower = jnp.concatenate([own, over_x, over_y, far_top, far_bottom], 0)
    return lower, swap(lower, 1), work, first


def gather_side(own):
    return lax.all_gather(own, "sp", axis_index_groups=[[0, 2, 4, 6], [1, 3, 5, 7]])


def gather_small(own):
    held = own[None]
    for distance in (2, 4, 1):
        held = jnp.concatenate([held, swap(held, distance)], 0)
    return held


def sum_small(parts, total):
    for distance in (1, 4, 2):
        keep = parts.shape[0] // 2
        got = swap(jnp.concatenate([parts[keep:], total], 0), distance)
        parts, total = parts[:keep] + got[:keep], total + got[keep:]
    return parts[0], total[0]


def sum_rows(upper, lower, task=None):
    rows = lower.shape[0] // 4
    half = rows // 2
    got = swap(upper, 1)
    chip = lower.astype(F32) + got.astype(F32)
    low = chip.astype(BF)
    own, over_x, over_y, far = (slice(k * rows, (k + 1) * rows) for k in range(4))
    low_x, low_y, low_far = low[over_x], low[over_y], low[far]
    from_x = swap(jnp.concatenate([low_far[:half], low_x[:half]], 0), 2)
    from_y = swap(jnp.concatenate([low_far[half:], low_y[half:]], 0), 4)
    (from_x, from_y), work = between((low,), (from_x, from_y), task)
    pass_y = (chip[over_y][:half] + from_x[:half].astype(F32)).astype(BF)
    pass_x = (chip[over_x][half:] + from_y[:half].astype(F32)).astype(BF)
    last_y, last_x = swap(pass_y, 4), swap(pass_x, 2)
    mine = chip[own]
    top = mine[:half] + from_x[half:].astype(F32) + last_y.astype(F32)
    bottom = mine[half:] + from_y[half:].astype(F32) + last_x.astype(F32)
    return jnp.concatenate([top, bottom], 0), work


def sum_groups(grads, dim):
    return lax.psum_scatter(grads, "dp", scatter_dimension=dim, tiled=True).astype(F32)


def shift_groups(blocks, total):
    size = lax.axis_size("dp")
    me = lax.axis_index("dp")
    pick = lambda k: lax.dynamic_index_in_dim(blocks, (me + k) % size, 0, keepdims=False)
    mine = jnp.stack([pick(0), total])
    summed = mine[0]
    totals = jnp.zeros((size,) + total.shape, total.dtype).at[me].set(total)
    for k in range(1, size):
        got = lax.ppermute(jnp.stack([pick(k), total]), "dp", [(i, (i + k) % size) for i in range(size)])
        summed = summed + got[0]
        totals = totals.at[(me - k) % size].set(got[1])
    return summed, jnp.sum(totals, axis=0)


def fetch_groups(own, chained=True):
    size = lax.axis_size("dp")
    got = []
    for k in range(1, size):
        moved, _ = after((own,), got[-1:] if chained else ())
        got.append(lax.ppermute(moved[0], "dp", [((i + k) % size, i) for i in range(size)]))
    return got


def own_columns(values, axis):
    share = values.shape[axis] // lax.axis_size("dp")
    return lax.dynamic_slice_in_dim(values, lax.axis_index("dp") * share, share, axis)


def slots_of(mask):
    return jnp.where(mask, jnp.cumsum(mask.astype(jnp.int32), axis=-1) - 1, -1)


def local_call(kernel, name, flops, **spec):
    return pl.pallas_call(
        kernel,
        name=name,
        cost_estimate=pl.CostEstimate(flops=flops, bytes_accessed=flops // 300, transcendentals=0),
        compiler_params=pltpu.CompilerParams(vmem_limit_bytes=56 * 2**20),
        **spec,
    )


def pick_kernel(slot_ref, scale_ref, lower_ref, upper_ref, out_ref):
    capacity, columns = out_ref.shape
    total = slot_ref.shape[-1]
    chosen = (slot_ref[...] == lax.broadcasted_iota(jnp.int32, (capacity, total), 0)).astype(F32).astype(BF)
    half = total // 2
    rows = jnp.dot(chosen[:, :half], lower_ref[...].reshape(half, columns), preferred_element_type=F32)
    rows += jnp.dot(chosen[:, half:], upper_ref[...].reshape(half, columns), preferred_element_type=F32)
    out_ref[...] = (rows * scale_ref[...]).astype(BF)


def pick_rows(slots, scale, lower, upper):
    blocks, groups, count, width = lower.shape
    total = 2 * blocks * count
    capacity = scale.shape[1]
    tile = 2048
    rows = pl.BlockSpec((blocks, None, count, tile), lambda g, j: (0, g, 0, j))
    return local_call(
        pick_kernel,
        "pick_rows",
        2 * groups * capacity * total * width,
        grid=(groups, width // tile),
        in_specs=[
            pl.BlockSpec((None, 1, total), lambda g, j: (g, 0, 0)),
            pl.BlockSpec((None, capacity, 1), lambda g, j: (g, 0, 0)),
            rows,
            rows,
        ],
        out_specs=pl.BlockSpec((None, capacity, tile), lambda g, j: (g, 0, j)),
        out_shape=jax.ShapeDtypeStruct((groups, capacity, width), BF),
    )(slots[:, None, :], scale, lower, upper)


def dot_nn(left, right):
    return lax.dot_general(left, right, (((1,), (0,)), ((), ())), preferred_element_type=F32)


def dot_nt(left, right):
    return lax.dot_general(left, right, (((1,), (1,)), ((), ())), preferred_element_type=F32)


def dot_tn(left, right):
    return lax.dot_general(left, right, (((0,), (0,)), ((), ())), preferred_element_type=F32)


def expert_kernel(x_ref, gateup_w, down_w, gate_ref, up_ref, act_ref, made_ref):
    x = x_ref[...]
    gate, up = dot_nn(x, gateup_w[0]), dot_nn(x, gateup_w[1])
    gate_ref[...], up_ref[...] = gate, up
    act = (gate * jax.nn.sigmoid(gate) * up).astype(BF)
    act_ref[...] = act
    made_ref[...] = dot_nn(act, down_w[...]).astype(BF)


def row_spec(block, columns):
    return pl.BlockSpec((block, columns), lambda i: (i, 0))


def held_spec(array):
    return pl.BlockSpec(array.shape, lambda i: (0,) * array.ndim, pipeline_mode=pl.Buffered(1))


def row_block(count):
    return max(b for b in range(16, min(count, 288) + 1, 16) if count % b == 0)


def expert_forward(x, gateup_w, down_w):
    count, width = x.shape
    hidden = gateup_w.shape[2]
    block = row_block(count)
    wide_shape = lambda dtype: jax.ShapeDtypeStruct((count, hidden), dtype)
    return local_call(
        expert_kernel,
        "expert_forward",
        6 * count * width * hidden,
        grid=(count // block,),
        in_specs=[row_spec(block, width), held_spec(gateup_w), held_spec(down_w)],
        out_specs=[row_spec(block, hidden)] * 3 + [row_spec(block, width)],
        out_shape=[wide_shape(F32), wide_shape(F32), wide_shape(BF), jax.ShapeDtypeStruct((count, width), BF)],
    )(x, gateup_w, down_w)


def middle_grads(gate, up, grad):
    sig = jax.nn.sigmoid(gate)
    slope = sig * (1.0 + gate * (1.0 - sig))
    return (grad * up * slope).astype(BF), (grad * (gate * sig)).astype(BF)


def expert_back_kernel(g_ref, gate_ref, up_ref, act_ref, gateup_w, down_w, gg_ref, gu_ref, back_ref, gain_ref):
    grad = dot_nt(g_ref[...], down_w[...])
    gain_ref[...] = jnp.sum(act_ref[...].astype(F32) * grad, axis=1, keepdims=True)
    grad_gate, grad_up = middle_grads(gate_ref[...], up_ref[...], grad)
    gg_ref[...], gu_ref[...] = grad_gate, grad_up
    back_ref[...] = (dot_nt(grad_gate, gateup_w[0]) + dot_nt(grad_up, gateup_w[1])).astype(BF)


def expert_back(g, gate, up, act, gateup_w, down_w):
    count, width = g.shape
    hidden = gateup_w.shape[2]
    block = row_block(count)
    rows, mids = row_spec(block, width), row_spec(block, hidden)
    return local_call(
        expert_back_kernel,
        "expert_back",
        6 * count * width * hidden,
        grid=(count // block,),
        in_specs=[rows, mids, mids, mids, held_spec(gateup_w), held_spec(down_w)],
        out_specs=[mids, mids, rows, row_spec(block, 1)],
        out_shape=[jax.ShapeDtypeStruct((count, hidden), BF)] * 2
        + [jax.ShapeDtypeStruct((count, width), BF), jax.ShapeDtypeStruct((count, 1), F32)],
    )(g, gate, up, act, gateup_w, down_w)


def expert_far_kernel(x_ref, g_ref, gateup_w, down_w, act_ref, gg_ref, gu_ref):
    x = x_ref[...]
    gate, up = dot_nn(x, gateup_w[0]), dot_nn(x, gateup_w[1])
    act_ref[...] = (gate * jax.nn.sigmoid(gate) * up).astype(BF)
    gg_ref[...], gu_ref[...] = middle_grads(gate, up, dot_nt(g_ref[...], down_w[...]))


def expert_far(x, g, gateup_w, down_w):
    count, width = x.shape
    hidden = gateup_w.shape[2]
    block = row_block(count)
    rows, mids = row_spec(block, width), row_spec(block, hidden)
    return local_call(
        expert_far_kernel,
        "expert_far",
        6 * count * width * hidden,
        grid=(count // block,),
        in_specs=[rows, rows, held_spec(gateup_w), held_spec(down_w)],
        out_specs=[mids] * 3,
        out_shape=[jax.ShapeDtypeStruct((count, hidden), BF)] * 3,
    )(x, g, gateup_w, down_w)


def expert_grad_kernel(_, x, g, act, gg, gu, far_x, far_g, far_act, far_gg, far_gu, gateup_ref, down_ref, acc_g, acc_u):
    step = pl.program_id(0)

    @pl.when(step == 0)
    def _():
        rows = x[...]
        acc_g[...] = dot_tn(rows, gg[...])
        acc_u[...] = dot_tn(rows, gu[...])
        down_ref[...] = dot_tn(act[...], g[...])

    @pl.when(step > 0)
    def _():
        rows = far_x[...]
        acc_g[...] += dot_tn(rows, far_gg[...])
        acc_u[...] += dot_tn(rows, far_gu[...])
        down_ref[...] += dot_tn(far_act[...], far_g[...])

    @pl.when(step == pl.num_programs(0) - 1)
    def _():
        gateup_ref[:, 0, :] = acc_g[...]
        gateup_ref[:, 1, :] = acc_u[...]


def expert_grads_of(own, far):
    count, width = own[0].shape
    hidden = own[2].shape[1]
    share = width // lax.axis_size("dp")
    steps = 1 + far[0].shape[0] // count
    held = lambda i, d: (0, 0)
    near_rows = pl.BlockSpec((count, share), lambda i, d: (0, d[0]))
    near_mid = pl.BlockSpec((count, hidden), held)
    far_rows = pl.BlockSpec((count, share), lambda i, d: (jnp.maximum(i - 1, 0), d[0]))
    far_mid = pl.BlockSpec((count, hidden), lambda i, d: (jnp.maximum(i - 1, 0), 0))
    return local_call(
        expert_grad_kernel,
        "expert_grads",
        6 * count * steps * share * hidden,
        grid_spec=pltpu.PrefetchScalarGridSpec(
            num_scalar_prefetch=1,
            grid=(steps,),
            in_specs=[near_rows, near_rows] + [near_mid] * 3 + [far_rows, far_rows] + [far_mid] * 3,
            out_specs=[
                pl.BlockSpec((share, 2, hidden), lambda i, d: (0, 0, 0)),
                pl.BlockSpec((hidden, share), held),
            ],
            scratch_shapes=[pltpu.VMEM((share, hidden), F32)] * 2,
        ),
        out_shape=[
            jax.ShapeDtypeStruct((share, 2, hidden), F32),
            jax.ShapeDtypeStruct((hidden, share), F32),
        ],
    )(lax.axis_index("dp").reshape(1), *own, *far)


def layout(length_row, place):
    blocks = (length_row + BLK - 1) // BLK
    ends = jnp.cumsum(blocks)
    starts = ends - blocks
    which = jnp.sum((place[:, None] // BLK >= ends[None, :]).astype(jnp.int32), axis=1)
    member = which[:, None] == jnp.arange(length_row.shape[0], dtype=jnp.int32)[None, :]
    opening = jnp.sum(jnp.where(member, starts[None, :], 0), axis=1)
    seq_len = jnp.sum(jnp.where(member, length_row[None, :], 0), axis=1)
    position = place - opening * BLK
    return (which, position, position < seq_len)


def rope_tables(position):
    half_dim = HD // 2
    freq = THETA ** (-2.0 * jnp.arange(half_dim, dtype=F32) / HD)
    angle = position.astype(F32)[:, None] * freq[None, :]
    return (
        jnp.concatenate([jnp.cos(angle), jnp.cos(angle)], -1),
        jnp.concatenate([jnp.sin(angle), jnp.sin(angle)], -1),
    )


def rotate(flat_rows, cosine, sine_table):
    count = flat_rows.shape[0]
    shaped = flat_rows.reshape(count, -1, HD)
    half_dim = HD // 2
    turned = jnp.concatenate([-shaped[..., half_dim:], shaped[..., :half_dim]], -1)
    return (shaped * cosine[:, None, :] + turned * sine_table[:, None, :]).reshape(count, -1)


def rotate_back(flat_rows, cosine, sine_table):
    count = flat_rows.shape[0]
    shaped = flat_rows.reshape(count, -1, HD)
    half_dim = HD // 2
    sined = shaped * sine_table[:, None, :]
    turned = jnp.concatenate([sined[..., half_dim:], -sined[..., :half_dim]], -1)
    return (shaped * cosine[:, None, :] + turned).reshape(count, -1)


def normalize(values, gain_vec):
    inverse = lax.rsqrt(jnp.mean(values * values, axis=-1, keepdims=True) + EPS)
    return (values * inverse * gain_vec, inverse)


def norm_back(values, inverse, gain_vec, gradient):
    scaled = values * inverse
    gain_term = jnp.sum(gradient * scaled, axis=0)
    grad_scaled = gradient * gain_vec
    back = inverse * (grad_scaled - scaled * jnp.mean(grad_scaled * scaled, axis=-1, keepdims=True))
    return (back, gain_term)


def silu_slope(values):
    sig = jax.nn.sigmoid(values)
    return sig * (1.0 + values * (1.0 - sig))


def scores_of(queries, key_rows, allowed):
    scores = dot(queries, key_rows, ((1,), (1,))) * HD ** (-0.5)
    return jnp.where(allowed, scores, FLOOR)


def attend_forward(queries, key_rows, values, allowed):
    pieces, totals = [], []
    for start in range(0, queries.shape[1], HD):
        head = slice(start, start + HD)
        scores = scores_of(queries[:, head], key_rows[:, head], allowed)
        peak = jnp.max(scores, axis=-1, keepdims=True)
        expon = jnp.exp(scores - peak)
        summed = jnp.sum(expon, axis=-1, keepdims=True)
        weights = (expon / summed).astype(BF)
        pieces.append(dot(weights, values[:, head], ((1,), (0,)), BF))
        totals.append(peak + jnp.log(summed))
    return (jnp.concatenate(pieces, 1), totals)


def attend_back(queries, key_rows, values, allowed, totals, grad_mixed):
    scale = HD ** (-0.5)
    grads = ([], [], [])
    for start, total in zip(range(0, queries.shape[1], HD), totals):
        head = slice(start, start + HD)
        block_q, block_k, block_g = queries[:, head], key_rows[:, head], grad_mixed[:, head]
        probs = jnp.exp(scores_of(block_q, block_k, allowed) - total)
        grad_p = dot(block_g, values[:, head], ((1,), (1,)))
        grad_s = (probs * (grad_p - jnp.sum(probs * grad_p, axis=-1, keepdims=True))).astype(BF)
        grads[0].append((dot(grad_s, block_k, ((1,), (0,))) * scale).astype(BF))
        grads[1].append((dot(grad_s, block_q, ((0,), (0,))) * scale).astype(BF))
        grads[2].append(dot(probs.astype(BF), block_g, ((0,), (0,)), BF))
    return tuple(jnp.concatenate(g, 1) for g in grads)


def on_device(
    hidden_in,
    teacher,
    seq_lengths,
    routes,
    attn_norm,
    qkv_proj,
    qkv_bias,
    out_proj,
    ffn_norm,
    router,
    shared_gateup,
    shared_down,
    shared_switch,
    expert_gateup,
    expert_down,
):
    tok_rows, width = hidden_in.shape
    sp_size = lax.axis_size("sp")
    dp_size = lax.axis_size("dp")
    me = lax.axis_index("sp")
    total_rows = tok_rows * sp_size
    lower_rows = total_rows // 2
    experts = router.shape[1]
    top_k = routes.shape[1]
    capacity = sp_size * min(tok_rows, 9 * tok_rows * top_k // (8 * experts))

    inputs = hidden_in.astype(F32)
    gain_one = attn_norm.astype(F32)
    normed_f, inverse_one = normalize(inputs, gain_one)
    *normed_halves, (gateup_w,), _ = gather_rows(
        normed_f.astype(BF), (lambda w: (w.transpose(1, 0, 2),), expert_gateup[0])
    )
    wide = dp_size <= 4

    owners = me ^ jnp.array(ORDER, jnp.int32)
    place = (owners[:, None] * tok_rows + jnp.arange(tok_rows, dtype=jnp.int32)[None, :]).reshape(-1)
    length_row = lax.dynamic_index_in_dim(seq_lengths, lax.axis_index("dp"), 0, keepdims=False)
    segment, position, is_valid = layout(length_row, place)
    cosine, sine_table = rope_tables(position)
    local_valid = is_valid[:tok_rows].astype(F32)
    allowed = (
        (segment[:, None] == segment[None, :])
        & (position[None, :] <= position[:, None])
        & is_valid[None, :]
    )

    bias = qkv_bias.reshape(3, 1, -1).astype(F32)
    normed_all = jnp.concatenate(normed_halves, 0)
    projected = [dot(normed_all, qkv_proj[j], ((1,), (0,))) + bias[j] for j in range(3)]
    queries = rotate(projected[0], cosine, sine_table).astype(BF)
    key_rows = rotate(projected[1], cosine, sine_table).astype(BF)
    values = projected[2].astype(BF)
    mixed, totals = attend_forward(queries, key_rows, values, allowed)
    upper = dot(mixed[lower_rows:], out_proj, ((1,), (0,)), BF)
    lower = dot(mixed[:lower_rows], out_proj, ((1,), (0,)), BF)

    (route_own,), _ = after((routes.T[None],), (mixed,))
    if wide:
        route_own = jnp.concatenate([route_own] + fetch_groups(route_own, False), 0)
    route_all = gather_small(route_own.reshape(-1, tok_rows))
    route_all = route_all.reshape(sp_size, -1, top_k, tok_rows)
    masks = jnp.any(route_all == me, axis=2)
    mask = masks[:, 0].reshape(total_rows)
    slots = slots_of(mask)[None]
    slot_range = jnp.arange(capacity, dtype=jnp.int32)
    pick = (slots[0][None, :] == slot_range[:, None]).astype(BF)

    middle = inputs + sum_rows(upper, lower)[0]

    gain_two = ffn_norm.astype(F32)
    normed_two_f, inverse_two = normalize(middle, gain_two)
    normed_two = normed_two_f.astype(BF)
    fetched_two = fetch_groups(normed_two, False) if wide else []
    *two_halves, _, (pick, slots) = gather_rows(normed_two, None, (pick, slots))

    heads_in = jnp.concatenate([router, shared_switch[:, None]], axis=1)
    is_me = (jnp.arange(experts) == me).astype(F32)

    def steer_rows(rows):
        logits = dot(rows, heads_in, ((1,), (0,)))
        return jax.nn.softmax(logits[:, :experts], axis=-1), jax.nn.sigmoid(logits[:, experts:])

    steered = [steer_rows(rows) for rows in two_halves]
    probs, switch = (jnp.concatenate(both, 0) for both in zip(*steered))
    share = jnp.sum(probs * is_me[None, :], axis=1) * mask.astype(F32)
    share_rows = jnp.sum(pick.astype(F32) * share[None, :], axis=1, keepdims=True)

    down_w = expert_down[0]
    blocks = (sp_size // 2, 1, tok_rows, width)
    ones = jnp.ones((1, capacity, 1), F32)
    rows_in = pick_rows(slots, ones, *(rows.reshape(blocks) for rows in two_halves))[0]
    gate_e, up_e, acted_e, made = expert_forward(rows_in, gateup_w, down_w)
    two_halves, (made, *fetched_two[:1]) = after(two_halves, (made, *fetched_two[:1]))

    gate_sw, up_sw = shared_gateup[:, 0, :], shared_gateup[:, 1, :]
    gate_s = [dot(rows, gate_sw, ((1,), (0,))) for rows in two_halves]
    up_s = [dot(rows, up_sw, ((1,), (0,))) for rows in two_halves]
    acted_s = [(jax.nn.silu(g) * u).astype(BF) for g, u in zip(gate_s, up_s)]
    (acted_s[1],), fetched_two[1:2] = after((acted_s[1],), fetched_two[1:2])
    halves = (slice(0, lower_rows), slice(lower_rows, None))

    def ffn_part(side):
        rows = halves[side]
        shared = dot(acted_s[side], shared_down, ((1,), (0,)))
        routed = dot(pick[:, rows], made, ((0,), (0,)))
        return (steered[side][1] * shared + share[rows, None] * routed).astype(BF)

    ffn_upper = ffn_part(1)
    ffn_lower = ffn_part(0)
    (ffn_lower,), fetched_two[2:] = after((ffn_lower,), fetched_two[2:])
    output = middle + sum_rows(ffn_upper, ffn_lower)[0]
    error = (output - teacher.astype(F32)) * local_valid[:, None]
    squares = jnp.sum(error * error)
    count = jnp.sum(seq_lengths).astype(F32)

    if wide:
        others = dp_size - 1
        sides = (me % 2) ^ jnp.arange(2, dtype=jnp.int32)
        in_order = (2 * jnp.arange(sp_size // 2, dtype=jnp.int32)[None, :] + sides[:, None]).reshape(-1)
        same_place = (in_order[:, None] ^ me) == jnp.array(ORDER, jnp.int32)[None, :]
        in_order = jnp.argmax(same_place, axis=1)
        far_slots = slots_of(masks[:, 1:].transpose(1, 0, 2).reshape(others, total_rows))
        sp_slots = far_slots.reshape(others, sp_size, tok_rows)[:, in_order].reshape(others, total_rows)

        def share_far(*rows_far):
            far_probs = [steer_rows(rows.reshape(-1, width))[0] for rows in rows_far]
            share = jnp.concatenate([jnp.sum(p * is_me[None, :], axis=1) for p in far_probs], 0)
            share = share.reshape(sp_size, others, tok_rows).transpose(1, 0, 2).reshape(others, 1, total_rows)
            share = jnp.where(sp_slots[:, None, :] == slot_range[None, :, None], share, 0.0)
            return jnp.sum(share, axis=2, keepdims=True)

    error_low = error.astype(BF)
    fetched_error = fetch_groups(error_low, False) if wide else []
    *error_halves, _, fetched_error[:1] = gather_rows(error_low, None, fetched_error[:1])
    if wide:
        fetched_two, _ = after(fetched_two, (output,))
        two_side = gather_side(jnp.stack(fetched_two, 0))
    grad_made = pick_rows(slots, share_rows[None], *(rows.reshape(blocks) for rows in error_halves))[0]
    grad_gate_e, grad_up_e, back_e, gain_rows = expert_back(
        grad_made, gate_e, up_e, acted_e, gateup_w, down_w
    )
    error_halves, (back_e, *fetched_error[1:2]) = after(error_halves, (back_e, *fetched_error[1:2]))
    grad_shared = [(s[1] * rows.astype(F32)).astype(BF) for s, rows in zip(steered, error_halves)]
    joined = lambda sides: jnp.concatenate(sides, 0)
    grad_act_s = [dot(g, shared_down, ((1,), (1,))) for g in grad_shared]
    grad_gate_s = [(g * u * silu_slope(v)).astype(BF) for g, u, v in zip(grad_act_s, up_s, gate_s)]
    grad_up_s = [(g * jax.nn.silu(v)).astype(BF) for g, v in zip(grad_act_s, gate_s)]
    own_act, own_grad = joined(acted_s), joined(grad_shared)
    down_term = dot(own_act, own_grad, ((0,), (0,)), BF)
    grad_up_s, (down_term, *fetched_error[2:]) = after(grad_up_s, (down_term, *fetched_error[2:]))
    if wide:
        far_own = jnp.stack(fetched_error, 0)
        far_half = tok_rows // 2
        far_x, far_y = swap(far_own, 2), swap(far_own, 4)
    two_all = joined(two_halves)
    mid_term = dot(two_all, jnp.concatenate([joined(grad_gate_s), joined(grad_up_s)], 1), ((0,), (0,)), BF)
    down_shared = sum_groups(down_term, 1)
    mid_shared = sum_groups(mid_term, 0)
    if wide:
        (back_e, far_own), _ = after((back_e, far_own), (mid_term,))
    switch_part = jnp.concatenate(
        [jnp.sum(a.astype(F32) * g, axis=1) for a, g in zip(acted_s, grad_act_s)], 0
    )

    def back_part(side):
        return (
            dot(grad_gate_s[side], gate_sw, ((1,), (1,)))
            + dot(grad_up_s[side], up_sw, ((1,), (1,)))
            + dot(pick[:, halves[side]], back_e, ((0,), (0,)))
        ).astype(BF)

    back_upper = back_part(1)
    if wide:
        (back_e,), (far_x, far_y, _) = after((back_e,), (far_x, far_y, back_upper))
        far_diag = jnp.concatenate([swap(far_y[:, :far_half], 2), swap(far_x[:, far_half:], 4)], 1)
    back_lower = back_part(0)
    gain_tokens = jnp.sum(pick.astype(F32) * gain_rows, axis=0)
    scalars = jnp.concatenate(
        [gain_tokens[None, :] * is_me[:, None], switch_part[None, :], jnp.zeros((7, total_rows), F32)], axis=0
    )
    scalars, _ = sum_small(scalars.reshape(16, sp_size, tok_rows).transpose(1, 0, 2), jnp.zeros((1, 16, tok_rows), F32))
    gains, switch_sum = scalars[:experts].T, scalars[experts]
    my_probs, my_switch = probs[:tok_rows], switch[:tok_rows, 0]
    grad_switch = switch_sum * (1.0 - my_switch)
    grad_logits = gains - my_probs * jnp.sum(gains, axis=1, keepdims=True)
    steer = jnp.concatenate([grad_logits, grad_switch[:, None]], axis=1)
    if wide:
        (back_lower,), (far_diag,) = after((back_lower,), (far_diag,))
        error_far = jnp.stack([far_own, far_x, far_y, far_diag], 0)
        error_far = (error_far, swap(error_far, 1))
        two_far = (two_side, swap(two_side, 1))
    far_task = None
    if wide:

        def make_far(lower, upper, *rows_far):
            share = share_far(*rows_far)
            return pick_rows(far_slots, share, lower, upper).reshape(-1, width), *rows_far

        far_task = (make_far, *error_far, *two_far)
    (back_lower,), (down_shared,) = after((back_lower,), (down_shared,))
    summed, far_work = sum_rows(back_upper, back_lower, far_task)
    grad_normed = summed + jnp.einsum(
        "te,de->td", steer, heads_in.astype(F32), precision=HIGH
    )
    steer_term = jnp.einsum("te,td->ed", steer, normed_two.astype(F32), precision=HIGH)
    grad_middle_n, ffnnorm_term = norm_back(middle, inverse_two, gain_two, grad_normed)
    grad_middle = error + grad_middle_n

    far_task = None
    if wide:
        far_made, *two_far = far_work
        ones_far = jnp.ones((others, capacity, 1), F32)
        far_task = (lambda *rows: (pick_rows(sp_slots, ones_far, *rows).reshape(-1, width),), *two_far)
    *attn_halves, far_work, _ = gather_rows(grad_middle.astype(BF), far_task)
    grad_mixed = joined([dot(rows, out_proj, ((1,), (1,)), BF) for rows in attn_halves])
    grad_q, grad_k, grad_v = attend_back(
        queries, key_rows, values, allowed, totals, grad_mixed
    )
    grad_proj = (
        rotate_back(grad_q.astype(F32), cosine, sine_table).astype(BF),
        rotate_back(grad_k.astype(F32), cosine, sine_table).astype(BF),
        grad_v,
    )

    def input_part(rows):
        return sum(dot(grad_proj[j][rows], qkv_proj[j], ((1,), (1,))) for j in range(3)).astype(BF)

    input_upper = input_part(halves[1])
    input_lower = input_part(halves[0])
    outproj_term = dot(mixed, joined(attn_halves), ((0,), (0,)), BF)
    qkv_terms = jnp.stack([dot(normed_all, g, ((0,), (0,)), BF) for g in grad_proj], 0)
    bias_term = jnp.stack([jnp.sum(g.astype(F32), axis=0) for g in grad_proj], 0)
    if wide:
        (far_in,) = far_work
        grad_normed_one, far_work = sum_rows(
            input_upper,
            input_lower,
            (lambda made, *_: (made, *expert_far(far_in, made, gateup_w, down_w)), far_made, outproj_term, qkv_terms, mid_shared),
        )
        far_made, far_act, far_gate, far_up = far_work
        gateup_expert, down_expert = expert_grads_of(
            (rows_in, grad_made, acted_e, grad_gate_e, grad_up_e),
            (far_in, far_made, far_act, far_gate, far_up),
        )
    else:
        grad_normed_one, _ = sum_rows(input_upper, input_lower)
        gateup_expert = jnp.stack(
            [
                sum_groups(dot(rows_in, grad_gate_e, ((0,), (0,)), BF), 0),
                sum_groups(dot(rows_in, grad_up_e, ((0,), (0,)), BF), 0),
            ],
            axis=1,
        )
        down_expert = sum_groups(dot(acted_e, grad_made, ((0,), (0,)), BF), 1)
    grad_input_n, attnnorm_term = norm_back(inputs, inverse_one, gain_one, grad_normed_one)
    hidden_grad = grad_middle + grad_input_n
    outproj_grad = sum_groups(outproj_term, 1)
    qkvproj_grad = sum_groups(qkv_terms, 1)

    small = jnp.concatenate([attnnorm_term[None], ffnnorm_term[None], steer_term], axis=0)
    kinds = small.shape[0]
    cell = width // (dp_size * sp_size)
    small = small.reshape(kinds, dp_size, sp_size, cell).transpose(2, 1, 0, 3)[owners]
    small = small.reshape(sp_size, dp_size, kinds * cell)
    small, squares = sum_small(small, jnp.full((1,) + small.shape[1:], squares, F32))
    pairs = bias_term.reshape(-1, HD)
    bias_cells = pairs.reshape(pairs.shape[0], dp_size, -1).transpose(1, 0, 2).reshape(dp_size, -1)
    small = jnp.concatenate([small, bias_cells], axis=1)
    small, squares = shift_groups(small, jnp.full(small.shape[1:], squares[0, 0], F32))
    loss_value = squares[0] / (2.0 * count * D)
    gains_out = small[: kinds * cell].reshape(kinds, cell)
    qkvbias_grad = small[kinds * cell :].reshape(3, -1, HD // dp_size)
    return (
        output,
        loss_value,
        hidden_grad,
        gains_out[0],
        qkvproj_grad,
        qkvbias_grad,
        outproj_grad,
        gains_out[1],
        gains_out[2 : 2 + experts].T,
        mid_shared.reshape(-1, 2, gate_sw.shape[1]),
        down_shared,
        gains_out[2 + experts],
        gateup_expert[None],
        down_expert[None],
    )


def solution(mesh):
    in_specs = (
        P(("dp", "sp"), None),
        P(("dp", "sp"), None),
        P(),
        P(("dp", "sp"), None),
        P(),
        P(None, None, "sp"),
        P(None, "sp", None),
        P("sp", None),
        P(),
        P(),
        P(None, None, "sp"),
        P("sp", None),
        P(),
        P("sp", None, None, None),
        P("sp", None, None),
    )
    out_specs = (
        P(("dp", "sp"), None),
        P(),
        P(("dp", "sp"), None),
        P(("dp", "sp")),
        P(None, "dp", "sp"),
        P(None, "sp", "dp"),
        P("sp", "dp"),
        P(("dp", "sp")),
        P(("dp", "sp"), None),
        P("dp", None, "sp"),
        P("sp", "dp"),
        P(("dp", "sp")),
        P("sp", "dp", None, None),
        P("sp", None, "dp"),
    )
    return jax.shard_map(
        on_device, mesh=mesh, in_specs=in_specs, out_specs=out_specs, check_vma=False
    )
```

```python
import jax
import jax.numpy as jnp
from jax import lax
from jax.experimental import pallas as pl
from jax.experimental.pallas import tpu as pltpu
from jax.sharding import PartitionSpec as P

D = 2048
HD = 128
BLK = 128
MAXSEQ = 8

EPS = 1e-06
THETA = 1000000.0
FLOOR = -1e30
HIGH = lax.Precision.HIGHEST
BF = jnp.bfloat16
F32 = jnp.float32

ORDER = (0, 2, 4, 6, 1, 3, 5, 7)


def after(values, work):
    values, work = tuple(values), tuple(work)
    if not work or not values:
        return values, work
    tied = lax.optimization_barrier((*values, *work))
    return tied[: len(values)], tied[len(values) :]


def between(first, last, task):
    if task is None:
        return tuple(last), ()
    function, *inputs = task
    inputs, _ = after(inputs, first)
    return after(last, function(*inputs))


def dot(left, right, dims, dtype=F32):
    return lax.dot_general(left, right, (dims, ((), ())), preferred_element_type=F32).astype(dtype)


def swap(values, distance):
    return lax.ppermute(values, "sp", [(i, i ^ distance) for i in range(8)])


def gather_rows(own, task=None, first=()):
    half = own.shape[0] // 2
    over_x, over_y = swap(own, 2), swap(own, 4)
    (over_x, over_y), work = between((own,), (over_x, over_y), task)
    (over_x, over_y), first = after((over_x, over_y), first)
    far_top, far_bottom = swap(over_y[:half], 2), swap(over_x[half:], 4)
    lower = jnp.concatenate([own, over_x, over_y, far_top, far_bottom], 0)
    return lower, swap(lower, 1), work, first


def gather_side(own):
    return lax.all_gather(own, "sp", axis_index_groups=[[0, 2, 4, 6], [1, 3, 5, 7]])


def gather_small(own):
    held = own[None]
    for distance in (2, 4, 1):
        held = jnp.concatenate([held, swap(held, distance)], 0)
    return held


def sum_small(parts, total):
    for distance in (1, 4, 2):
        keep = parts.shape[0] // 2
        got = swap(jnp.concatenate([parts[keep:], total], 0), distance)
        parts, total = parts[:keep] + got[:keep], total + got[keep:]
    return parts[0], total[0]


def sum_rows(upper, lower, task=None):
    rows = lower.shape[0] // 4
    half = rows // 2
    got = swap(upper, 1)
    chip = lower.astype(F32) + got.astype(F32)
    low = chip.astype(BF)
    own, over_x, over_y, far = (slice(k * rows, (k + 1) * rows) for k in range(4))
    low_x, low_y, low_far = low[over_x], low[over_y], low[far]
    from_x = swap(jnp.concatenate([low_far[:half], low_x[:half]], 0), 2)
    from_y = swap(jnp.concatenate([low_far[half:], low_y[half:]], 0), 4)
    (from_x, from_y), work = between((low,), (from_x, from_y), task)
    pass_y = (chip[over_y][:half] + from_x[:half].astype(F32)).astype(BF)
    pass_x = (chip[over_x][half:] + from_y[:half].astype(F32)).astype(BF)
    last_y, last_x = swap(pass_y, 4), swap(pass_x, 2)
    mine = chip[own]
    top = mine[:half] + from_x[half:].astype(F32) + last_y.astype(F32)
    bottom = mine[half:] + from_y[half:].astype(F32) + last_x.astype(F32)
    return jnp.concatenate([top, bottom], 0), work


def sum_groups(grads, dim):
    return lax.psum_scatter(grads, "dp", scatter_dimension=dim, tiled=True).astype(F32)


def shift_groups(blocks, total):
    size = lax.axis_size("dp")
    me = lax.axis_index("dp")
    pick = lambda k: lax.dynamic_index_in_dim(blocks, (me + k) % size, 0, keepdims=False)
    mine = jnp.stack([pick(0), total])
    summed = mine[0]
    totals = jnp.zeros((size,) + total.shape, total.dtype).at[me].set(total)
    for k in range(1, size):
        got = lax.ppermute(jnp.stack([pick(k), total]), "dp", [(i, (i + k) % size) for i in range(size)])
        summed = summed + got[0]
        totals = totals.at[(me - k) % size].set(got[1])
    return summed, jnp.sum(totals, axis=0)


def fetch_groups(own, chained=True):
    size = lax.axis_size("dp")
    got = []
    for k in range(1, size):
        moved, _ = after((own,), got[-1:] if chained else ())
        got.append(lax.ppermute(moved[0], "dp", [((i + k) % size, i) for i in range(size)]))
    return got


def own_columns(values, axis):
    share = values.shape[axis] // lax.axis_size("dp")
    return lax.dynamic_slice_in_dim(values, lax.axis_index("dp") * share, share, axis)


def slots_of(mask):
    return jnp.where(mask, jnp.cumsum(mask.astype(jnp.int32), axis=-1) - 1, -1)


def local_call(kernel, name, flops, **spec):
    return pl.pallas_call(
        kernel,
        name=name,
        cost_estimate=pl.CostEstimate(flops=flops, bytes_accessed=flops // 300, transcendentals=0),
        compiler_params=pltpu.CompilerParams(vmem_limit_bytes=56 * 2**20),
        **spec,
    )


def pick_kernel(slot_ref, scale_ref, lower_ref, upper_ref, out_ref):
    capacity, columns = out_ref.shape
    total = slot_ref.shape[-1]
    chosen = (slot_ref[...] == lax.broadcasted_iota(jnp.int32, (capacity, total), 0)).astype(F32).astype(BF)
    half = total // 2
    rows = jnp.dot(chosen[:, :half], lower_ref[...].reshape(half, columns), preferred_element_type=F32)
    rows += jnp.dot(chosen[:, half:], upper_ref[...].reshape(half, columns), preferred_element_type=F32)
    out_ref[...] = (rows * scale_ref[...]).astype(BF)


def pick_rows(slots, scale, lower, upper):
    blocks, groups, count, width = lower.shape
    total = 2 * blocks * count
    capacity = scale.shape[1]
    tile = 2048
    rows = pl.BlockSpec((blocks, None, count, tile), lambda g, j: (0, g, 0, j))
    return local_call(
        pick_kernel,
        "pick_rows",
        2 * groups * capacity * total * width,
        grid=(groups, width // tile),
        in_specs=[
            pl.BlockSpec((None, 1, total), lambda g, j: (g, 0, 0)),
            pl.BlockSpec((None, capacity, 1), lambda g, j: (g, 0, 0)),
            rows,
            rows,
        ],
        out_specs=pl.BlockSpec((None, capacity, tile), lambda g, j: (g, 0, j)),
        out_shape=jax.ShapeDtypeStruct((groups, capacity, width), BF),
    )(slots[:, None, :], scale, lower, upper)


def dot_nn(left, right):
    return lax.dot_general(left, right, (((1,), (0,)), ((), ())), preferred_element_type=F32)


def dot_nt(left, right):
    return lax.dot_general(left, right, (((1,), (1,)), ((), ())), preferred_element_type=F32)


def dot_tn(left, right):
    return lax.dot_general(left, right, (((0,), (0,)), ((), ())), preferred_element_type=F32)


def expert_kernel(x_ref, gateup_w, down_w, gate_ref, up_ref, act_ref, made_ref):
    x = x_ref[...]
    gate, up = dot_nn(x, gateup_w[0]), dot_nn(x, gateup_w[1])
    gate_ref[...], up_ref[...] = gate, up
    act = (gate * jax.nn.sigmoid(gate) * up).astype(BF)
    act_ref[...] = act
    made_ref[...] = dot_nn(act, down_w[...]).astype(BF)


def row_spec(block, columns):
    return pl.BlockSpec((block, columns), lambda i: (i, 0))


def held_spec(array):
    return pl.BlockSpec(array.shape, lambda i: (0,) * array.ndim, pipeline_mode=pl.Buffered(1))


def row_block(count):
    return max(b for b in range(16, min(count, 288) + 1, 16) if count % b == 0)


def expert_forward(x, gateup_w, down_w):
    count, width = x.shape
    hidden = gateup_w.shape[2]
    block = row_block(count)
    wide_shape = lambda dtype: jax.ShapeDtypeStruct((count, hidden), dtype)
    return local_call(
        expert_kernel,
        "expert_forward",
        6 * count * width * hidden,
        grid=(count // block,),
        in_specs=[row_spec(block, width), held_spec(gateup_w), held_spec(down_w)],
        out_specs=[row_spec(block, hidden)] * 3 + [row_spec(block, width)],
        out_shape=[wide_shape(F32), wide_shape(F32), wide_shape(BF), jax.ShapeDtypeStruct((count, width), BF)],
    )(x, gateup_w, down_w)


def middle_grads(gate, up, grad):
    sig = jax.nn.sigmoid(gate)
    slope = sig * (1.0 + gate * (1.0 - sig))
    return (grad * up * slope).astype(BF), (grad * (gate * sig)).astype(BF)


def expert_back_kernel(g_ref, gate_ref, up_ref, act_ref, gateup_w, down_w, gg_ref, gu_ref, back_ref, gain_ref):
    grad = dot_nt(g_ref[...], down_w[...])
    gain_ref[...] = jnp.sum(act_ref[...].astype(F32) * grad, axis=1, keepdims=True)
    grad_gate, grad_up = middle_grads(gate_ref[...], up_ref[...], grad)
    gg_ref[...], gu_ref[...] = grad_gate, grad_up
    back_ref[...] = (dot_nt(grad_gate, gateup_w[0]) + dot_nt(grad_up, gateup_w[1])).astype(BF)


def expert_back(g, gate, up, act, gateup_w, down_w):
    count, width = g.shape
    hidden = gateup_w.shape[2]
    block = row_block(count)
    rows, mids = row_spec(block, width), row_spec(block, hidden)
    return local_call(
        expert_back_kernel,
        "expert_back",
        6 * count * width * hidden,
        grid=(count // block,),
        in_specs=[rows, mids, mids, mids, held_spec(gateup_w), held_spec(down_w)],
        out_specs=[mids, mids, rows, row_spec(block, 1)],
        out_shape=[jax.ShapeDtypeStruct((count, hidden), BF)] * 2
        + [jax.ShapeDtypeStruct((count, width), BF), jax.ShapeDtypeStruct((count, 1), F32)],
    )(g, gate, up, act, gateup_w, down_w)


def expert_far_kernel(x_ref, g_ref, gateup_w, down_w, act_ref, gg_ref, gu_ref):
    x = x_ref[...]
    gate, up = dot_nn(x, gateup_w[0]), dot_nn(x, gateup_w[1])
    act_ref[...] = (gate * jax.nn.sigmoid(gate) * up).astype(BF)
    gg_ref[...], gu_ref[...] = middle_grads(gate, up, dot_nt(g_ref[...], down_w[...]))


def expert_far(x, g, gateup_w, down_w):
    count, width = x.shape
    hidden = gateup_w.shape[2]
    block = row_block(count)
    rows, mids = row_spec(block, width), row_spec(block, hidden)
    return local_call(
        expert_far_kernel,
        "expert_far",
        6 * count * width * hidden,
        grid=(count // block,),
        in_specs=[rows, rows, held_spec(gateup_w), held_spec(down_w)],
        out_specs=[mids] * 3,
        out_shape=[jax.ShapeDtypeStruct((count, hidden), BF)] * 3,
    )(x, g, gateup_w, down_w)


def expert_grad_kernel(_, x, g, act, gg, gu, far_x, far_g, far_act, far_gg, far_gu, gateup_ref, down_ref, acc_g, acc_u):
    step = pl.program_id(0)

    @pl.when(step == 0)
    def _():
        rows = x[...]
        acc_g[...] = dot_tn(rows, gg[...])
        acc_u[...] = dot_tn(rows, gu[...])
        down_ref[...] = dot_tn(act[...], g[...])

    @pl.when(step > 0)
    def _():
        rows = far_x[...]
        acc_g[...] += dot_tn(rows, far_gg[...])
        acc_u[...] += dot_tn(rows, far_gu[...])
        down_ref[...] += dot_tn(far_act[...], far_g[...])

    @pl.when(step == pl.num_programs(0) - 1)
    def _():
        gateup_ref[:, 0, :] = acc_g[...]
        gateup_ref[:, 1, :] = acc_u[...]


def expert_grads_of(own, far):
    count, width = own[0].shape
    hidden = own[2].shape[1]
    share = width // lax.axis_size("dp")
    steps = 1 + far[0].shape[0] // count
    held = lambda i, d: (0, 0)
    near_rows = pl.BlockSpec((count, share), lambda i, d: (0, d[0]))
    near_mid = pl.BlockSpec((count, hidden), held)
    far_rows = pl.BlockSpec((count, share), lambda i, d: (jnp.maximum(i - 1, 0), d[0]))
    far_mid = pl.BlockSpec((count, hidden), lambda i, d: (jnp.maximum(i - 1, 0), 0))
    return local_call(
        expert_grad_kernel,
        "expert_grads",
        6 * count * steps * share * hidden,
        grid_spec=pltpu.PrefetchScalarGridSpec(
            num_scalar_prefetch=1,
            grid=(steps,),
            in_specs=[near_rows, near_rows] + [near_mid] * 3 + [far_rows, far_rows] + [far_mid] * 3,
            out_specs=[
                pl.BlockSpec((share, 2, hidden), lambda i, d: (0, 0, 0)),
                pl.BlockSpec((hidden, share), held),
            ],
            scratch_shapes=[pltpu.VMEM((share, hidden), F32)] * 2,
        ),
        out_shape=[
            jax.ShapeDtypeStruct((share, 2, hidden), F32),
            jax.ShapeDtypeStruct((hidden, share), F32),
        ],
    )(lax.axis_index("dp").reshape(1), *own, *far)


def layout(length_row, place):
    blocks = (length_row + BLK - 1) // BLK
    ends = jnp.cumsum(blocks)
    starts = ends - blocks
    which = jnp.sum((place[:, None] // BLK >= ends[None, :]).astype(jnp.int32), axis=1)
    member = which[:, None] == jnp.arange(length_row.shape[0], dtype=jnp.int32)[None, :]
    opening = jnp.sum(jnp.where(member, starts[None, :], 0), axis=1)
    seq_len = jnp.sum(jnp.where(member, length_row[None, :], 0), axis=1)
    position = place - opening * BLK
    return (which, position, position < seq_len)


def rope_tables(position):
    half_dim = HD // 2
    freq = THETA ** (-2.0 * jnp.arange(half_dim, dtype=F32) / HD)
    angle = position.astype(F32)[:, None] * freq[None, :]
    return (
        jnp.concatenate([jnp.cos(angle), jnp.cos(angle)], -1),
        jnp.concatenate([jnp.sin(angle), jnp.sin(angle)], -1),
    )


def rotate(flat_rows, cosine, sine_table):
    count = flat_rows.shape[0]
    shaped = flat_rows.reshape(count, -1, HD)
    half_dim = HD // 2
    turned = jnp.concatenate([-shaped[..., half_dim:], shaped[..., :half_dim]], -1)
    return (shaped * cosine[:, None, :] + turned * sine_table[:, None, :]).reshape(count, -1)


def rotate_back(flat_rows, cosine, sine_table):
    count = flat_rows.shape[0]
    shaped = flat_rows.reshape(count, -1, HD)
    half_dim = HD // 2
    sined = shaped * sine_table[:, None, :]
    turned = jnp.concatenate([sined[..., half_dim:], -sined[..., :half_dim]], -1)
    return (shaped * cosine[:, None, :] + turned).reshape(count, -1)


def normalize(values, gain_vec):
    inverse = lax.rsqrt(jnp.mean(values * values, axis=-1, keepdims=True) + EPS)
    return (values * inverse * gain_vec, inverse)


def norm_back(values, inverse, gain_vec, gradient):
    scaled = values * inverse
    gain_term = jnp.sum(gradient * scaled, axis=0)
    grad_scaled = gradient * gain_vec
    back = inverse * (grad_scaled - scaled * jnp.mean(grad_scaled * scaled, axis=-1, keepdims=True))
    return (back, gain_term)


def silu_slope(values):
    sig = jax.nn.sigmoid(values)
    return sig * (1.0 + values * (1.0 - sig))


def scores_of(queries, key_rows, allowed):
    scores = dot(queries, key_rows, ((1,), (1,))) * HD ** (-0.5)
    return jnp.where(allowed, scores, FLOOR)


def attend_forward(queries, key_rows, values, allowed):
    pieces, totals = [], []
    for start in range(0, queries.shape[1], HD):
        head = slice(start, start + HD)
        scores = scores_of(queries[:, head], key_rows[:, head], allowed)
        peak = jnp.max(scores, axis=-1, keepdims=True)
        expon = jnp.exp(scores - peak)
        summed = jnp.sum(expon, axis=-1, keepdims=True)
        weights = (expon / summed).astype(BF)
        pieces.append(dot(weights, values[:, head], ((1,), (0,)), BF))
        totals.append(peak + jnp.log(summed))
    return (jnp.concatenate(pieces, 1), totals)


def attend_back(queries, key_rows, values, allowed, totals, grad_mixed):
    scale = HD ** (-0.5)
    grads = ([], [], [])
    for start, total in zip(range(0, queries.shape[1], HD), totals):
        head = slice(start, start + HD)
        block_q, block_k, block_g = queries[:, head], key_rows[:, head], grad_mixed[:, head]
        probs = jnp.exp(scores_of(block_q, block_k, allowed) - total)
        grad_p = dot(block_g, values[:, head], ((1,), (1,)))
        grad_s = (probs * (grad_p - jnp.sum(probs * grad_p, axis=-1, keepdims=True))).astype(BF)
        grads[0].append((dot(grad_s, block_k, ((1,), (0,))) * scale).astype(BF))
        grads[1].append((dot(grad_s, block_q, ((0,), (0,))) * scale).astype(BF))
        grads[2].append(dot(probs.astype(BF), block_g, ((0,), (0,)), BF))
    return tuple(jnp.concatenate(g, 1) for g in grads)


def on_device(
    hidden_in,
    teacher,
    seq_lengths,
    routes,
    attn_norm,
    qkv_proj,
    qkv_bias,
    out_proj,
    ffn_norm,
    router,
    shared_gateup,
    shared_down,
    shared_switch,
    expert_gateup,
    expert_down,
):
    tok_rows, width = hidden_in.shape
    sp_size = lax.axis_size("sp")
    dp_size = lax.axis_size("dp")
    me = lax.axis_index("sp")
    total_rows = tok_rows * sp_size
    lower_rows = total_rows // 2
    experts = router.shape[1]
    top_k = routes.shape[1]
    capacity = sp_size * min(tok_rows, 9 * tok_rows * top_k // (8 * experts))

    inputs = hidden_in.astype(F32)
    gain_one = attn_norm.astype(F32)
    normed_f, inverse_one = normalize(inputs, gain_one)
    *normed_halves, (gateup_w,), _ = gather_rows(
        normed_f.astype(BF), (lambda w: (w.transpose(1, 0, 2),), expert_gateup[0])
    )
    wide = dp_size <= 4

    owners = me ^ jnp.array(ORDER, jnp.int32)
    place = (owners[:, None] * tok_rows + jnp.arange(tok_rows, dtype=jnp.int32)[None, :]).reshape(-1)
    length_row = lax.dynamic_index_in_dim(seq_lengths, lax.axis_index("dp"), 0, keepdims=False)
    segment, position, is_valid = layout(length_row, place)
    cosine, sine_table = rope_tables(position)
    local_valid = is_valid[:tok_rows].astype(F32)
    allowed = (
        (segment[:, None] == segment[None, :])
        & (position[None, :] <= position[:, None])
        & is_valid[None, :]
    )

    bias = qkv_bias.reshape(3, 1, -1).astype(F32)
    normed_all = jnp.concatenate(normed_halves, 0)
    projected = [dot(normed_all, qkv_proj[j], ((1,), (0,))) + bias[j] for j in range(3)]
    queries = rotate(projected[0], cosine, sine_table).astype(BF)
    key_rows = rotate(projected[1], cosine, sine_table).astype(BF)
    values = projected[2].astype(BF)
    mixed, totals = attend_forward(queries, key_rows, values, allowed)
    upper = dot(mixed[lower_rows:], out_proj, ((1,), (0,)), BF)
    lower = dot(mixed[:lower_rows], out_proj, ((1,), (0,)), BF)

    (route_own,), _ = after((routes.T[None],), (mixed,))
    if wide:
        route_own = jnp.concatenate([route_own] + fetch_groups(route_own, False), 0)
    route_all = gather_small(route_own.reshape(-1, tok_rows))
    route_all = route_all.reshape(sp_size, -1, top_k, tok_rows)
    masks = jnp.any(route_all == me, axis=2)
    mask = masks[:, 0].reshape(total_rows)
    slots = slots_of(mask)[None]
    slot_range = jnp.arange(capacity, dtype=jnp.int32)
    pick = (slots[0][None, :] == slot_range[:, None]).astype(BF)

    middle = inputs + sum_rows(upper, lower)[0]

    gain_two = ffn_norm.astype(F32)
    normed_two_f, inverse_two = normalize(middle, gain_two)
    normed_two = normed_two_f.astype(BF)
    fetched_two = fetch_groups(normed_two, False) if wide else []
    *two_halves, _, (pick, slots) = gather_rows(normed_two, None, (pick, slots))

    heads_in = jnp.concatenate([router, shared_switch[:, None]], axis=1)
    is_me = (jnp.arange(experts) == me).astype(F32)

    def steer_rows(rows):
        logits = dot(rows, heads_in, ((1,), (0,)))
        return jax.nn.softmax(logits[:, :experts], axis=-1), jax.nn.sigmoid(logits[:, experts:])

    steered = [steer_rows(rows) for rows in two_halves]
    probs, switch = (jnp.concatenate(both, 0) for both in zip(*steered))
    share = jnp.sum(probs * is_me[None, :], axis=1) * mask.astype(F32)
    share_rows = jnp.sum(pick.astype(F32) * share[None, :], axis=1, keepdims=True)

    down_w = expert_down[0]
    blocks = (sp_size // 2, 1, tok_rows, width)
    ones = jnp.ones((1, capacity, 1), F32)
    rows_in = pick_rows(slots, ones, *(rows.reshape(blocks) for rows in two_halves))[0]
    gate_e, up_e, acted_e, made = expert_forward(rows_in, gateup_w, down_w)
    two_halves, (made, *fetched_two[:1]) = after(two_halves, (made, *fetched_two[:1]))

    gate_sw, up_sw = shared_gateup[:, 0, :], shared_gateup[:, 1, :]
    gate_s = [dot(rows, gate_sw, ((1,), (0,))) for rows in two_halves]
    up_s = [dot(rows, up_sw, ((1,), (0,))) for rows in two_halves]
    acted_s = [(jax.nn.silu(g) * u).astype(BF) for g, u in zip(gate_s, up_s)]
    (acted_s[1],), fetched_two[1:2] = after((acted_s[1],), fetched_two[1:2])
    halves = (slice(0, lower_rows), slice(lower_rows, None))

    def ffn_part(side):
        rows = halves[side]
        shared = dot(acted_s[side], shared_down, ((1,), (0,)))
        routed = dot(pick[:, rows], made, ((0,), (0,)))
        return (steered[side][1] * shared + share[rows, None] * routed).astype(BF)

    ffn_upper = ffn_part(1)
    ffn_lower = ffn_part(0)
    (ffn_lower,), fetched_two[2:] = after((ffn_lower,), fetched_two[2:])
    output = middle + sum_rows(ffn_upper, ffn_lower)[0]
    error = (output - teacher.astype(F32)) * local_valid[:, None]
    squares = jnp.sum(error * error)
    count = jnp.sum(seq_lengths).astype(F32)

    if wide:
        others = dp_size - 1
        sides = (me % 2) ^ jnp.arange(2, dtype=jnp.int32)
        in_order = (2 * jnp.arange(sp_size // 2, dtype=jnp.int32)[None, :] + sides[:, None]).reshape(-1)
        same_place = (in_order[:, None] ^ me) == jnp.array(ORDER, jnp.int32)[None, :]
        in_order = jnp.argmax(same_place, axis=1)
        far_slots = slots_of(masks[:, 1:].transpose(1, 0, 2).reshape(others, total_rows))
        sp_slots = far_slots.reshape(others, sp_size, tok_rows)[:, in_order].reshape(others, total_rows)

        def share_far(*rows_far):
            far_probs = [steer_rows(rows.reshape(-1, width))[0] for rows in rows_far]
            share = jnp.concatenate([jnp.sum(p * is_me[None, :], axis=1) for p in far_probs], 0)
            share = share.reshape(sp_size, others, tok_rows).transpose(1, 0, 2).reshape(others, 1, total_rows)
            share = jnp.where(sp_slots[:, None, :] == slot_range[None, :, None], share, 0.0)
            return jnp.sum(share, axis=2, keepdims=True)

    error_low = error.astype(BF)
    fetched_error = fetch_groups(error_low, False) if wide else []
    *error_halves, _, fetched_error[:1] = gather_rows(error_low, None, fetched_error[:1])
    if wide:
        fetched_two, _ = after(fetched_two, (output,))
        two_side = gather_side(jnp.stack(fetched_two, 0))
    grad_made = pick_rows(slots, share_rows[None], *(rows.reshape(blocks) for rows in error_halves))[0]
    grad_gate_e, grad_up_e, back_e, gain_rows = expert_back(
        grad_made, gate_e, up_e, acted_e, gateup_w, down_w
    )
    error_halves, (back_e, *fetched_error[1:2]) = after(error_halves, (back_e, *fetched_error[1:2]))
    grad_shared = [(s[1] * rows.astype(F32)).astype(BF) for s, rows in zip(steered, error_halves)]
    joined = lambda sides: jnp.concatenate(sides, 0)
    grad_act_s = [dot(g, shared_down, ((1,), (1,))) for g in grad_shared]
    grad_gate_s = [(g * u * silu_slope(v)).astype(BF) for g, u, v in zip(grad_act_s, up_s, gate_s)]
    grad_up_s = [(g * jax.nn.silu(v)).astype(BF) for g, v in zip(grad_act_s, gate_s)]
    own_act, own_grad = joined(acted_s), joined(grad_shared)
    down_term = dot(own_act, own_grad, ((0,), (0,)), BF)
    grad_up_s, (down_term, *fetched_error[2:]) = after(grad_up_s, (down_term, *fetched_error[2:]))
    if wide:
        far_own = jnp.stack(fetched_error, 0)
        far_half = tok_rows // 2
        far_x, far_y = swap(far_own, 2), swap(far_own, 4)
    two_all = joined(two_halves)
    mid_term = dot(two_all, jnp.concatenate([joined(grad_gate_s), joined(grad_up_s)], 1), ((0,), (0,)), BF)
    down_shared = sum_groups(down_term, 1)
    mid_shared = sum_groups(mid_term, 0)
    if wide:
        (back_e, far_own), _ = after((back_e, far_own), (mid_term,))
    switch_part = jnp.concatenate(
        [jnp.sum(a.astype(F32) * g, axis=1) for a, g in zip(acted_s, grad_act_s)], 0
    )

    def back_part(side):
        return (
            dot(grad_gate_s[side], gate_sw, ((1,), (1,)))
            + dot(grad_up_s[side], up_sw, ((1,), (1,)))
            + dot(pick[:, halves[side]], back_e, ((0,), (0,)))
        ).astype(BF)

    back_upper = back_part(1)
    if wide:
        (back_e,), (far_x, far_y, _) = after((back_e,), (far_x, far_y, back_upper))
        far_diag = jnp.concatenate([swap(far_y[:, :far_half], 2), swap(far_x[:, far_half:], 4)], 1)
    back_lower = back_part(0)
    gain_tokens = jnp.sum(pick.astype(F32) * gain_rows, axis=0)
    scalars = jnp.concatenate(
        [gain_tokens[None, :] * is_me[:, None], switch_part[None, :], jnp.zeros((7, total_rows), F32)], axis=0
    )
    scalars, _ = sum_small(scalars.reshape(16, sp_size, tok_rows).transpose(1, 0, 2), jnp.zeros((1, 16, tok_rows), F32))
    gains, switch_sum = scalars[:experts].T, scalars[experts]
    my_probs, my_switch = probs[:tok_rows], switch[:tok_rows, 0]
    grad_switch = switch_sum * (1.0 - my_switch)
    grad_logits = gains - my_probs * jnp.sum(gains, axis=1, keepdims=True)
    steer = jnp.concatenate([grad_logits, grad_switch[:, None]], axis=1)
    if wide:
        error_far = jnp.stack([far_own, far_x, far_y, far_diag], 0)
        error_far = (error_far, swap(error_far, 1))
        two_far = (two_side, swap(two_side, 1))
    far_task = None
    if wide:

        def make_far(lower, upper, *rows_far):
            share = share_far(*rows_far)
            return pick_rows(far_slots, share, lower, upper).reshape(-1, width), *rows_far

        far_task = (make_far, *error_far, *two_far)
    (back_lower,), (down_shared,) = after((back_lower,), (down_shared,))
    summed, far_work = sum_rows(back_upper, back_lower, far_task)
    grad_normed = summed + jnp.einsum(
        "te,de->td", steer, heads_in.astype(F32), precision=HIGH
    )
    steer_term = jnp.einsum("te,td->ed", steer, normed_two.astype(F32), precision=HIGH)
    grad_middle_n, ffnnorm_term = norm_back(middle, inverse_two, gain_two, grad_normed)
    grad_middle = error + grad_middle_n

    far_task = None
    if wide:
        far_made, *two_far = far_work
        ones_far = jnp.ones((others, capacity, 1), F32)
        far_task = (lambda *rows: (pick_rows(sp_slots, ones_far, *rows).reshape(-1, width),), *two_far)
    *attn_halves, far_work, _ = gather_rows(grad_middle.astype(BF), far_task)
    grad_mixed = joined([dot(rows, out_proj, ((1,), (1,)), BF) for rows in attn_halves])
    grad_q, grad_k, grad_v = attend_back(
        queries, key_rows, values, allowed, totals, grad_mixed
    )
    grad_proj = (
        rotate_back(grad_q.astype(F32), cosine, sine_table).astype(BF),
        rotate_back(grad_k.astype(F32), cosine, sine_table).astype(BF),
        grad_v,
    )

    def input_part(rows):
        return sum(dot(grad_proj[j][rows], qkv_proj[j], ((1,), (1,))) for j in range(3)).astype(BF)

    input_upper = input_part(halves[1])
    input_lower = input_part(halves[0])
    outproj_term = dot(mixed, joined(attn_halves), ((0,), (0,)), BF)
    qkv_terms = jnp.stack([dot(normed_all, g, ((0,), (0,)), BF) for g in grad_proj], 0)
    bias_term = jnp.stack([jnp.sum(g.astype(F32), axis=0) for g in grad_proj], 0)
    if wide:
        (far_in,) = far_work
        grad_normed_one, far_work = sum_rows(
            input_upper,
            input_lower,
            (lambda made, *_: (made, *expert_far(far_in, made, gateup_w, down_w)), far_made, outproj_term, qkv_terms, mid_shared),
        )
        far_made, far_act, far_gate, far_up = far_work
        gateup_expert, down_expert = expert_grads_of(
            (rows_in, grad_made, acted_e, grad_gate_e, grad_up_e),
            (far_in, far_made, far_act, far_gate, far_up),
        )
    else:
        grad_normed_one, _ = sum_rows(input_upper, input_lower)
        gateup_expert = jnp.stack(
            [
                sum_groups(dot(rows_in, grad_gate_e, ((0,), (0,)), BF), 0),
                sum_groups(dot(rows_in, grad_up_e, ((0,), (0,)), BF), 0),
            ],
            axis=1,
        )
        down_expert = sum_groups(dot(acted_e, grad_made, ((0,), (0,)), BF), 1)
    grad_input_n, attnnorm_term = norm_back(inputs, inverse_one, gain_one, grad_normed_one)
    hidden_grad = grad_middle + grad_input_n
    outproj_grad = sum_groups(outproj_term, 1)
    qkvproj_grad = sum_groups(qkv_terms, 1)

    small = jnp.concatenate([attnnorm_term[None], ffnnorm_term[None], steer_term], axis=0)
    kinds = small.shape[0]
    cell = width // (dp_size * sp_size)
    small = small.reshape(kinds, dp_size, sp_size, cell).transpose(2, 1, 0, 3)[owners]
    small = small.reshape(sp_size, dp_size, kinds * cell)
    small, squares = sum_small(small, jnp.full((1,) + small.shape[1:], squares, F32))
    pairs = bias_term.reshape(-1, HD)
    bias_cells = pairs.reshape(pairs.shape[0], dp_size, -1).transpose(1, 0, 2).reshape(dp_size, -1)
    small = jnp.concatenate([small, bias_cells], axis=1)
    small, squares = shift_groups(small, jnp.full(small.shape[1:], squares[0, 0], F32))
    loss_value = squares[0] / (2.0 * count * D)
    gains_out = small[: kinds * cell].reshape(kinds, cell)
    qkvbias_grad = small[kinds * cell :].reshape(3, -1, HD // dp_size)
    return (
        output,
        loss_value,
        hidden_grad,
        gains_out[0],
        qkvproj_grad,
        qkvbias_grad,
        outproj_grad,
        gains_out[1],
        gains_out[2 : 2 + experts].T,
        mid_shared.reshape(-1, 2, gate_sw.shape[1]),
        down_shared,
        gains_out[2 + experts],
        gateup_expert[None],
        down_expert[None],
    )


def solution(mesh):
    in_specs = (
        P(("dp", "sp"), None),
        P(("dp", "sp"), None),
        P(),
        P(("dp", "sp"), None),
        P(),
        P(None, None, "sp"),
        P(None, "sp", None),
        P("sp", None),
        P(),
        P(),
        P(None, None, "sp"),
        P("sp", None),
        P(),
        P("sp", None, None, None),
        P("sp", None, None),
    )
    out_specs = (
        P(("dp", "sp"), None),
        P(),
        P(("dp", "sp"), None),
        P(("dp", "sp")),
        P(None, "dp", "sp"),
        P(None, "sp", "dp"),
        P("sp", "dp"),
        P(("dp", "sp")),
        P(("dp", "sp"), None),
        P("dp", None, "sp"),
        P("sp", "dp"),
        P(("dp", "sp")),
        P("sp", "dp", None, None),
        P("sp", None, "dp"),
    )
    return jax.shard_map(
        on_device, mesh=mesh, in_specs=in_specs, out_specs=out_specs, check_vma=False
    )
```
